32 devices in a mesh: lat: 8 (over z, x), batch: 4 (over y, core).
Axes of the slice: x: 2, y: 2, z: 4, core: 2. Of those that a mesh axis runs over, the one named last changes fastest.
Arguments:
- analysis: bfloat16 [8, 12, 96, 2, 12, 128], P('batch', None, 'lat'), may hold values from -6 to 6
- target: float32 [8, 12, 96, 2, 12, 128], P('batch', None, 'lat'), may hold values from -6 to 6
- lead_step: int32 [8], P('batch'), may hold values from 1 to 20
- loss_mask: int32 [8, 12, 96, 2, 12], P('batch', None, 'lat'), may hold values from 0 to 1, as said below
- embed_w: float32 [128, 192], replicated, may hold values from -0.5 to 0.5
- lead_table: float32 [20, 192], replicated, may hold values from -3 to 3
- qkv_w: float32 [2, 192, 576], replicated, may hold values from -0.4375 to 0.4375
- proj_w: float32 [2, 192, 192], replicated, may hold values from -1.5 to 1.5
- up_w: float32 [2, 192, 768], replicated, may hold values from -0.4375 to 0.4375
- down_w: float32 [2, 768, 192], replicated, may hold values from -0.4375 to 0.4375
- decode_w: float32 [192, 128], replicated, may hold values from -0.4375 to 0.4375
- norm_params: float32 [2, 5, 192], replicated
- loss_scale: float32 [128], replicated, may hold values from -1 to -0.3
- embed_mom: float32 [128, 192], replicated, may hold values from -5.9604645e-07 to 5.9604645e-07
- lead_mom: float32 [20, 192], replicated, may hold values from -5.9604645e-07 to 5.9604645e-07
- qkv_mom: float32 [2, 192, 576], replicated, may hold values from -5.9604645e-07 to 5.9604645e-07
- proj_mom: float32 [2, 192, 192], replicated, may hold values from -5.9604645e-07 to 5.9604645e-07
- up_mom: float32 [2, 192, 768], replicated, may hold values from -5.9604645e-07 to 5.9604645e-07
- down_mom: float32 [2, 768, 192], replicated, may hold values from -5.9604645e-07 to 5.9604645e-07
- decode_mom: float32 [192, 128], replicated, may hold values from -5.9604645e-07 to 5.9604645e-07
- norm_mom: float32 [2, 5, 192], replicated, may hold values from -5.9604645e-07 to 5.9604645e-07
- scale_mom: float32 [128], replicated, may hold values from -0.00030517578 to 0.00030517578
- embed_sec: float32 [128, 192], replicated, may hold values from 8.830318e-16 to 3.5321272e-15
- lead_sec: float32 [20, 192], replicated, may hold values from 8.830318e-16 to 3.5321272e-15
- qkv_sec: float32 [2, 192, 576], replicated, may hold values from 8.830318e-16 to 3.5321272e-15
- proj_sec: float32 [2, 192, 192], replicated, may hold values from 8.830318e-16 to 3.5321272e-15
- up_sec: float32 [2, 192, 768], replicated, may hold values from 8.830318e-16 to 3.5321272e-15
- down_sec: float32 [2, 768, 192], replicated, may hold values from 8.830318e-16 to 3.5321272e-15
- decode_sec: float32 [192, 128], replicated, may hold values from 8.830318e-16 to 3.5321272e-15
- norm_sec: float32 [2, 5, 192], replicated, may hold values from 8.830318e-16 to 3.5321272e-15
- scale_sec: float32 [128], replicated, may hold values from 1.953125e-10 to 7.8125e-10
Outputs:
- embed_new: float32 [128, 192], replicated
- lead_new: float32 [20, 192], replicated
- qkv_new: float32 [2, 192, 576], replicated
- proj_new: float32 [2, 192, 192], replicated
- up_new: float32 [2, 192, 768], replicated
- down_new: float32 [2, 768, 192], replicated
- decode_new: float32 [192, 128], replicated
- norm_new: float32 [2, 5, 192], replicated
- scale_new: float32 [128], replicated
- embed_mom_new: float32 [128, 192], replicated
- lead_mom_new: float32 [20, 192], replicated
- qkv_mom_new: float32 [2, 192, 576], replicated
- proj_mom_new: float32 [2, 192, 192], replicated
- up_mom_new: float32 [2, 192, 768], replicated
- down_mom_new: float32 [2, 768, 192], replicated
- decode_mom_new: float32 [192, 128], replicated
- norm_mom_new: float32 [2, 5, 192], replicated
- scale_mom_new: float32 [128], replicated
- embed_sec_new: float32 [128, 192], replicated
- lead_sec_new: float32 [20, 192], replicated
- qkv_sec_new: float32 [2, 192, 576], replicated
- proj_sec_new: float32 [2, 192, 192], replicated
- up_sec_new: float32 [2, 192, 768], replicated
- down_sec_new: float32 [2, 768, 192], replicated
- decode_sec_new: float32 [192, 128], replicated
- norm_sec_new: float32 [2, 5, 192], replicated
- scale_sec_new: float32 [128], replicated
- loss_sum: float32 [], replicated
- loss_count: float32 [], replicated
- grad_norm: float32 [], replicated
The draws below stay inside these ranges and needn't reach their ends.
Inputs may be any that keep to these rules, and one draw needn't show every extreme that they name: `loss_mask`: 1 where a cell counts; the first longitude column always counts.
All inputs are finite; a program needn't handle non-finite values.
Results may differ from the reference program's by a relative error of at most 0.0017.
The reference program's roundings to bfloat16 on the way count: a program that leaves them out, or rounds other values in their place, can miss the bound.
Values may be sent and summed in bfloat16 or wider, within the bound.
A program may use at most 640 MiB of HBM per device.

```python
import math
import jax
import jax.numpy as jnp
from jax import lax

C = 192
HEADS = 6
HDIM = 32
FF = 768
CIN = 128
LEADS = 20
ZL = 2
STEP = 10
LON = 144
H = 96
SAMPLES = 8
TOKENS = 221184


def draw_loss_mask(key, part):
    key = jax.random.fold_in(key, 7)
    row_index = jnp.arange(H, dtype=jnp.int32)[None, None, :, None, None]
    sample_index = jnp.arange(SAMPLES, dtype=jnp.int32)[:, None, None, None, None]
    block_index = jnp.arange(LON // 12, dtype=jnp.int32)[None, :, None, None, None]
    inner_index = jnp.arange(12, dtype=jnp.int32)[None, None, None, None, :]
    row_level = 100 + 400 * row_index // max(H - 1, 1)
    sample_level = 1 + 2 * sample_index // max(SAMPLES - 1, 1)
    draws = jax.random.randint(key, (SAMPLES, LON // 12, H, ZL, 12), 0, 1500, dtype=jnp.int32)
    counted = (draws < row_level * sample_level).astype(jnp.int32)
    first_column = (block_index == 0) & (inner_index == 0)
    return jnp.where(first_column, 1, counted).astype(jnp.int32)


def draw_norm_params(key, part):
    key = jax.random.fold_in(key, 11)
    first_key, second_key = jax.random.split(key)
    gains = 1.0 + 0.3 * jax.random.uniform(first_key, (5, C), jnp.float32, -1.0, 1.0)
    biases = 0.2 * jax.random.normal(second_key, (5, C), jnp.float32)
    return jnp.stack([gains, biases]).astype(jnp.float32)


def set_ends(entries, rng, smallest, high):
    longest = entries.shape.index(max(entries.shape))
    spots = []
    for shift in (0, 1):
        where = [jax.random.randint(jax.random.fold_in(rng, axis), (), 0, length) for axis, length in enumerate(entries.shape)]
        where[longest] = (where[longest] + shift) % entries.shape[longest]
        spots.append(tuple(where))
    return entries.at[spots[0]].set(smallest).at[spots[1]].set(high)


def block_levels(rng, extent, shards, low, largest):
    def one(axis_at, shards_of):
        steps = jax.random.uniform(jax.random.fold_in(jax.random.fold_in(rng, 6), axis_at), (shards_of,), jnp.float32, low / len(shards), largest / len(shards))
        return jnp.repeat(jnp.exp(steps), extent[axis_at] // shards_of).reshape((-1,) + (1,) * (len(extent) - axis_at - 1))

    level = one(*shards[0])
    for cut in shards[1:]:
        level = level * one(*cut)
    return level


def centred(stream_key, dims, deviation, bound, pieces=(), held_as=jnp.bfloat16):
    result = jax.random.normal(stream_key, dims, jnp.float32) * deviation
    if len(pieces) > 0:
        result = block_levels(stream_key, dims, pieces, -0.22, 0.18) * result
    return jnp.clip(result, min=-bound, max=bound).astype(held_as)


def setup_inputs(seed: int = 0) -> dict:
    key_list = jax.random.split(jax.random.key(seed), 32)
    return {
        "analysis": centred(key_list[0], (SAMPLES, LON // 12, H, ZL, 12, CIN), 1.0, 6.0, ((0, 4), (2, 8))),
        "target": centred(key_list[1], (SAMPLES, LON // 12, H, ZL, 12, CIN), 1.0, 6.0, ((0, 4), (2, 8)), jnp.float32),
        "lead_step": set_ends(jax.random.randint(key_list[2], (SAMPLES,), 1, 21), jax.random.fold_in(key_list[2], 1), 1, 20).astype(jnp.int32),
        "loss_mask": draw_loss_mask(jax.random.fold_in(key_list[31], 71), 0),
        "embed_w": centred(key_list[4], (CIN, C), CIN ** -0.5, 0.5, (), jnp.float32),
        "lead_table": centred(key_list[5], (LEADS, C), 0.5, 3.0, (), jnp.float32),
        "qkv_w": centred(key_list[6], (2, C, 3 * C), C ** -0.5, 0.4375, (), jnp.float32),
        "proj_w": centred(key_list[7], (2, C, C), (C // 12) ** -0.5, 1.5, (), jnp.float32),
        "up_w": centred(key_list[8], (2, C, FF), C ** -0.5, 0.4375, (), jnp.float32),
        "down_w": centred(key_list[9], (2, FF, C), (FF // 4) ** -0.5, 0.4375, (), jnp.float32),
        "decode_w": centred(key_list[10], (C, CIN), C ** -0.5, 0.4375, (), jnp.float32),
        "norm_params": draw_norm_params(jax.random.fold_in(key_list[31], 71), 0),
        "loss_scale": jnp.clip(jax.random.uniform(key_list[12], (CIN,), jnp.float32, -1.0, -0.3), -1.0, -0.3),
        "embed_mom": centred(key_list[13], (CIN, C), (0.00055 / (TOKENS * CIN) ** 0.5), 5.960464477539062e-07, (), jnp.float32),
        "lead_mom": centred(key_list[14], (LEADS, C), (0.00055 / (TOKENS * CIN) ** 0.5), 5.960464477539062e-07, (), jnp.float32),
        "qkv_mom": centred(key_list[15], (2, C, 3 * C), (0.00055 / (TOKENS * CIN) ** 0.5), 5.960464477539062e-07, (), jnp.float32),
        "proj_mom": centred(key_list[16], (2, C, C), (0.00055 / (TOKENS * CIN) ** 0.5), 5.960464477539062e-07, (), jnp.float32),
        "up_mom": centred(key_list[17], (2, C, FF), (0.00055 / (TOKENS * CIN) ** 0.5), 5.960464477539062e-07, (), jnp.float32),
        "down_mom": centred(key_list[18], (2, FF, C), (0.00055 / (TOKENS * CIN) ** 0.5), 5.960464477539062e-07, (), jnp.float32),
        "decode_mom": centred(key_list[19], (C, CIN), (0.00055 / (TOKENS * CIN) ** 0.5), 5.960464477539062e-07, (), jnp.float32),
        "norm_mom": centred(key_list[20], (2, 5, C), (0.00055 / (TOKENS * CIN) ** 0.5), 5.960464477539062e-07, (), jnp.float32),
        "scale_mom": centred(key_list[21], (CIN,), (0.00055 / CIN ** 0.5), 0.00030517578, (), jnp.float32),
        "embed_sec": jnp.clip(jnp.exp(jax.random.uniform(key_list[22], (CIN, C), jnp.float32, math.log(8.830317945730489e-16), math.log(3.5321271782921956e-15))), 8.830317945730489e-16, 3.5321271782921956e-15),
        "lead_sec": jnp.clip(jnp.exp(jax.random.uniform(key_list[23], (LEADS, C), jnp.float32, math.log(8.830317945730489e-16), math.log(3.5321271782921956e-15))), 8.830317945730489e-16, 3.5321271782921956e-15),
        "qkv_sec": jnp.clip(jnp.exp(jax.random.uniform(key_list[24], (2, C, 3 * C), jnp.float32, math.log(8.830317945730489e-16), math.log(3.5321271782921956e-15))), 8.830317945730489e-16, 3.5321271782921956e-15),
        "proj_sec": jnp.clip(jnp.exp(jax.random.uniform(key_list[25], (2, C, C), jnp.float32, math.log(8.830317945730489e-16), math.log(3.5321271782921956e-15))), 8.830317945730489e-16, 3.5321271782921956e-15),
        "up_sec": jnp.clip(jnp.exp(jax.random.uniform(key_list[26], (2, C, FF), jnp.float32, math.log(8.830317945730489e-16), math.log(3.5321271782921956e-15))), 8.830317945730489e-16, 3.5321271782921956e-15),
        "down_sec": jnp.clip(jnp.exp(jax.random.uniform(key_list[27], (2, FF, C), jnp.float32, math.log(8.830317945730489e-16), math.log(3.5321271782921956e-15))), 8.830317945730489e-16, 3.5321271782921956e-15),
        "decode_sec": jnp.clip(jnp.exp(jax.random.uniform(key_list[28], (C, CIN), jnp.float32, math.log(8.830317945730489e-16), math.log(3.5321271782921956e-15))), 8.830317945730489e-16, 3.5321271782921956e-15),
        "norm_sec": jnp.clip(jnp.exp(jax.random.uniform(key_list[29], (2, 5, C), jnp.float32, math.log(8.830317945730489e-16), math.log(3.5321271782921956e-15))), 8.830317945730489e-16, 3.5321271782921956e-15),
        "scale_sec": jnp.clip(jnp.exp(jax.random.uniform(key_list[30], (CIN,), jnp.float32, math.log(1.953125022824409e-10), math.log(7.812500091297636e-10))), 1.953125022824409e-10, 7.812500091297636e-10),
    }


beta_one = 0.9
beta_two = 0.999
adam_eps = 1e-08
clip_max = 0.005
rate_table = (0.2, 1.0, 0.2, 0.2, 0.2, 0.2, 0.2, 1.0, 1.0)
decay_table = (0.1, 0.1, 0.1, 0.1, 0.1, 0.1, 0.1, 0.0, 0.0)

@jax.custom_vjp
def low(v):
    return lax.optimization_barrier(v.astype(jnp.bfloat16)).astype(jnp.float32)

@jax.custom_vjp
def low_back(v):
    return v

def low_keep(v):
    return (low(v), None)

def low_pass(kept, grad):
    return (grad,)

def back_keep(v):
    return (v, None)

def back_low(kept, grad):
    return (low(grad),)
low.defvjp(low_keep, low_pass)
low_back.defvjp(back_keep, back_low)

def layer_norm(field, gain, bias):
    center = field - lax.optimization_barrier(jnp.mean(field, axis=-1, keepdims=True))
    spread = lax.optimization_barrier(jnp.mean(center * center, axis=-1, keepdims=True))
    return center * lax.rsqrt(spread + 1e-05) * gain + bias

def matmul(left, right):
    return jnp.matmul(left, right, precision=lax.Precision.HIGHEST)

def to_windows(field):
    blocks, row_count = (field.shape[0], field.shape[1])
    return field.reshape(blocks * (row_count // 6), -1, field.shape[-1])

def attention(normed, w_qkv, w_proj, shifted):
    blocks, row_count, levels, twelve, channels = normed.shape
    global_row = jnp.arange(row_count + 6 if shifted else row_count, dtype=jnp.int32)
    if shifted:
        normed = jnp.pad(normed, ((0, 0), (3, 3), (0, 0), (0, 0), (0, 0)))
        row_ok = ((global_row >= 3) & (global_row < row_count + 3)).astype(jnp.float32)
    else:
        row_ok = jnp.ones(global_row.shape, jnp.float32)
    padded_rows = normed.shape[1]
    row_grid = jnp.broadcast_to(row_ok[None, :, None, None, None], (blocks, padded_rows, levels, twelve, 1))
    validity = to_windows(row_grid)[..., 0] > 0.5
    windows = to_windows(normed)
    count_w = windows.shape[0]
    packed = low_back(low(matmul(windows, w_qkv)))
    packed = packed.reshape(count_w, -1, 3, HEADS, HDIM)
    query_rows, key_rows, value_rows = (packed[:, :, 0], packed[:, :, 1], packed[:, :, 2])
    scores = low_back(jnp.einsum('wqhd,wkhd->whqk', query_rows, key_rows, precision=lax.Precision.HIGHEST) * HDIM ** (-0.5))
    scores = jnp.where(validity[:, None, None, :], scores, -1e+30)
    probability = low(jax.nn.softmax(scores, axis=-1))
    mixture = low_back(low(jnp.einsum('whqk,wkhd->wqhd', probability, value_rows, precision=lax.Precision.HIGHEST)))
    output = low_back(matmul(mixture.reshape(count_w, -1, channels), w_proj))
    output = output.reshape(blocks, padded_rows, levels, twelve, channels)
    if shifted:
        output = output[:, 3:3 + row_count]
    return output

def swin_block(hidden, w_qkv, w_proj, w_up, w_down, gains, shifted):
    normed = low(layer_norm(hidden, gains[0, 0], gains[1, 0]))
    hidden = hidden + attention(normed, low(w_qkv), low(w_proj), shifted)
    normed = low(layer_norm(hidden, gains[0, 1], gains[1, 1]))
    inner_pre = low_back(matmul(normed, low(w_up)))
    return hidden + low_back(matmul(low(jax.nn.gelu(inner_pre)), low(w_down)))

def sample_loss(weights, analysis, target, lead_step, loss_mask):
    embed_w, lead_table, qkv_w, proj_w, up_w, down_w, decode_w, norm_params, loss_scale = weights
    hidden = low_back(matmul(analysis, low(embed_w)))
    lead_hot = (jnp.arange(LEADS, dtype=jnp.int32) == lead_step - 1).astype(jnp.float32)
    hidden = hidden + matmul(lead_hot, lead_table)
    for depth_index in range(2):
        hidden = swin_block(hidden, qkv_w[depth_index], proj_w[depth_index], up_w[depth_index], down_w[depth_index], norm_params[:, 2 * depth_index:2 * depth_index + 2], depth_index == 1)
    normed = low(layer_norm(hidden, norm_params[0, 4], norm_params[1, 4]))
    predicted = low_back(matmul(normed, low(decode_w)))
    error = predicted - target
    terms = jnp.sqrt(error * error + 1.0) * jnp.exp(-loss_scale) + loss_scale
    return jnp.sum(terms * loss_mask.astype(jnp.float32)[..., None])

def total_loss(weights, analysis, target, lead_step, loss_mask):

    def one_sample(running, sample_items):
        return (running + jax.checkpoint(sample_loss)(weights, *sample_items), None)
    totals, _ = lax.scan(one_sample, jnp.zeros((), jnp.float32), (analysis, target, lead_step, loss_mask))
    return totals

def apply_update(weights, gradients, firsts, seconds, cell_count):
    scaled = [member / cell_count for member in gradients]
    grad_norm = jnp.sqrt(sum((jnp.sum(member * member) for member in scaled)))
    factor = jnp.minimum(1.0, clip_max / grad_norm)
    news, moments, squares = ([], [], [])
    for weight, member, first, second, rate, shrink in zip(weights, scaled, firsts, seconds, rate_table, decay_table):
        clipped = member * factor
        first = beta_one * first + (1.0 - beta_one) * clipped
        second = beta_two * second + (1.0 - beta_two) * clipped * clipped
        first_hat = first / (1.0 - beta_one ** STEP)
        second_hat = second / (1.0 - beta_two ** STEP)
        news.append(weight - rate * (first_hat / (jnp.sqrt(second_hat) + adam_eps) + shrink * weight))
        moments.append(first)
        squares.append(second)
    return (news, moments, squares, grad_norm)

def reference(analysis, target, lead_step, loss_mask, embed_w, lead_table, qkv_w, proj_w, up_w, down_w, decode_w, norm_params, loss_scale, embed_mom, lead_mom, qkv_mom, proj_mom, up_mom, down_mom, decode_mom, norm_mom, scale_mom, embed_sec, lead_sec, qkv_sec, proj_sec, up_sec, down_sec, decode_sec, norm_sec, scale_sec):
    weights = (embed_w, lead_table, qkv_w, proj_w, up_w, down_w, decode_w, norm_params, loss_scale)
    firsts = (embed_mom, lead_mom, qkv_mom, proj_mom, up_mom, down_mom, decode_mom, norm_mom, scale_mom)
    seconds = (embed_sec, lead_sec, qkv_sec, proj_sec, up_sec, down_sec, decode_sec, norm_sec, scale_sec)
    analysis_f = analysis.astype(jnp.float32)

    def closed(params):
        return total_loss(params, analysis_f, target, lead_step, loss_mask)
    loss_sum, pull = jax.vjp(closed, weights)
    gradients = pull(jnp.ones((), jnp.float32))[0]
    cell_count = jnp.sum(loss_mask.astype(jnp.float32)) * CIN
    news, moments, squares, grad_norm = apply_update(weights, gradients, firsts, seconds, cell_count)
    return (news[0], news[1], news[2], news[3], news[4], news[5], news[6], news[7], news[8], moments[0], moments[1], moments[2], moments[3], moments[4], moments[5], moments[6], moments[7], moments[8], squares[0], squares[1], squares[2], squares[3], squares[4], squares[5], squares[6], squares[7], squares[8], loss_sum, cell_count, grad_norm)
```

```python
from functools import partial
import math

import jax
import jax.numpy as jnp
from jax import lax
from jax.experimental import pallas as pl
from jax.experimental.pallas import tpu as pltpu
from jax.sharding import PartitionSpec as P

HEADS = 6
LEADS = 20
STEP = 10
C = 192
FF = 768
CIN = 128
HDIM = 32
COL = 288
WIN = 144
HALF = 72
LANES = 896
SCALE = HDIM ** (-0.5)
SCALE2 = SCALE * math.log2(math.e)
BF = jnp.bfloat16
F32 = jnp.float32

beta_one = 0.9
beta_two = 0.999
adam_eps = 1e-08
clip_max = 0.005
rate_table = (0.2, 1.0, 0.2, 0.2, 0.2, 0.2, 0.2, 1.0, 1.0)
decay_table = (0.1, 0.1, 0.1, 0.1, 0.1, 0.1, 0.1, 0.0, 0.0)

VMEM_BYTES = 56 * 1024 * 1024


def dot(a, b):
    return lax.dot_general(a, b, (((1,), (0,)), ((), ())), preferred_element_type=F32)


def dot_nt(a, b):
    return lax.dot_general(a, b, (((1,), (1,)), ((), ())), preferred_element_type=F32)


def dot_tn(a, b):
    return lax.dot_general(a, b, (((0,), (0,)), ((), ())), preferred_element_type=F32)


def norm_stats(x):
    center = x - jnp.mean(x, axis=-1, keepdims=True)
    rstd = lax.rsqrt(jnp.mean(center * center, axis=-1, keepdims=True) + 1e-05)
    return center * rstd, rstd


def norm_back(dy, xhat, rstd, gain):
    dxhat = dy * gain
    first = jnp.mean(dxhat, axis=-1, keepdims=True)
    second = jnp.mean(dxhat * xhat, axis=-1, keepdims=True)
    return rstd * (dxhat - first - xhat * second)


def add_norm_grads(acc_ref, index, dy, xhat):
    acc_ref[2 * index : 2 * index + 1] += jnp.sum(dy * xhat, axis=0, keepdims=True)
    acc_ref[2 * index + 1 : 2 * index + 2] += jnp.sum(dy, axis=0, keepdims=True)


def gelu_both(x):
    c0 = math.sqrt(2.0 / math.pi)
    c1 = c0 * 0.044715
    square = x * x
    slope = jnp.tanh(x * (c0 + c1 * square))
    half = 0.5 + 0.5 * slope
    active = x * half
    return active, half + active * ((1.0 - slope) * (c0 + (3.0 * c1) * square))


def head_masks():
    lane = lax.broadcasted_iota(jnp.int32, (1, C), 1) // HDIM
    return [(lane == h).astype(F32).astype(BF) for h in range(HEADS)]


def expand(x, masks, edge):
    rem = [x[128:144] * masks[h] for h in range(HEADS)] + [jnp.zeros((32, C), BF)]
    if edge:
        low = [x[0:64] * masks[h] for h in range(HEADS)]
        high = [x[64:128] * masks[h] for h in range(HEADS)]
        return jnp.concatenate(low + rem + high, axis=0)
    return jnp.concatenate([x[0:128] * masks[h] for h in range(HEADS)] + rem, axis=0)


def low_lanes():
    return lax.broadcasted_iota(jnp.int32, (1, 128), 1) % 16 < 8


def score_like(keys, expanded, edge):
    if not edge:
        return dot_nt(keys, expanded)
    low = dot_nt(keys[0], expanded[0:512])
    high = dot_nt(keys[1], expanded[384:896])
    rem = jnp.where(low_lanes(), low[:, 384:512], high[:, 0:128])
    return jnp.concatenate([low[:, 0:384], rem, high[:, 128:512]], axis=1)


def pick_rem(rem, masks32):
    back = rem.T
    total = back[0:16] * masks32[0]
    for h in range(1, HEADS):
        total = total + back[16 * h : 16 * h + 16] * masks32[h]
    return total


def query_side(vals_t, weights, masks32, edge):
    if not edge:
        blocks = []
        for pair in range(3):
            both = dot(vals_t[64 * pair : 64 * pair + 64], weights[:, 256 * pair : 256 * pair + 256])
            blocks += [both[0:32, 0:128], both[32:64, 128:256]]
        rem = dot(vals_t, weights[:, 768:896])
    else:
        low_a = dot(vals_t[0][0:128], weights[:, 0:256])
        low_b = dot(vals_t[0][128:192], weights[:, 256:384])
        high_a = dot(vals_t[1][0:128], weights[:, 512:768])
        high_b = dot(vals_t[1][128:192], weights[:, 768:896])
        rem_low = dot(vals_t[0], weights[:, 384:512])
        rem_high = dot(vals_t[1], weights[:, 384:512])
        rem = jnp.where(low_lanes(), rem_low, rem_high)
        left = lax.broadcasted_iota(jnp.int32, (1, 128), 1) < 64
        blocks = []
        for h in range(HEADS):
            src_low, src_high, local = (low_a, high_a, h) if h < 4 else (low_b, high_b, h - 4)
            group = slice(128 * (local // 2), 128 * (local // 2) + 128)
            low = src_low[32 * local : 32 * local + 32, group]
            high = src_high[32 * local : 32 * local + 32, group]
            if h % 2:
                low = pltpu.roll(low, 64, 1)
            else:
                high = pltpu.roll(high, 64, 1)
            blocks.append(jnp.where(left, low, high))
    main = jnp.concatenate(blocks, axis=0).T
    return jnp.concatenate([main, pick_rem(rem, masks32)], axis=0)


def key_side(weights, expanded, edge):
    if not edge:
        return dot(weights, expanded)
    mask = low_lanes()
    rem = weights[:, 384:512]
    zero = jnp.zeros((), weights.dtype)
    low = jnp.concatenate([weights[:, 0:384], jnp.where(mask, rem, zero)], axis=1)
    high = jnp.concatenate([jnp.where(mask, zero, rem), weights[:, 512:896]], axis=1)
    return dot(low, expanded[0:512]), dot(high, expanded[384:896])


def edge_bias(scores, bias):
    low, high = bias
    low_rem = jnp.where(low_lanes(), low, high)
    top = scores[0:HALF]
    top = jnp.concatenate([top[:, 0:384] + low, top[:, 384:512] + low_rem, top[:, 512:896] + high], axis=1)
    return jnp.concatenate([top, scores[HALF:]], axis=0)


def attention_forward(q, k, vals, masks, masks32, edge, bias=None):
    queries = expand(q, masks, edge)
    scores = score_like(k, queries, edge)
    if edge:
        scores = edge_bias(scores, bias)
    scores = scores * SCALE2
    highest = jnp.max(scores, axis=0, keepdims=True)
    expo = jnp.exp2(scores - highest)
    total = jnp.sum(expo, axis=0, keepdims=True)
    probs = (expo * (1.0 / total)).astype(BF)
    vals_t = (vals[0].T, vals[1].T) if edge else vals.T
    mixture = query_side(vals_t, probs, masks32, edge)
    return mixture, highest + jnp.log2(total)


def attention_backward(q, k, vals, log_total, dmix, masks, masks32, edge, bias=None):
    queries = expand(q, masks, edge)
    scores = score_like(k, queries, edge)
    if edge:
        scores = edge_bias(scores, bias)
    probs = jnp.exp2(scores * SCALE2 - log_total)
    douts = expand(dmix, masks, edge)
    dprobs = score_like(vals, douts, edge)
    row_terms = jnp.sum(dprobs * probs, axis=0, keepdims=True)
    dscores = (probs * (dprobs - row_terms)).astype(BF)
    dvals = key_side(probs.astype(BF), douts, edge)
    dkeys = key_side(dscores, queries, edge)
    k_t = (k[0].T, k[1].T) if edge else k.T
    dq = query_side(k_t, dscores, masks32, edge) * SCALE
    if edge:
        dkeys = (dkeys[0] * SCALE, dkeys[1] * SCALE)
    else:
        dkeys = dkeys * SCALE
    return dq, dkeys, dvals


def forward_zero(
    columns,
    step_ref,
    an_ref,
    lead_ref,
    embed_ref,
    qkv_ref,
    proj_ref,
    up_ref,
    down_ref,
    norm_ref,
    h0_ref,
    pack_ref,
    lse_ref,
    mix_ref,
    h2_ref,
    act_ref,
    slope_ref,
    h1_ref,
    top_ref,
    bot_ref,
    wembed,
    wqkv,
    wproj,
    wup,
    wdown,
    sample,
):
    @pl.when(pl.program_id(0) == 0)
    def _():
        wembed[...] = embed_ref[...].astype(BF)
        wqkv[...] = qkv_ref[0].astype(BF)
        wproj[...] = proj_ref[0].astype(BF)
        wup[...] = up_ref[0].astype(BF)
        wdown[...] = down_ref[0].astype(BF)

    masks = head_masks()
    masks32 = [m.astype(F32) for m in masks]
    lead_row = lead_ref[pl.ds(step_ref[sample] - 1, 1), :]
    for col in range(columns):
        hidden = dot_nt(an_ref[col], wembed[...]) + lead_row
        h0_ref[col] = hidden
        xhat, _ = norm_stats(hidden)
        normed = (xhat * norm_ref[0, 0:1] + norm_ref[0, 1:2]).astype(BF)
        packed = dot(normed, wqkv[...]).astype(BF)
        pack_ref[col] = packed
        mixtures = []
        for w in range(2):
            part = packed[WIN * w : WIN * w + WIN]
            mixture, log_total = attention_forward(
                part[:, 0:C], part[:, C : 2 * C], part[:, 2 * C :], masks, masks32, False
            )
            lse_ref[col, w : w + 1] = log_total
            mixtures.append(mixture)
        mixture = jnp.concatenate(mixtures, axis=0).astype(BF)
        mix_ref[col] = mixture
        hidden_two = hidden + dot(mixture, wproj[...])
        h2_ref[col] = hidden_two
        xhat, _ = norm_stats(hidden_two)
        normed_two = (xhat * norm_ref[1, 0:1] + norm_ref[1, 1:2]).astype(BF)
        active, slope = gelu_both(dot(normed_two, wup[...]))
        active = active.astype(BF)
        act_ref[col] = active
        slope_ref[col] = slope
        hidden_one = hidden_two + dot_nt(active, wdown[...])
        h1_ref[col] = hidden_one
        xhat, _ = norm_stats(jnp.concatenate([hidden_one[0:HALF], hidden_one[COL - HALF :]], axis=0))
        normed = xhat * norm_ref[2, 0:1] + norm_ref[2, 1:2]
        top_ref[col] = normed[0:HALF].astype(BF)
        bot_ref[col] = normed[HALF:].astype(BF)


def spread(top, middle_and_ends):
    return jnp.concatenate([top[0:64], middle_and_ends[0:64], top[64:72], middle_and_ends[64:72]], axis=0)


def middle(
    columns,
    flag_ref,
    h1_ref,
    up_in_ref,
    down_in_ref,
    target_ref,
    mask_ref,
    qkv_ref,
    proj_ref,
    up_ref,
    down_ref,
    decode_ref,
    norm_ref,
    scale_ref,
    *rest,
    first,
):
    if first:
        prev = None
    else:
        prev, rest = rest[:8], rest[8:]
    (
        dh2_ref,
        dn_ref,
        dtop_ref,
        dbot_ref,
        gqkv_ref,
        gproj_ref,
        gup_ref,
        gdown_ref,
        gdec_ref,
        gnorm_ref,
        gscale_ref,
        count_ref,
        wqkv,
        wproj,
        wup,
        wdown,
        wdec,
    ) = rest
    sums = (gqkv_ref, gproj_ref, gup_ref, gdown_ref, gdec_ref, gnorm_ref, gscale_ref, count_ref)

    @pl.when(pl.program_id(0) == 0)
    def _():
        wqkv[...] = qkv_ref[0].astype(BF)
        wproj[...] = proj_ref[0].astype(BF)
        wup[...] = up_ref[0].astype(BF)
        wdown[...] = down_ref[0].astype(BF)
        wdec[...] = decode_ref[...].astype(BF)
        for at, ref in enumerate(sums):
            ref[...] = jnp.zeros_like(ref) if prev is None else prev[at][...]

    masks = head_masks()
    masks32 = [m.astype(F32) for m in masks]
    bias = (flag_ref[0], flag_ref[1])
    inverse = jnp.exp(-scale_ref[...])
    for col in range(columns):
        h1 = jnp.concatenate(
            [
                h1_ref[col, 0:64],
                h1_ref[col, 216:280],
                h1_ref[col, 64:72],
                h1_ref[col, 280:288],
                h1_ref[col, 72:216],
            ],
            axis=0,
        )
        xhat_one, rstd_one = norm_stats(h1)
        normed = xhat_one * norm_ref[2, 0:1] + norm_ref[2, 1:2]
        normed_low = normed.astype(BF)
        n_top = jnp.concatenate([up_in_ref[col].astype(F32), normed[0:64], normed[128:136]], axis=0).astype(BF)
        n_bot = jnp.concatenate([down_in_ref[col].astype(F32), normed[64:128], normed[136:144]], axis=0).astype(BF)
        n_kv = jnp.concatenate([n_top, n_bot, normed_low[WIN:]], axis=0)
        queries = dot(normed_low, wqkv[:, 0:C]).astype(BF)
        keys_vals = dot(n_kv, wqkv[:, C:]).astype(BF)
        keys, vals = keys_vals[:, 0:C], keys_vals[:, C:]
        k_edge, v_edge = (keys[0:WIN], keys[WIN : 2 * WIN]), (vals[0:WIN], vals[WIN : 2 * WIN])
        mix_e, lse_e = attention_forward(queries[0:WIN], k_edge, v_edge, masks, masks32, True, bias)
        mix_m, lse_m = attention_forward(queries[WIN:], keys[2 * WIN :], vals[2 * WIN :], masks, masks32, False)
        mixture = jnp.concatenate([mix_e, mix_m], axis=0).astype(BF)
        hidden_two = h1 + dot(mixture, wproj[...])
        xhat_two, rstd_two = norm_stats(hidden_two)
        normed_two = (xhat_two * norm_ref[3, 0:1] + norm_ref[3, 1:2]).astype(BF)
        active, slope = gelu_both(dot(normed_two, wup[...]))
        active = active.astype(BF)
        hidden = hidden_two + dot_nt(active, wdown[...])
        xhat, rstd = norm_stats(hidden)
        normed_last = (xhat * norm_ref[4, 0:1] + norm_ref[4, 1:2]).astype(BF)
        predicted = dot(normed_last, wdec[...])
        target = jnp.concatenate(
            [
                target_ref[col, 0:64],
                target_ref[col, 216:280],
                target_ref[col, 64:72],
                target_ref[col, 280:288],
                target_ref[col, 72:216],
            ],
            axis=0,
        )
        cells = dot_tn(mask_ref[col], jnp.ones((8, CIN), BF))
        cells = jnp.concatenate([cells[0:64], cells[216:280], cells[64:72], cells[280:288], cells[72:216]], axis=0)
        error = predicted - target
        square = error * error + 1.0
        back = lax.rsqrt(square)
        gscale_ref[0:1] += jnp.sum(cells * (1.0 - square * back * inverse), axis=0, keepdims=True)
        count_ref[0:1] += jnp.sum(cells, axis=0, keepdims=True)
        dpred = (cells * inverse * error * back).astype(BF)
        gdec_ref[...] += dot_tn(normed_last, dpred)
        dnorm = dot_nt(dpred, wdec[...])
        add_norm_grads(gnorm_ref, 2, dnorm, xhat)
        grad = norm_back(dnorm, xhat, rstd, norm_ref[4, 0:1])
        grad_low = grad.astype(BF)
        gdown_ref[...] += dot_tn(grad_low, active)
        dinner = (dot(grad_low, wdown[...]) * slope).astype(BF)
        gup_ref[...] += dot_tn(normed_two, dinner)
        dnorm = dot_nt(dinner, wup[...])
        add_norm_grads(gnorm_ref, 1, dnorm, xhat_two)
        grad = grad + norm_back(dnorm, xhat_two, rstd_two, norm_ref[3, 0:1])
        grad_low = grad.astype(BF)
        gproj_ref[...] += dot_tn(mixture, grad_low)
        dmix = dot_nt(grad_low, wproj[...]).astype(BF)
        dq_e, dk_e, dv_e = attention_backward(
            queries[0:WIN], k_edge, v_edge, lse_e, dmix[0:WIN], masks, masks32, True, bias
        )
        dq_m, dk_m, dv_m = attention_backward(
            queries[WIN:], keys[2 * WIN :], vals[2 * WIN :], lse_m, dmix[WIN:], masks, masks32, False
        )
        dq = jnp.concatenate([dq_e, dq_m], axis=0).astype(BF)
        dk = jnp.concatenate([dk_e[0], dk_e[1], dk_m], axis=0).astype(BF)
        dv = jnp.concatenate([dv_e[0], dv_e[1], dv_m], axis=0).astype(BF)
        dkv = jnp.concatenate([dk, dv], axis=1)
        gqkv_ref[:, 0:C] += dot_tn(normed_low, dq)
        gqkv_ref[:, C:] += dot_tn(n_kv, dkv)
        dn_q = dot_nt(dq, wqkv[:, 0:C])
        dn_kv = dot_nt(dkv, wqkv[:, C:])
        dtop_ref[col] = dn_kv[0:HALF].astype(BF)
        dbot_ref[col] = dn_kv[WIN : WIN + HALF].astype(BF)
        dn_ref[col, 0:64] = dn_q[0:64] + dn_kv[72:136]
        dn_ref[col, 64:72] = dn_q[128:136] + dn_kv[136:144]
        dn_ref[col, 72:216] = dn_q[144:288] + dn_kv[288:432]
        dn_ref[col, 216:280] = dn_q[64:128] + dn_kv[216:280]
        dn_ref[col, 280:288] = dn_q[136:144] + dn_kv[280:288]
        dh2_ref[col, 0:64] = grad[0:64]
        dh2_ref[col, 64:72] = grad[128:136]
        dh2_ref[col, 72:216] = grad[144:288]
        dh2_ref[col, 216:280] = grad[64:128]
        dh2_ref[col, 280:288] = grad[136:144]


def backward_zero(
    columns,
    step_ref,
    an_ref,
    h0_ref,
    pack_ref,
    lse_ref,
    mix_ref,
    h2_ref,
    act_ref,
    slope_ref,
    h1_ref,
    dh2_ref,
    dn_ref,
    ret_top_ref,
    ret_bot_ref,
    qkv_ref,
    proj_ref,
    up_ref,
    down_ref,
    norm_ref,
    *rest,
    first,
    sample,
):
    if first:
        prev = None
    else:
        prev, rest = rest[:7], rest[7:]
    (
        gembed_ref,
        glead_ref,
        gqkv_ref,
        gproj_ref,
        gup_ref,
        gdown_ref,
        gnorm_ref,
        wqkv,
        wproj,
        wup,
        wdown,
    ) = rest
    sums = (gembed_ref, glead_ref, gqkv_ref, gproj_ref, gup_ref, gdown_ref, gnorm_ref)

    @pl.when(pl.program_id(0) == 0)
    def _():
        wqkv[...] = qkv_ref[0].astype(BF)
        wproj[...] = proj_ref[0].astype(BF)
        wup[...] = up_ref[0].astype(BF)
        wdown[...] = down_ref[0].astype(BF)
        for at, ref in enumerate(sums):
            ref[...] = jnp.zeros_like(ref) if prev is None else prev[at][...]

    masks = head_masks()
    masks32 = [m.astype(F32) for m in masks]
    lead_at = pl.ds(step_ref[sample] - 1, 1)
    for col in range(columns):
        dn = jnp.concatenate(
            [
                dn_ref[col, 0:HALF] + ret_top_ref[col].astype(F32),
                dn_ref[col, HALF : COL - HALF],
                dn_ref[col, COL - HALF :] + ret_bot_ref[col].astype(F32),
            ],
            axis=0,
        )
        xhat, rstd = norm_stats(h1_ref[col])
        add_norm_grads(gnorm_ref, 2, dn, xhat)
        grad = dh2_ref[col] + norm_back(dn, xhat, rstd, norm_ref[2, 0:1])
        grad_low = grad.astype(BF)
        gdown_ref[...] += dot_tn(grad_low, act_ref[col])
        dinner = (dot(grad_low, wdown[...]) * slope_ref[col]).astype(BF)
        xhat, rstd = norm_stats(h2_ref[col])
        normed_two = (xhat * norm_ref[1, 0:1] + norm_ref[1, 1:2]).astype(BF)
        gup_ref[...] += dot_tn(normed_two, dinner)
        dnorm = dot_nt(dinner, wup[...])
        add_norm_grads(gnorm_ref, 1, dnorm, xhat)
        grad = grad + norm_back(dnorm, xhat, rstd, norm_ref[1, 0:1])
        grad_low = grad.astype(BF)
        gproj_ref[...] += dot_tn(mix_ref[col], grad_low)
        dmix = dot_nt(grad_low, wproj[...]).astype(BF)
        parts = []
        for w in range(2):
            part = pack_ref[col, WIN * w : WIN * w + WIN]
            dq, dk, dv = attention_backward(
                part[:, 0:C],
                part[:, C : 2 * C],
                part[:, 2 * C :],
                lse_ref[col, w : w + 1],
                dmix[WIN * w : WIN * w + WIN],
                masks,
                masks32,
                False,
            )
            parts.append(jnp.concatenate([dq.astype(BF), dk.astype(BF), dv.astype(BF)], axis=1))
        dpacked = jnp.concatenate(parts, axis=0)
        xhat, rstd = norm_stats(h0_ref[col])
        normed = (xhat * norm_ref[0, 0:1] + norm_ref[0, 1:2]).astype(BF)
        gqkv_ref[...] += dot_tn(normed, dpacked)
        dn = dot_nt(dpacked, wqkv[...])
        add_norm_grads(gnorm_ref, 0, dn, xhat)
        grad = grad + norm_back(dn, xhat, rstd, norm_ref[0, 0:1])
        gembed_ref[...] += dot_tn(an_ref[col], grad.astype(BF))
        glead_ref[lead_at, :] += jnp.sum(grad, axis=0, keepdims=True)


def whole(shape):
    zeros = (0,) * len(shape)
    return pl.BlockSpec(shape, lambda i: zeros)


def layer(shape, index):
    at = (index,) + (0,) * len(shape)
    return pl.BlockSpec((1,) + shape, lambda i: at)


def rows(columns, *shape):
    tail = (0,) * len(shape)
    return pl.BlockSpec((columns,) + shape, lambda i: (i,) + tail)


def rows_of(columns, offset, *shape):
    tail = (0,) * len(shape)
    return pl.BlockSpec((columns,) + shape, lambda i: (i + offset,) + tail)


SMEM = pl.BlockSpec(memory_space=pltpu.SMEM)


def struct(shape, dtype):
    return jax.ShapeDtypeStruct(shape, dtype)


def run_forward(lead_step, tokens, lead_table, embed_t, qkv_w, proj_w, up_w, down_t, norm_t, sample, count, columns):
    steps = count // columns
    outs = [
        ((count, COL, C), F32),
        ((count, COL, 3 * C), BF),
        ((count, 2, LANES), F32),
        ((count, COL, C), BF),
        ((count, COL, C), F32),
        ((count, COL, FF), BF),
        ((count, COL, FF), F32),
        ((count, COL, C), F32),
        ((count, HALF, C), BF),
        ((count, HALF, C), BF),
    ]

    def body(*refs):
        forward_zero(columns, *refs, sample=sample)

    return pl.pallas_call(
        body,
        grid=(steps,),
        in_specs=[
            SMEM,
            rows_of(columns, sample * steps, COL, CIN),
            whole((LEADS, C)),
            whole((C, CIN)),
            layer((C, 3 * C), 0),
            layer((C, C), 0),
            layer((C, FF), 0),
            layer((C, FF), 0),
            whole((5, 2, C)),
        ],
        out_specs=[rows(columns, *shape[1:]) for shape, _ in outs],
        out_shape=[struct(*o) for o in outs],
        scratch_shapes=[
            pltpu.VMEM((C, CIN), BF),
            pltpu.VMEM((C, 3 * C), BF),
            pltpu.VMEM((C, C), BF),
            pltpu.VMEM((C, FF), BF),
            pltpu.VMEM((C, FF), BF),
        ],
        compiler_params=pltpu.CompilerParams(vmem_limit_bytes=VMEM_BYTES),
        name="forward_zero",
    )(lead_step, tokens, lead_table, embed_t, qkv_w, proj_w, up_w, down_t, norm_t)


MIDDLE_SUMS = [
    ((C, 3 * C), F32),
    ((C, C), F32),
    ((C, FF), F32),
    ((C, FF), F32),
    ((C, CIN), F32),
    ((8, C), F32),
    ((8, CIN), F32),
    ((8, CIN), F32),
]


def run_middle(flags, h1, up_in, down_in, target, cells, qkv_w, proj_w, up_w, down_t, decode_w, norm_t, scale, prev, sample, count, columns):
    steps = count // columns
    outs = [
        ((count, COL, C), F32),
        ((count, COL, C), F32),
        ((count, HALF, C), BF),
        ((count, HALF, C), BF),
    ]
    first = prev is None
    return pl.pallas_call(
        partial(middle, columns, first=first),
        grid=(steps,),
        in_specs=[
            SMEM,
            rows(columns, COL, C),
            rows(columns, HALF, C),
            rows(columns, HALF, C),
            rows_of(columns, sample * steps, COL, CIN),
            rows_of(columns, sample * steps, 8, COL),
            layer((C, 3 * C), 1),
            layer((C, C), 1),
            layer((C, FF), 1),
            layer((C, FF), 1),
            whole((C, CIN)),
            whole((5, 2, C)),
            whole((1, CIN)),
        ]
        + ([] if first else [whole(shape) for shape, _ in MIDDLE_SUMS]),
        out_specs=[rows(columns, *shape[1:]) for shape, _ in outs] + [whole(shape) for shape, _ in MIDDLE_SUMS],
        out_shape=[struct(*o) for o in outs + MIDDLE_SUMS],
        scratch_shapes=[
            pltpu.VMEM((C, 3 * C), BF),
            pltpu.VMEM((C, C), BF),
            pltpu.VMEM((C, FF), BF),
            pltpu.VMEM((C, FF), BF),
            pltpu.VMEM((C, CIN), BF),
        ],
        compiler_params=pltpu.CompilerParams(vmem_limit_bytes=VMEM_BYTES),
        name="middle",
    )(flags, h1, up_in, down_in, target, cells, qkv_w, proj_w, up_w, down_t, decode_w, norm_t, scale, *(prev or ()))


BACK_SUMS = [
    ((CIN, C), F32),
    ((LEADS, C), F32),
    ((C, 3 * C), F32),
    ((C, C), F32),
    ((C, FF), F32),
    ((C, FF), F32),
    ((8, C), F32),
]


def run_backward(lead_step, tokens, saved, dh2, dn, ret_top, ret_bot, qkv_w, proj_w, up_w, down_t, norm_t, prev, sample, count, columns):
    steps = count // columns
    first = prev is None
    return pl.pallas_call(
        partial(backward_zero, columns, first=first, sample=sample),
        grid=(steps,),
        in_specs=[
            SMEM,
            rows_of(columns, sample * steps, COL, CIN),
            rows(columns, COL, C),
            rows(columns, COL, 3 * C),
            rows(columns, 2, LANES),
            rows(columns, COL, C),
            rows(columns, COL, C),
            rows(columns, COL, FF),
            rows(columns, COL, FF),
            rows(columns, COL, C),
            rows(columns, COL, C),
            rows(columns, COL, C),
            rows(columns, HALF, C),
            rows(columns, HALF, C),
            layer((C, 3 * C), 0),
            layer((C, C), 0),
            layer((C, FF), 0),
            layer((C, FF), 0),
            whole((5, 2, C)),
        ]
        + ([] if first else [whole(shape) for shape, _ in BACK_SUMS]),
        out_specs=[whole(shape) for shape, _ in BACK_SUMS],
        out_shape=[struct(*o) for o in BACK_SUMS],
        scratch_shapes=[
            pltpu.VMEM((C, 3 * C), BF),
            pltpu.VMEM((C, C), BF),
            pltpu.VMEM((C, FF), BF),
            pltpu.VMEM((C, FF), BF),
        ],
        compiler_params=pltpu.CompilerParams(vmem_limit_bytes=VMEM_BYTES),
        name="backward_zero",
    )(lead_step, tokens, *saved, dh2, dn, ret_top, ret_bot, qkv_w, proj_w, up_w, down_t, norm_t, *(prev or ()))


def apply_update(weights, gradients, firsts, seconds, cell_count):
    scaled = [member / cell_count for member in gradients]
    grad_norm = jnp.sqrt(sum((jnp.sum(member * member) for member in scaled)))
    factor = jnp.minimum(1.0, clip_max / grad_norm)
    news, moments, squares = ([], [], [])
    for weight, member, first, second, rate, shrink in zip(
        weights, scaled, firsts, seconds, rate_table, decay_table
    ):
        clipped = member * factor
        first = beta_one * first + (1.0 - beta_one) * clipped
        second = beta_two * second + (1.0 - beta_two) * clipped * clipped
        first_hat = first / (1.0 - beta_one**STEP)
        second_hat = second / (1.0 - beta_two**STEP)
        news.append(
            weight - rate * (first_hat / (jnp.sqrt(second_hat) + adam_eps) + shrink * weight)
        )
        moments.append(first)
        squares.append(second)
    return (news, moments, squares, grad_norm)


def neighbours(low, high):
    count = lax.axis_size("lat")
    forward = [(i, i + 1) for i in range(count - 1)]
    backward = [(b, a) for a, b in forward]
    return lax.ppermute(high, "lat", forward), lax.ppermute(low, "lat", backward)


def on_device(analysis, target, lead_step, loss_mask, *state):
    weights, firsts, seconds = state[0:9], state[9:18], state[18:27]
    embed_w, lead_table, qkv_w, proj_w, up_w, down_w, decode_w, norm_params, loss_scale = weights
    samples, blocks = analysis.shape[0], analysis.shape[1]
    tokens = analysis.transpose(0, 1, 2, 4, 3, 5).reshape(samples * blocks, COL, CIN)
    truth = target.transpose(0, 1, 2, 4, 3, 5).reshape(samples * blocks, COL, CIN)
    cells = loss_mask.transpose(0, 1, 2, 4, 3).reshape(samples * blocks, 1, COL).astype(BF)
    cells = jnp.pad(cells, ((0, 0), (0, 7), (0, 0)))
    embed_t = embed_w.T
    down_t = down_w.transpose(0, 2, 1)
    norm_t = norm_params.transpose(1, 0, 2)
    scale = loss_scale[None, :]
    at = lax.axis_index("lat")
    flags = jnp.stack(
        [jnp.where(at > 0, 0.0, -1e30), jnp.where(at < lax.axis_size("lat") - 1, 0.0, -1e30)]
    ).astype(F32)

    forward = [
        run_forward(lead_step, tokens, lead_table, embed_t, qkv_w, proj_w, up_w, down_t, norm_t, s, blocks, 1)
        for s in range(samples)
    ]
    edges = [neighbours(f[8], f[9]) for f in forward]
    sums = None
    mids = []
    for s in range(samples):
        up_in, down_in = edges[s]
        out = run_middle(
            flags, forward[s][7], up_in, down_in, truth, cells, qkv_w, proj_w, up_w, down_t, decode_w, norm_t, scale,
            sums, s, blocks, 1,
        )
        sums = out[4:]
        mids.append(out[:4])
    returned = [neighbours(m[2], m[3]) for m in mids]
    back = None
    for s in range(samples):
        ret_top, ret_bot = returned[s]
        back = run_backward(
            lead_step, tokens, forward[s][:8], mids[s][0], mids[s][1], ret_top, ret_bot,
            qkv_w, proj_w, up_w, down_t, norm_t, back, s, blocks, 1,
        )
    sums, back = lax.psum((sums, back), ("lat", "batch"))
    g_qkv1, g_proj1, g_up1, g_down1, g_dec, g_norm1, g_scale, count = sums
    g_embed, g_lead, g_qkv0, g_proj0, g_up0, g_down0, g_norm0 = back
    g_scale = g_scale[0]
    cell_total = count[0, 0]
    cell_count = cell_total * CIN
    loss_sum = jnp.sum((cell_total - g_scale) + loss_scale * cell_total)
    g_norm = jnp.stack(
        [g_norm0[0:2], g_norm0[2:4], g_norm0[4:6], g_norm1[2:4], g_norm1[4:6]], axis=1
    )
    gradients = (
        g_embed,
        g_lead,
        jnp.stack([g_qkv0, g_qkv1]),
        jnp.stack([g_proj0, g_proj1]),
        jnp.stack([g_up0, g_up1]),
        jnp.stack([g_down0, g_down1]).transpose(0, 2, 1),
        g_dec,
        g_norm,
        g_scale,
    )
    news, moments, squares, grad_norm = apply_update(weights, gradients, firsts, seconds, cell_count)
    return (*news, *moments, *squares, loss_sum, cell_count, grad_norm)


def solution(mesh):
    split = P("batch", None, "lat", None, None, None)
    placed = (split, split, P("batch"), P("batch", None, "lat", None, None)) + (P(),) * 27
    return jax.shard_map(
        on_device, mesh=mesh, in_specs=placed, out_specs=(P(),) * 30, check_vma=False
    )
```

```python
from functools import partial
import math

import jax
import jax.numpy as jnp
from jax import lax
from jax.experimental import pallas as pl
from jax.experimental.pallas import tpu as pltpu
from jax.sharding import PartitionSpec as P

HEADS = 6
LEADS = 20
STEP = 10
C = 192
FF = 768
CIN = 128
HDIM = 32
COL = 288
WIN = 144
HALF = 72
LANES = 896
TAIL = COL - 256
KV = 3 * WIN
SCALE = HDIM ** (-0.5)
SCALE2 = SCALE * math.log2(math.e)
BF = jnp.bfloat16
F32 = jnp.float32

beta_one = 0.9
beta_two = 0.999
adam_eps = 1e-08
clip_max = 0.005
rate_table = (0.2, 1.0, 0.2, 0.2, 0.2, 0.2, 0.2, 1.0, 1.0)
decay_table = (0.1, 0.1, 0.1, 0.1, 0.1, 0.1, 0.1, 0.0, 0.0)

VMEM_BYTES = 56 * 1024 * 1024
OFFSET = 1


def dot(a, b):
    return lax.dot_general(a, b, (((1,), (0,)), ((), ())), preferred_element_type=F32)


def dot_nt(a, b):
    return lax.dot_general(a, b, (((1,), (1,)), ((), ())), preferred_element_type=F32)


def dot_tn(a, b):
    return lax.dot_general(a, b, (((0,), (0,)), ((), ())), preferred_element_type=F32)


def drive(parts, offset):
    live = [(at * offset, part) for at, part in enumerate(parts)]
    tick = 0
    while live:
        left = []
        for start, part in live:
            if tick >= start and next(part, 0) == 0:
                continue
            left.append((start, part))
        live = left
        tick += 1


def norm_stats(x):
    center = x - jnp.mean(x, axis=-1, keepdims=True)
    rstd = lax.rsqrt(jnp.mean(center * center, axis=-1, keepdims=True) + 1e-05)
    return center * rstd, rstd


def norm_back(dy, xhat, rstd, gain):
    dxhat = dy * gain
    first = jnp.mean(dxhat, axis=-1, keepdims=True)
    second = jnp.mean(dxhat * xhat, axis=-1, keepdims=True)
    return rstd * (dxhat - first - xhat * second)


def add_norm_grads(acc_ref, index, dy, xhat):
    acc_ref[2 * index : 2 * index + 1] += jnp.sum(dy * xhat, axis=0, keepdims=True)
    acc_ref[2 * index + 1 : 2 * index + 2] += jnp.sum(dy, axis=0, keepdims=True)


def gelu_both(x):
    c0 = math.sqrt(2.0 / math.pi)
    c1 = c0 * 0.044715
    square = x * x
    slope = jnp.tanh(x * (c0 + c1 * square))
    half = 0.5 + 0.5 * slope
    active = x * half
    return active, half + active * ((1.0 - slope) * (c0 + (3.0 * c1) * square))


def head_masks():
    lane = lax.broadcasted_iota(jnp.int32, (1, C), 1) // HDIM
    return [(lane == h).astype(F32).astype(BF) for h in range(HEADS)]


def expand(x, masks, edge):
    rem = [x[128:144] * masks[h] for h in range(HEADS)] + [jnp.zeros((32, C), BF)]
    if edge:
        low = [x[0:64] * masks[h] for h in range(HEADS)]
        high = [x[64:128] * masks[h] for h in (4, 5, 0, 1, 2, 3)]
        return jnp.concatenate(low + rem + high, axis=0)
    return jnp.concatenate([x[0:128] * masks[h] for h in range(HEADS)] + rem, axis=0)


def low_lanes():
    return lax.broadcasted_iota(jnp.int32, (1, 128), 1) % 16 < 8


CHUNKS = ((0, 256), (256, 512), (512, 768), (768, 896))
EDGE_CHUNKS = ((0, 256), (256, 640), (640, 896))


def chunks_of(edge):
    return EDGE_CHUNKS if edge else CHUNKS


def add_bias(scores, bias):
    return jnp.concatenate([scores[0:HALF] + bias, scores[HALF:]], axis=0)


def score_chunk(keys, expanded, edge, at, bias=None):
    a, b = chunks_of(edge)[at]
    if not edge:
        return dot_nt(keys, expanded[a:b])
    if at != 1:
        out = dot_nt(keys[at // 2], expanded[a:b])
        return out if bias is None else add_bias(out, bias[at // 2])
    low = dot_nt(keys[0], expanded[256:512])
    high = dot_nt(keys[1], expanded[384:640])
    rem = jnp.where(low_lanes(), low[:, 128:256], high[:, 0:128])
    low, high = low[:, 0:128], high[:, 128:256]
    if bias is not None:
        low, high = add_bias(low, bias[0]), add_bias(high, bias[1])
        rem = add_bias(rem, jnp.where(low_lanes(), bias[0], bias[1]))
    return jnp.concatenate([low, rem, high], axis=1)


def query_chunk(vals_t, weights, edge, at):
    if not edge:
        return dot(vals_t[64 * at : 64 * at + 64] if at < 3 else vals_t, weights)
    if at != 1:
        return dot(vals_t[at // 2][0:128], weights)
    return dot(vals_t[0], weights[:, 0:256]), dot(vals_t[1], weights[:, 128:384])


def query_gather(parts, masks32, edge):
    if not edge:
        blocks = []
        for both in parts[:3]:
            blocks += [both[0:32, 0:128], both[32:64, 128:256]]
        rem = parts[3]
    else:
        low_a, (low_b, high_b), high_a = parts
        rem = jnp.where(low_lanes(), low_b[:, 128:256], high_b[:, 0:128])
        low_b, high_b = low_b[128:192, 0:128], high_b[128:192, 128:256]
        left = lax.broadcasted_iota(jnp.int32, (1, 128), 1) < 64
        blocks = []
        for h in range(HEADS):
            src_low, src_high, local = (low_a, high_a, h) if h < 4 else (low_b, high_b, h - 4)
            group = slice(128 * (local // 2), 128 * (local // 2) + 128)
            low = src_low[32 * local : 32 * local + 32, group]
            high = src_high[32 * local : 32 * local + 32, group]
            if h % 2:
                low = pltpu.roll(low, 64, 1)
            else:
                high = pltpu.roll(high, 64, 1)
            blocks.append(jnp.where(left, low, high))
    main = jnp.concatenate(blocks, axis=0).T
    back = rem.T
    total = back[0:16] * masks32[0]
    for h in range(1, HEADS):
        total = total + back[16 * h : 16 * h + 16] * masks32[h]
    return jnp.concatenate([main, total], axis=0)


def key_side(weights, expanded, edge):
    if not edge:
        return dot(jnp.concatenate(weights, axis=1), expanded)
    mask = low_lanes()
    rem = weights[1][:, 128:256]
    zero = jnp.zeros((), rem.dtype)
    low = jnp.concatenate([weights[0], weights[1][:, 0:128], jnp.where(mask, rem, zero)], axis=1)
    high = jnp.concatenate([jnp.where(mask, zero, rem), weights[1][:, 256:384], weights[2]], axis=1)
    return dot(low, expanded[0:512]), dot(high, expanded[384:896])


def attention_forward(q, k, vals, masks, masks32, edge, probs_ref, result, bias=None):
    queries = expand(q, masks, edge)
    vals_t = (vals[0].T, vals[1].T) if edge else vals.T
    spans = chunks_of(edge)
    ahead = score_chunk(k, queries, edge, 0, bias)
    yield 1
    parts = []
    for at, (a, b) in enumerate(spans):
        scores = ahead * SCALE2
        if at + 1 < len(spans):
            ahead = score_chunk(k, queries, edge, at + 1, bias)
        expo = jnp.exp2(scores - jnp.max(scores, axis=0, keepdims=True))
        probs = expo * (1.0 / jnp.sum(expo, axis=0, keepdims=True))
        probs_ref[:, a:b] = probs
        yield 1
        parts.append(query_chunk(vals_t, probs.astype(BF), edge, at))
        yield 1
    result.append(query_gather(parts, masks32, edge))


def attention_backward(q, k, vals, probs_ref, dmix, masks, masks32, edge, result):
    queries = expand(q, masks, edge)
    douts = expand(dmix, masks, edge)
    k_t = (k[0].T, k[1].T) if edge else k.T
    spans = chunks_of(edge)
    ahead = score_chunk(vals, douts, edge, 0)
    yield 1
    parts, lows, dlows = [], [], []
    for at, (a, b) in enumerate(spans):
        dprobs = ahead
        if at + 1 < len(spans):
            ahead = score_chunk(vals, douts, edge, at + 1)
        probs = probs_ref[:, a:b]
        row_terms = jnp.sum(dprobs * probs, axis=0, keepdims=True)
        dscores = (probs * (dprobs - row_terms)).astype(BF)
        lows.append(probs.astype(BF))
        dlows.append(dscores)
        yield 1
        parts.append(query_chunk(k_t, dscores, edge, at))
        yield 1
    dvals = key_side(lows, douts, edge)
    yield 1
    dkeys = key_side(dlows, queries, edge)
    yield 1
    dq = query_gather(parts, masks32, edge) * SCALE
    dkeys = (dkeys[0] * SCALE, dkeys[1] * SCALE) if edge else dkeys * SCALE
    result.extend([dq, dkeys, dvals])


def store_wide(out_ref, row, acc_ref, width):
    for j in range(width // 128):
        out_ref[row + C * j : row + C * j + C] = acc_ref[:, 128 * j : 128 * j + 128]


def store_qkv_proj(out_ref, row, qkv_ref, proj_ref):
    store_wide(out_ref, row, qkv_ref, 512)
    out_ref[row + 4 * C : row + 5 * C] = jnp.concatenate([qkv_ref[:, 512:576], proj_ref[:, 128:192]], axis=1)
    out_ref[row + 5 * C : row + 6 * C] = proj_ref[:, 0:128]


def clear_from(out_ref, row):
    if out_ref.shape[0] > row:
        out_ref[row:] = jnp.zeros((out_ref.shape[0] - row, 128), F32)


def store_narrow(out_ref, row, acc_ref, rows):
    out_ref[row : row + rows] = acc_ref[:, 0:128]
    out_ref[row + rows : row + 2 * rows] = jnp.concatenate(
        [acc_ref[:, 128:192], jnp.zeros((rows, 64), F32)], axis=1
    )


FLAT_MIDDLE = 19 * C + 24
FLAT_ZERO = 19 * C + 64


def forward_zero(
    columns,
    sample,
    step_ref,
    an_ref,
    lead_ref,
    embed_ref,
    qkv_ref,
    proj_ref,
    up_ref,
    down_ref,
    norm_ref,
    x0_ref,
    r0_ref,
    pack_ref,
    probs_ref,
    mix_ref,
    x1_ref,
    r1_ref,
    act_ref,
    slope_ref,
    h1_ref,
    top_ref,
    bot_ref,
    wembed,
    wqkv,
    wproj,
    wup,
    wdown,
):
    @pl.when(pl.program_id(0) == 0)
    def _():
        wembed[...] = embed_ref[...].astype(BF)
        wqkv[...] = qkv_ref[0].astype(BF)
        wproj[...] = proj_ref[0].astype(BF)
        wup[...] = up_ref[0].astype(BF)
        wdown[...] = down_ref[0].astype(BF)

    masks = head_masks()
    masks32 = [m.astype(F32) for m in masks]
    lead_row = lead_ref[pl.ds(step_ref[sample] - 1, 1), :]

    def one(col):
        hidden = dot_nt(an_ref[col], wembed[...]) + lead_row
        yield 1
        xhat, rstd = norm_stats(hidden)
        x0_ref[col] = xhat
        r0_ref[col] = rstd
        normed = (xhat * norm_ref[0, 0:1] + norm_ref[0, 1:2]).astype(BF)
        yield 1
        packed = dot(normed, wqkv[...]).astype(BF)
        pack_ref[col] = packed
        yield 1
        mixtures = []
        for w in range(2):
            part = packed[WIN * w : WIN * w + WIN]
            yield from attention_forward(
                part[:, 0:C], part[:, C : 2 * C], part[:, 2 * C :], masks, masks32, False, probs_ref.at[col, w], mixtures
            )
        mixture = jnp.concatenate(mixtures, axis=0).astype(BF)
        mix_ref[col] = mixture
        yield 1
        hidden_two = hidden + dot(mixture, wproj[...])
        yield 1
        xhat, rstd = norm_stats(hidden_two)
        x1_ref[col] = xhat
        r1_ref[col] = rstd
        normed_two = (xhat * norm_ref[1, 0:1] + norm_ref[1, 1:2]).astype(BF)
        yield 1
        yield from feed_forward(normed_two, wup, act_ref.at[col], slope_ref.at[col])
        hidden_one = hidden_two + dot_nt(act_ref[col], wdown[...])
        h1_ref[col] = hidden_one
        yield 1
        xhat, _ = norm_stats(jnp.concatenate([hidden_one[0:HALF], hidden_one[COL - HALF :]], axis=0))
        normed = xhat * norm_ref[2, 0:1] + norm_ref[2, 1:2]
        top_ref[col] = normed[0:HALF].astype(BF)
        bot_ref[col] = normed[HALF:].astype(BF)

    drive([one(col) for col in range(columns)], OFFSET)


def feed_forward(normed_two, wup, act_ref, slope_ref):
    ahead = dot(normed_two, wup[:, 0:256])
    yield 1
    for c in range(3):
        span = slice(256 * c, 256 * c + 256)
        inner = ahead
        if c < 2:
            ahead = dot(normed_two, wup[:, 256 * c + 256 : 256 * c + 512])
        active, slope = gelu_both(inner)
        act_ref[:, span] = active.astype(BF)
        slope_ref[:, span] = slope
        yield 1


def feed_backward(grad_low, wdown, act_ref, slope_ref, normed_two, gup_ref, gdown_ref, du_ref, keep):
    ahead = dot(grad_low, wdown[:, 0:256])
    yield 1
    for c in range(3):
        span = slice(256 * c, 256 * c + 256)
        dactive = ahead
        if c < 2:
            ahead = dot(grad_low, wdown[:, 256 * c + 256 : 256 * c + 512])
        dinner = (dactive * slope_ref[:, span]).astype(BF)
        du_ref[:, span] = dinner
        yield 1
        gdown_ref[:, span] += dot_tn(grad_low[0:256], act_ref[0:256, span])
        yield 1
        gup_ref[:, span] += dot_tn(normed_two[0:256], dinner[0:256])
        yield 1
    keep("act", act_ref[256:COL, :])
    keep("du", du_ref[256:COL, :])
    keep("dm", grad_low[256:COL])
    keep("n2", normed_two[256:COL])


MIDDLE_KEEP = (
    ("act", TAIL, FF),
    ("du", TAIL, FF),
    ("dm", TAIL, C),
    ("n2", TAIL, C),
    ("mix", TAIL, C),
    ("da", TAIL, C),
    ("n", TAIL, C),
    ("dq", TAIL, C),
    ("nkv", KV - 256, C),
    ("dkv", KV - 256, 2 * C),
    ("last", TAIL, C),
    ("dp", TAIL, CIN),
)


def edge_first(ref):
    return jnp.concatenate([ref[0:64], ref[216:280], ref[64:72], ref[280:288], ref[72:216]], axis=0)


def middle(columns, count, first, *refs):
    (
        flag_ref,
        h1_ref,
        up_in_ref,
        down_in_ref,
        target_ref,
        mask_ref,
        qkv_ref,
        proj_ref,
        up_ref,
        down_ref,
        decode_ref,
        norm_ref,
        scale_ref,
    ) = refs[:13]
    refs = refs[13:]
    if not first:
        prev_ref, refs = refs[0], refs[1:]
    (
        dh2_ref,
        dn_ref,
        x2_ref,
        r2_ref,
        dtop_ref,
        dbot_ref,
        flat_ref,
        wqkv,
        wproj,
        wup,
        wdown,
        wdec,
        probs_ref,
        act_ref,
        slope_ref,
        du_ref,
        gqkv_ref,
        gproj_ref,
        gup_ref,
        gdown_ref,
        gdec_ref,
        gnorm_ref,
        gscale_ref,
    ) = refs[:23]
    kept = {name: ref for (name, _, _), ref in zip(MIDDLE_KEEP, refs[23:])}
    sums = (gqkv_ref, gproj_ref, gup_ref, gdown_ref, gdec_ref, gnorm_ref, gscale_ref)
    step = pl.program_id(0)

    @pl.when(step == 0)
    def _():
        wqkv[...] = qkv_ref[0].astype(BF)
        wproj[...] = proj_ref[0].astype(BF)
        wup[...] = up_ref[0].astype(BF)
        wdown[...] = down_ref[0].astype(BF)
        wdec[...] = decode_ref[...].astype(BF)
        for ref in sums:
            ref[...] = jnp.zeros_like(ref)

    masks = head_masks()
    masks32 = [m.astype(F32) for m in masks]
    bias = (flag_ref[0], flag_ref[1])
    inverse = jnp.exp(-scale_ref[...])

    def one(col):
        def keep(name, value):
            rows = value.shape[0]
            at = pl.multiple_of((step * columns + col) * rows, 16)
            kept[name][pl.ds(at, rows), :] = value

        act, slope, du = act_ref.at[col], slope_ref.at[col], du_ref.at[col]
        h1 = edge_first(h1_ref[col])
        xhat_one, rstd_one = norm_stats(h1)
        normed = xhat_one * norm_ref[2, 0:1] + norm_ref[2, 1:2]
        normed_low = normed.astype(BF)
        n_top = jnp.concatenate([up_in_ref[col].astype(F32), normed[0:64], normed[128:136]], axis=0).astype(BF)
        n_bot = jnp.concatenate([down_in_ref[col].astype(F32), normed[64:128], normed[136:144]], axis=0).astype(BF)
        n_kv = jnp.concatenate([n_top, n_bot, normed_low[WIN:]], axis=0)
        yield 1
        keys_vals = dot(n_kv, wqkv[:, C:]).astype(BF)
        yield 1
        queries = dot(normed_low, wqkv[:, 0:C]).astype(BF)
        yield 1
        keys, vals = keys_vals[:, 0:C], keys_vals[:, C:]
        k_edge, v_edge = (keys[0:WIN], keys[WIN : 2 * WIN]), (vals[0:WIN], vals[WIN : 2 * WIN])
        k_mid, v_mid = keys[2 * WIN :], vals[2 * WIN :]
        mixtures = []
        yield from attention_forward(
            queries[0:WIN], k_edge, v_edge, masks, masks32, True, probs_ref.at[col, 0], mixtures, bias
        )
        yield from attention_forward(queries[WIN:], k_mid, v_mid, masks, masks32, False, probs_ref.at[col, 1], mixtures)
        mixture = jnp.concatenate(mixtures, axis=0).astype(BF)
        yield 1
        hidden_two = h1 + dot(mixture, wproj[...])
        yield 1
        xhat_two, rstd_two = norm_stats(hidden_two)
        normed_two = (xhat_two * norm_ref[3, 0:1] + norm_ref[3, 1:2]).astype(BF)
        yield 1
        yield from feed_forward(normed_two, wup, act, slope)
        hidden = hidden_two + dot_nt(act[...], wdown[...])
        yield 1
        xhat, rstd = norm_stats(hidden)
        normed_last = (xhat * norm_ref[4, 0:1] + norm_ref[4, 1:2]).astype(BF)
        yield 1
        predicted = dot(normed_last, wdec[...])
        cells = dot_tn(mask_ref[col], jnp.ones((8, CIN), BF))
        yield 1
        error = predicted - edge_first(target_ref[col])
        cells = edge_first(cells)
        square = error * error + 1.0
        back = lax.rsqrt(square)
        gscale_ref[0:1] += jnp.sum(cells * (1.0 - square * back * inverse), axis=0, keepdims=True)
        gscale_ref[1:2] += jnp.sum(cells, axis=0, keepdims=True)
        dpred = (cells * inverse * error * back).astype(BF)
        yield 1
        dnorm = dot_nt(dpred, wdec[...])
        yield 1
        gdec_ref[...] += dot_tn(normed_last[0:256], dpred[0:256])
        keep("last", normed_last[256:])
        keep("dp", dpred[256:])
        yield 1
        add_norm_grads(gnorm_ref, 2, dnorm, xhat)
        grad = norm_back(dnorm, xhat, rstd, norm_ref[4, 0:1])
        grad_low = grad.astype(BF)
        yield 1
        yield from feed_backward(grad_low, wdown, act, slope, normed_two, gup_ref, gdown_ref, du, keep)
        dnorm = dot_nt(du[...], wup[...])
        yield 1
        add_norm_grads(gnorm_ref, 1, dnorm, xhat_two)
        grad = grad + norm_back(dnorm, xhat_two, rstd_two, norm_ref[3, 0:1])
        grad_low = grad.astype(BF)
        dh2_ref[col, 0:64] = grad[0:64]
        dh2_ref[col, 64:72] = grad[128:136]
        dh2_ref[col, 72:216] = grad[144:288]
        dh2_ref[col, 216:280] = grad[64:128]
        dh2_ref[col, 280:288] = grad[136:144]
        x2_ref[col, 0:64] = xhat_one[0:64]
        x2_ref[col, 64:72] = xhat_one[128:136]
        x2_ref[col, 72:216] = xhat_one[144:288]
        x2_ref[col, 216:280] = xhat_one[64:128]
        x2_ref[col, 280:288] = xhat_one[136:144]
        r2_ref[col, 0:64] = rstd_one[0:64]
        r2_ref[col, 64:72] = rstd_one[128:136]
        r2_ref[col, 72:216] = rstd_one[144:288]
        r2_ref[col, 216:280] = rstd_one[64:128]
        r2_ref[col, 280:288] = rstd_one[136:144]
        yield 1
        dmix = dot_nt(grad_low, wproj[...]).astype(BF)
        yield 1
        gproj_ref[...] += dot_tn(mixture[0:256], grad_low[0:256])
        keep("mix", mixture[256:])
        keep("da", grad_low[256:])
        yield 1
        found = []
        yield from attention_backward(
            queries[0:WIN], k_edge, v_edge, probs_ref.at[col, 0], dmix[0:WIN], masks, masks32, True, found
        )
        yield 1
        yield from attention_backward(
            queries[WIN:], k_mid, v_mid, probs_ref.at[col, 1], dmix[WIN:], masks, masks32, False, found
        )
        dq_e, dk_e, dv_e, dq_m, dk_m, dv_m = found
        dq = jnp.concatenate([dq_e, dq_m], axis=0).astype(BF)
        dk = jnp.concatenate([dk_e[0], dk_e[1], dk_m], axis=0).astype(BF)
        dv = jnp.concatenate([dv_e[0], dv_e[1], dv_m], axis=0).astype(BF)
        dkv = jnp.concatenate([dk, dv], axis=1)
        yield 1
        dn_kv = dot_nt(dkv, wqkv[:, C:])
        dtop_ref[col] = dn_kv[0:HALF].astype(BF)
        dbot_ref[col] = dn_kv[WIN : WIN + HALF].astype(BF)
        yield 1
        dn_q = dot_nt(dq, wqkv[:, 0:C])
        dn_ref[col, 0:64] = dn_q[0:64] + dn_kv[72:136]
        dn_ref[col, 64:72] = dn_q[128:136] + dn_kv[136:144]
        dn_ref[col, 72:216] = dn_q[144:288] + dn_kv[288:432]
        dn_ref[col, 216:280] = dn_q[64:128] + dn_kv[216:280]
        dn_ref[col, 280:288] = dn_q[136:144] + dn_kv[280:288]
        yield 1
        gqkv_ref[:, 0:C] += dot_tn(normed_low[0:256], dq[0:256])
        yield 1
        gqkv_ref[:, C:] += dot_tn(n_kv[0:256], dkv[0:256])
        keep("n", normed_low[256:])
        keep("dq", dq[256:])
        keep("nkv", n_kv[256:])
        keep("dkv", dkv[256:])

    drive([one(col) for col in range(columns)], OFFSET)

    @pl.when(step == pl.num_programs(0) - 1)
    def _():
        gup_ref[...] += dot_tn(kept["n2"][...], kept["du"][...])
        gdown_ref[...] += dot_tn(kept["dm"][...], kept["act"][...])
        gproj_ref[...] += dot_tn(kept["mix"][...], kept["da"][...])
        gqkv_ref[:, 0:C] += dot_tn(kept["n"][...], kept["dq"][...])
        gqkv_ref[:, C:] += dot_tn(kept["nkv"][...], kept["dkv"][...])
        gdec_ref[...] += dot_tn(kept["last"][...], kept["dp"][...])
        store_qkv_proj(flat_ref, 0, gqkv_ref, gproj_ref)
        store_wide(flat_ref, 6 * C, gup_ref, FF)
        store_wide(flat_ref, 12 * C, gdown_ref, FF)
        flat_ref[18 * C : 19 * C] = gdec_ref[...]
        store_narrow(flat_ref, 19 * C, gnorm_ref, 8)
        flat_ref[19 * C + 16 : 19 * C + 24] = gscale_ref[...]
        clear_from(flat_ref, FLAT_MIDDLE)
        if not first:
            flat_ref[...] += prev_ref[...]


ZERO_KEEP = (
    ("act", TAIL, FF),
    ("du", TAIL, FF),
    ("dm", TAIL, C),
    ("n2", TAIL, C),
    ("mix", TAIL, C),
    ("da", TAIL, C),
    ("n", TAIL, C),
    ("dp", TAIL, 3 * C),
    ("an", TAIL, CIN),
    ("dh", TAIL, C),
)


def backward_zero(columns, count, first, sample, *refs):
    step_ref, an_ref, x0_ref, r0_ref, pack_ref, probs_ref, mix_ref, x1_ref, r1_ref, act_ref, slope_ref = refs[:11]
    dh2_ref, dn_ref, x2_ref, r2_ref, ret_top_ref, ret_bot_ref = refs[11:17]
    qkv_ref, proj_ref, up_ref, down_ref, norm_ref = refs[17:22]
    refs = refs[22:]
    if not first:
        prev_ref, refs = refs[0], refs[1:]
    flat_ref, wqkv, wproj, wup, wdown, du_ref = refs[:6]
    sums = refs[6:13]
    gembed_ref, glead_ref, gqkv_ref, gproj_ref, gup_ref, gdown_ref, gnorm_ref = sums
    kept = {name: ref for (name, _, _), ref in zip(ZERO_KEEP, refs[13:])}
    step = pl.program_id(0)

    @pl.when(step == 0)
    def _():
        wqkv[...] = qkv_ref[0].astype(BF)
        wproj[...] = proj_ref[0].astype(BF)
        wup[...] = up_ref[0].astype(BF)
        wdown[...] = down_ref[0].astype(BF)
        for ref in sums:
            ref[...] = jnp.zeros_like(ref)

    masks = head_masks()
    masks32 = [m.astype(F32) for m in masks]
    lead_at = pl.ds(step_ref[sample] - 1, 1)

    def one(col):
        def keep(name, value):
            rows = value.shape[0]
            at = pl.multiple_of((step * columns + col) * rows, 16)
            kept[name][pl.ds(at, rows), :] = value

        dn = jnp.concatenate(
            [
                dn_ref[col, 0:HALF] + ret_top_ref[col].astype(F32),
                dn_ref[col, HALF : COL - HALF],
                dn_ref[col, COL - HALF :] + ret_bot_ref[col].astype(F32),
            ],
            axis=0,
        )
        xhat = x2_ref[col]
        add_norm_grads(gnorm_ref, 2, dn, xhat)
        grad = dh2_ref[col] + norm_back(dn, xhat, r2_ref[col], norm_ref[2, 0:1])
        grad_low = grad.astype(BF)
        yield 1
        xhat = x1_ref[col]
        normed_two = (xhat * norm_ref[1, 0:1] + norm_ref[1, 1:2]).astype(BF)
        yield 1
        yield from feed_backward(
            grad_low, wdown, act_ref.at[col], slope_ref.at[col], normed_two, gup_ref, gdown_ref, du_ref.at[col], keep
        )
        dnorm = dot_nt(du_ref[col], wup[...])
        yield 1
        add_norm_grads(gnorm_ref, 1, dnorm, xhat)
        grad = grad + norm_back(dnorm, xhat, r1_ref[col], norm_ref[1, 0:1])
        grad_low = grad.astype(BF)
        yield 1
        dmix = dot_nt(grad_low, wproj[...]).astype(BF)
        yield 1
        gproj_ref[...] += dot_tn(mix_ref[col, 0:256], grad_low[0:256])
        keep("mix", mix_ref[col, 256:COL])
        keep("da", grad_low[256:])
        yield 1
        parts = []
        for w in range(2):
            part = pack_ref[col, WIN * w : WIN * w + WIN]
            found = []
            yield from attention_backward(
                part[:, 0:C],
                part[:, C : 2 * C],
                part[:, 2 * C :],
                probs_ref.at[col, w],
                dmix[WIN * w : WIN * w + WIN],
                masks,
                masks32,
                False,
                found,
            )
            parts.append(jnp.concatenate([g.astype(BF) for g in found], axis=1))
        dpacked = jnp.concatenate(parts, axis=0)
        yield 1
        dn = dot_nt(dpacked, wqkv[...])
        yield 1
        xhat = x0_ref[col]
        normed = (xhat * norm_ref[0, 0:1] + norm_ref[0, 1:2]).astype(BF)
        gqkv_ref[...] += dot_tn(normed[0:256], dpacked[0:256])
        keep("n", normed[256:])
        keep("dp", dpacked[256:])
        yield 1
        add_norm_grads(gnorm_ref, 0, dn, xhat)
        grad = grad + norm_back(dn, xhat, r0_ref[col], norm_ref[0, 0:1])
        glead_ref[lead_at, :] += jnp.sum(grad, axis=0, keepdims=True)
        grad_low = grad.astype(BF)
        yield 1
        gembed_ref[...] += dot_tn(grad_low[0:256], an_ref[col, 0:256])
        keep("an", an_ref[col, 256:COL])
        keep("dh", grad_low[256:])

    drive([one(col) for col in range(columns)], OFFSET)

    @pl.when(step == pl.num_programs(0) - 1)
    def _():
        gup_ref[...] += dot_tn(kept["n2"][...], kept["du"][...])
        gdown_ref[...] += dot_tn(kept["dm"][...], kept["act"][...])
        gproj_ref[...] += dot_tn(kept["mix"][...], kept["da"][...])
        gqkv_ref[...] += dot_tn(kept["n"][...], kept["dp"][...])
        gembed_ref[...] += dot_tn(kept["dh"][...], kept["an"][...])
        store_qkv_proj(flat_ref, 0, gqkv_ref, gproj_ref)
        store_wide(flat_ref, 6 * C, gup_ref, FF)
        store_wide(flat_ref, 12 * C, gdown_ref, FF)
        flat_ref[18 * C : 19 * C] = gembed_ref[...]
        store_narrow(flat_ref, 19 * C, gnorm_ref, 8)
        store_narrow(flat_ref, 19 * C + 16, glead_ref, 24)
        clear_from(flat_ref, FLAT_ZERO)
        if not first:
            flat_ref[...] += prev_ref[...]


def exchanges(sizes):
    out = []
    for axis in ("batch", "lat"):
        size = sizes[axis]
        if size % 2 == 0:
            out.append((axis, 1, 2))
            if size > 2:
                out.append((axis, 2, size // 2))
        elif size > 1:
            out.append((axis, 1, size))
    return out


def streams_of(sizes, arrays, rows):
    base = exchanges(sizes)
    unit = 8 * sizes["lat"] * sizes["batch"]
    orders = [base]
    if len(base) == 4:
        orders = [[base[0], base[i], base[j], base[k]] for i, j, k in ORDERS]
    out = []
    for array in range(arrays):
        units = rows // unit
        at = 0
        for n, order in enumerate(orders):
            left = len(orders) - n
            share = units - at if left == 1 else min(units - at, -(-units * SHARES[n] // sum(SHARES)))
            if share:
                out.append((array, at * unit, share * unit, order))
            at += share
    return out


ORDERS = ((1, 2, 3), (2, 1, 3), (3, 1, 2))
SHARES = (2, 2, 1)


def all_sum(streams, arrays, *refs):
    sources, outs, scratch = refs[:arrays], refs[arrays : 2 * arrays], list(refs[2 * arrays :])

    def take(count):
        head = scratch[:count]
        del scratch[:count]
        return head

    met = []
    for _, _, _, order in streams:
        for stage in order:
            if stage not in met:
                met.append(stage)
    places, peers = {}, {}
    for axis, stride, count in met:
        index = lax.axis_index(axis)
        place = lax.rem(index // stride, count)
        others = []
        for hop in range(1, count):
            other = lax.rem(place + hop, count)
            others.append((other, {axis: index + (other - place) * stride}))
        places[axis, stride, count] = place
        peers[axis, stride, count] = others

    barrier = pltpu.get_barrier_semaphore()
    for others in peers.values():
        for _, device in others:
            pl.semaphore_signal(barrier, inc=1, device_id=device, device_id_type=pl.DeviceIdType.MESH)
    pl.semaphore_wait(barrier, sum(len(others) for others in peers.values()))

    def span(place, rows):
        return pl.ds(pl.multiple_of(place * rows, 8), rows)

    def stream(array, start, length, order):
        levels = len(order)
        held, landed, gathered = take(levels), take(levels), take(levels - 1)
        send, recv, send_back, recv_back = take(levels), take(levels), take(levels), take(levels)
        whole_in = sources[array].at[pl.ds(start, length)]
        whole_out = outs[array].at[pl.ds(start, length)]

        def out_copies(s, outgoing):
            rows = held[s].shape[0]
            source = whole_in if s == 0 else held[s - 1]
            place = places[order[s]]
            return [
                pltpu.make_async_remote_copy(
                    src_ref=source.at[span(other, rows)],
                    dst_ref=landed[s].at[place if outgoing else other],
                    send_sem=send[s].at[other],
                    recv_sem=recv[s].at[place if outgoing else other],
                    device_id=device,
                    device_id_type=pl.DeviceIdType.MESH,
                )
                for other, device in peers[order[s]]
            ]

        def back_copies(s, outgoing):
            rows = held[s].shape[0]
            own = held[s] if s == levels - 1 else gathered[s]
            target = whole_out if s == 0 else gathered[s - 1]
            place = places[order[s]]
            return [
                pltpu.make_async_remote_copy(
                    src_ref=own,
                    dst_ref=target.at[span(place if outgoing else other, rows)],
                    send_sem=send_back[s].at[other],
                    recv_sem=recv_back[s].at[place if outgoing else other],
                    device_id=device,
                    device_id_type=pl.DeviceIdType.MESH,
                )
                for other, device in peers[order[s]]
            ]

        for s in range(levels):
            rows = held[s].shape[0]
            source = whole_in if s == 0 else held[s - 1]
            for copy in out_copies(s, True):
                copy.start()
            yield 1
            for copy in out_copies(s, False):
                copy.wait()
            total = source[span(places[order[s]], rows), :]
            for other, _ in peers[order[s]]:
                total = total + landed[s][other]
            held[s][...] = total
        for s in reversed(range(levels)):
            rows = held[s].shape[0]
            own = held[s] if s == levels - 1 else gathered[s]
            target = whole_out if s == 0 else gathered[s - 1]
            for copy in back_copies(s, True):
                copy.start()
            target[span(places[order[s]], rows), :] = own[...]
            yield 1
            for copy in back_copies(s, False):
                copy.wait()

    drive([stream(*each) for each in streams], 0)


def run_all_sum(flats, sizes):
    rows = flats[0].shape[0]
    streams = streams_of(sizes, len(flats), rows)
    scratch = []
    for _, _, length, order in streams:
        held, landed, sems = [], [], []
        for _, _, count in order:
            length //= count
            held.append(pltpu.VMEM((length, 128), F32))
            landed.append(pltpu.VMEM((count, length, 128), F32))
            sems.append(pltpu.SemaphoreType.DMA((count,)))
        scratch += held + landed + held[:-1] + sems * 4
    return pl.pallas_call(
        partial(all_sum, streams, len(flats)),
        out_shape=[struct(flat.shape, F32) for flat in flats],
        in_specs=[pl.BlockSpec(memory_space=pltpu.VMEM)] * len(flats),
        out_specs=[pl.BlockSpec(memory_space=pltpu.VMEM)] * len(flats),
        scratch_shapes=scratch,
        compiler_params=pltpu.CompilerParams(
            collective_id=0, has_side_effects=True, vmem_limit_bytes=VMEM_BYTES
        ),
        name="all_sum",
    )(*flats)


def update(steps, mid_ref, zero_ref, *refs):
    weights, firsts, seconds = refs[0:9], refs[9:18], refs[18:27]
    news, moms, secs = refs[27:36], refs[36:45], refs[45:54]
    small_ref, factor_ref = refs[54], refs[55]
    step = pl.program_id(0)
    scale_at = 19 * C + 16

    @pl.when(step == 0)
    def _():
        total = mid_ref[scale_at + 1 : scale_at + 2]
        count = total * CIN
        inverse = 1.0 / count

        def squares(ref, a, b):
            part = ref[a:b] * inverse
            return jnp.sum((part * part).reshape((b - a) // 8, 8, 128), axis=0)

        row = lax.broadcasted_iota(jnp.int32, (8, 128), 0)
        scale_grad = mid_ref[scale_at : scale_at + 1]
        mean_grad = scale_grad * inverse
        norms = jnp.sum(
            squares(mid_ref, 0, scale_at)
            + squares(zero_ref, 0, FLAT_ZERO)
            + jnp.where(row == 0, mean_grad * mean_grad, 0.0),
        )
        norm = jnp.sqrt(jnp.broadcast_to(norms, (1, 128)))
        factor_ref[...] = jnp.minimum(1.0, clip_max / norm) * inverse
        loss = jnp.broadcast_to(jnp.sum(total - scale_grad + weights[8][...] * total), (1, 128))
        small_ref[...] = jnp.where(row == 0, loss, jnp.where(row == 1, count, norm))

    factor = factor_ref[...]

    def adam(at, where, grad):
        clipped = grad * factor[:, 0 : grad.shape[-1]]
        first = beta_one * firsts[at][where] + (1.0 - beta_one) * clipped
        second = beta_two * seconds[at][where] + ((1.0 - beta_two) * clipped) * clipped
        weight = weights[at][where]
        root = second * (1.0 / (1.0 - beta_two**STEP))
        root = root * lax.rsqrt(root) + adam_eps
        rate = rate_table[at] / (1.0 - beta_one**STEP)
        new = weight - rate * first * pl.reciprocal(root)
        if decay_table[at]:
            new = new - (rate_table[at] * decay_table[at]) * weight
        news[at][where] = new
        moms[at][where] = first
        secs[at][where] = second

    rows = C // steps
    low = step * rows

    def take(ref, base):
        return ref[pl.ds(pl.multiple_of(base + low, 8), rows), :]

    for layer_at, ref in enumerate((zero_ref, mid_ref)):

        def put(at, a, b, grad):
            adam(at, (layer_at, slice(None), slice(a, b)), grad)

        for j in range(4):
            put(2, 128 * j, 128 * j + 128, take(ref, j * C))
        both = take(ref, 4 * C)
        put(2, 512, 576, both[:, 0:64])
        put(3, 128, 192, both[:, 64:128])
        put(3, 0, 128, take(ref, 5 * C))
        for j in range(6):
            put(4, 128 * j, 128 * j + 128, take(ref, (6 + j) * C))
            put(5, 128 * j, 128 * j + 128, take(ref, (12 + j) * C))
    everything = (slice(None), slice(None))
    adam(0, everything, take(zero_ref, 18 * C))
    adam(6, everything, take(mid_ref, 18 * C))

    @pl.when(step == 0)
    def _():
        lead_at = 19 * C + 16
        adam(1, (slice(None), slice(0, 128)), zero_ref[lead_at : lead_at + LEADS])
        adam(1, (slice(None), slice(128, 192)), zero_ref[lead_at + 24 : lead_at + 24 + LEADS, 0:64])
        adam(8, everything, mid_ref[scale_at : scale_at + 1])
        for at, (ref, index) in enumerate(((zero_ref, 0), (zero_ref, 1), (zero_ref, 2), (mid_ref, 1), (mid_ref, 2))):
            a = 19 * C + 2 * index
            adam(7, (at, slice(None), slice(0, 128)), ref[a : a + 2])
            adam(7, (at, slice(None), slice(128, 192)), ref[a + 8 : a + 10, 0:64])


def run_update(mid, zero, weights, firsts, seconds):
    steps = 6
    rows = C // steps
    kinds = (
        ((C, CIN), True),
        ((LEADS, C), False),
        ((2, C, 3 * C), True),
        ((2, C, C), True),
        ((2, C, FF), True),
        ((2, C, FF), True),
        ((C, CIN), True),
        ((5, 2, C), False),
        ((1, CIN), False),
    )
    specs = []
    for shape, cut in kinds:
        if not cut:
            specs.append(whole(shape))
        elif len(shape) == 2:
            specs.append(pl.BlockSpec((rows, shape[1]), lambda i: (i, 0)))
        else:
            specs.append(pl.BlockSpec((2, rows, shape[2]), lambda i: (0, i, 0)))
    shapes = [struct(shape, F32) for shape, _ in kinds]
    out = pl.pallas_call(
        partial(update, steps),
        grid=(steps,),
        in_specs=[whole(mid.shape), whole(zero.shape)] + specs * 3,
        out_specs=specs * 3 + [whole((8, 128))],
        out_shape=shapes * 3 + [struct((8, 128), F32)],
        scratch_shapes=[pltpu.VMEM((1, 128), F32)],
        compiler_params=pltpu.CompilerParams(vmem_limit_bytes=VMEM_BYTES),
        name="update",
    )(mid, zero, *weights, *firsts, *seconds)
    return out[0:9], out[9:18], out[18:27], out[27]


def whole(shape):
    zeros = (0,) * len(shape)
    return pl.BlockSpec(shape, lambda i: zeros)


def layer(shape, index):
    at = (index,) + (0,) * len(shape)
    return pl.BlockSpec((1,) + shape, lambda i: at)


def rows_of(columns, offset, *shape):
    tail = (0,) * len(shape)
    return pl.BlockSpec((columns,) + shape, lambda i: (i + offset,) + tail)


def rows(columns, *shape):
    return rows_of(columns, 0, *shape)


SMEM = pl.BlockSpec(memory_space=pltpu.SMEM)


def struct(shape, dtype):
    return jax.ShapeDtypeStruct(shape, dtype)


def low(*shape):
    return pltpu.VMEM(shape, BF)


def full(*shape):
    return pltpu.VMEM(shape, F32)


def kept_scratch(kept, count):
    return [low(count * rows, width) for _, rows, width in kept]


def run_forward(lead_step, tokens, lead_table, embed_t, qkv_w, proj_w, up_w, down_t, norm_t, sample, count, columns):
    steps = count // columns
    outs = [
        ((count, COL, C), F32),
        ((count, COL, 1), F32),
        ((count, COL, 3 * C), BF),
        ((count, 2, WIN, LANES), F32),
        ((count, COL, C), BF),
        ((count, COL, C), F32),
        ((count, COL, 1), F32),
        ((count, COL, FF), BF),
        ((count, COL, FF), F32),
        ((count, COL, C), F32),
        ((count, HALF, C), BF),
        ((count, HALF, C), BF),
    ]
    return pl.pallas_call(
        partial(forward_zero, columns, sample),
        grid=(steps,),
        in_specs=[
            SMEM,
            rows_of(columns, sample * steps, COL, CIN),
            whole((LEADS, C)),
            whole((C, CIN)),
            layer((C, 3 * C), 0),
            layer((C, C), 0),
            layer((C, FF), 0),
            layer((C, FF), 0),
            whole((5, 2, C)),
        ],
        out_specs=[rows(columns, *shape[1:]) for shape, _ in outs],
        out_shape=[struct(*o) for o in outs],
        scratch_shapes=[low(C, CIN), low(C, 3 * C), low(C, C), low(C, FF), low(C, FF)],
        compiler_params=pltpu.CompilerParams(vmem_limit_bytes=VMEM_BYTES),
        name="forward_zero",
    )(lead_step, tokens, lead_table, embed_t, qkv_w, proj_w, up_w, down_t, norm_t)


def run_middle(flags, h1, up_in, down_in, target, cells, qkv_w, proj_w, up_w, down_t, decode_w, norm_t, scale, prev, flat_rows, sample, count, columns):
    steps = count // columns
    outs = [
        ((count, COL, C), F32),
        ((count, COL, C), F32),
        ((count, COL, C), F32),
        ((count, COL, 1), F32),
        ((count, HALF, C), BF),
        ((count, HALF, C), BF),
    ]
    first = prev is None
    return pl.pallas_call(
        partial(middle, columns, count, first),
        grid=(steps,),
        in_specs=[
            SMEM,
            rows(columns, COL, C),
            rows(columns, HALF, C),
            rows(columns, HALF, C),
            rows_of(columns, sample * steps, COL, CIN),
            rows_of(columns, sample * steps, 8, COL),
            layer((C, 3 * C), 1),
            layer((C, C), 1),
            layer((C, FF), 1),
            layer((C, FF), 1),
            whole((C, CIN)),
            whole((5, 2, C)),
            whole((1, CIN)),
        ]
        + ([] if first else [whole((flat_rows, 128))]),
        out_specs=[rows(columns, *shape[1:]) for shape, _ in outs] + [whole((flat_rows, 128))],
        out_shape=[struct(*o) for o in outs] + [struct((flat_rows, 128), F32)],
        scratch_shapes=[
            low(C, 3 * C),
            low(C, C),
            low(C, FF),
            low(C, FF),
            low(C, CIN),
            full(columns, 2, WIN, LANES),
            low(columns, COL, FF),
            full(columns, COL, FF),
            low(columns, COL, FF),
            full(C, 3 * C),
            full(C, C),
            full(C, FF),
            full(C, FF),
            full(C, CIN),
            full(8, C),
            full(8, CIN),
        ]
        + kept_scratch(MIDDLE_KEEP, count),
        compiler_params=pltpu.CompilerParams(vmem_limit_bytes=VMEM_BYTES),
        name="middle",
    )(flags, h1, up_in, down_in, target, cells, qkv_w, proj_w, up_w, down_t, decode_w, norm_t, scale, *([] if first else [prev]))


def run_backward(lead_step, tokens, saved, mid_out, returned, qkv_w, proj_w, up_w, down_t, norm_t, prev, flat_rows, sample, count, columns):
    steps = count // columns
    first = prev is None
    return pl.pallas_call(
        partial(backward_zero, columns, count, first, sample),
        grid=(steps,),
        in_specs=[
            SMEM,
            rows_of(columns, sample * steps, COL, CIN),
            rows(columns, COL, C),
            rows(columns, COL, 1),
            rows(columns, COL, 3 * C),
            rows(columns, 2, WIN, LANES),
            rows(columns, COL, C),
            rows(columns, COL, C),
            rows(columns, COL, 1),
            rows(columns, COL, FF),
            rows(columns, COL, FF),
            rows(columns, COL, C),
            rows(columns, COL, C),
            rows(columns, COL, C),
            rows(columns, COL, 1),
            rows(columns, HALF, C),
            rows(columns, HALF, C),
            layer((C, 3 * C), 0),
            layer((C, C), 0),
            layer((C, FF), 0),
            layer((C, FF), 0),
            whole((5, 2, C)),
        ]
        + ([] if first else [whole((flat_rows, 128))]),
        out_specs=whole((flat_rows, 128)),
        out_shape=struct((flat_rows, 128), F32),
        scratch_shapes=[
            low(C, 3 * C),
            low(C, C),
            low(C, FF),
            low(C, FF),
            low(columns, COL, FF),
            full(C, CIN),
            full(24, C),
            full(C, 3 * C),
            full(C, C),
            full(C, FF),
            full(C, FF),
            full(8, C),
        ]
        + kept_scratch(ZERO_KEEP, count),
        compiler_params=pltpu.CompilerParams(vmem_limit_bytes=VMEM_BYTES),
        name="backward_zero",
    )(lead_step, tokens, *saved, *mid_out, *returned, qkv_w, proj_w, up_w, down_t, norm_t, *([] if first else [prev]))


def neighbours(low, high):
    count = lax.axis_size("lat")
    forward = [(i, i + 1) for i in range(count - 1)]
    backward = [(b, a) for a, b in forward]
    return lax.ppermute(high, "lat", forward), lax.ppermute(low, "lat", backward)


def views(group):
    embed, lead, qkv, proj, up, down, decode, norm, scale = group
    return (embed.T, lead, qkv, proj, up, down.transpose(0, 2, 1), decode, norm.transpose(1, 0, 2), scale[None, :])


def unviews(group):
    embed, lead, qkv, proj, up, down, decode, norm, scale = group
    return (embed.T, lead, qkv, proj, up, down.transpose(0, 2, 1), decode, norm.transpose(1, 0, 2), scale[0])


def on_device(analysis, target, lead_step, loss_mask, *state):
    weights, firsts, seconds = (views(state[9 * i : 9 * i + 9]) for i in range(3))
    embed_t, lead_table, qkv_w, proj_w, up_w, down_t, decode_w, norm_t, scale = weights
    samples, blocks = analysis.shape[0], analysis.shape[1]
    sizes = {axis: lax.axis_size(axis) for axis in ("lat", "batch")}
    tokens = analysis.transpose(0, 1, 2, 4, 3, 5).reshape(samples * blocks, COL, CIN)
    truth = target.transpose(0, 1, 2, 4, 3, 5).reshape(samples * blocks, COL, CIN)
    cells = loss_mask.transpose(0, 1, 2, 4, 3).reshape(samples * blocks, 1, COL).astype(BF)
    cells = jnp.pad(cells, ((0, 0), (0, 7), (0, 0)))
    at = lax.axis_index("lat")
    flags = jnp.stack([jnp.where(at > 0, 0.0, -1e30), jnp.where(at < sizes["lat"] - 1, 0.0, -1e30)]).astype(F32)
    columns = 2 if blocks % 2 == 0 else 1
    unit = 8 * sizes["lat"] * sizes["batch"]
    flat_rows = -(-max(FLAT_MIDDLE, FLAT_ZERO) // unit) * unit

    forward = [
        run_forward(lead_step, tokens, lead_table, embed_t, qkv_w, proj_w, up_w, down_t, norm_t, s, blocks, columns)
        for s in range(samples)
    ]
    edges = [neighbours(f[10], f[11]) for f in forward]
    mid = None
    mids = []
    for s in range(samples):
        up_in, down_in = edges[s]
        *out, mid = run_middle(
            flags, forward[s][9], up_in, down_in, truth, cells, qkv_w, proj_w, up_w, down_t, decode_w, norm_t, scale,
            mid, flat_rows, s, blocks, columns,
        )
        mids.append(out)
    returned = [neighbours(m[4], m[5]) for m in mids]
    zero = None
    for s in range(samples):
        zero = run_backward(
            lead_step, tokens, forward[s][:9], mids[s][:4], returned[s], qkv_w, proj_w, up_w, down_t, norm_t,
            zero, flat_rows, s, blocks, columns,
        )
    if unit > 8:
        mid, zero = run_all_sum([mid, zero], sizes)
    news, moments, squares, small = run_update(mid, zero, weights, firsts, seconds)
    return (*unviews(news), *unviews(moments), *unviews(squares), small[0, 0], small[1, 0], small[2, 0])


def solution(mesh):
    split = P("batch", None, "lat", None, None, None)
    placed = (split, split, P("batch"), P("batch", None, "lat", None, None)) + (P(),) * 27
    return jax.shard_map(
        on_device, mesh=mesh, in_specs=placed, out_specs=(P(),) * 30, check_vma=False
    )
```

```python
from functools import partial
import math

import jax
import jax.numpy as jnp
from jax import lax
from jax.experimental import pallas as pl
from jax.experimental.pallas import tpu as pltpu
from jax.sharding import PartitionSpec as P

HEADS = 6
LEADS = 20
STEP = 10
C = 192
FF = 768
CIN = 128
HDIM = 32
COL = 288
WIN = 144
HALF = 72
LANES = 896
TAIL = COL - 256
KV = 3 * WIN
SCALE = HDIM ** (-0.5)
SCALE2 = SCALE * math.log2(math.e)
BF = jnp.bfloat16
F32 = jnp.float32

beta_one = 0.9
beta_two = 0.999
adam_eps = 1e-08
clip_max = 0.005
rate_table = (0.2, 1.0, 0.2, 0.2, 0.2, 0.2, 0.2, 1.0, 1.0)
decay_table = (0.1, 0.1, 0.1, 0.1, 0.1, 0.1, 0.1, 0.0, 0.0)

VMEM_BYTES = 60 * 1024 * 1024
OFFSET = 0
COLUMNS = 4
XW = 256


def dot(a, b):
    return lax.dot_general(a, b, (((1,), (0,)), ((), ())), preferred_element_type=F32)


def dot_nt(a, b):
    return lax.dot_general(a, b, (((1,), (1,)), ((), ())), preferred_element_type=F32)


def dot_tn(a, b):
    return lax.dot_general(a, b, (((0,), (0,)), ((), ())), preferred_element_type=F32)


def drive(parts, offset):
    live = [(at * offset, part) for at, part in enumerate(parts)]
    tick = 0
    while live:
        left = []
        for start, part in live:
            if tick >= start and next(part, 0) == 0:
                continue
            left.append((start, part))
        live = left
        tick += 1


def norm_stats(x):
    center = x - jnp.mean(x, axis=-1, keepdims=True)
    rstd = lax.rsqrt(jnp.mean(center * center, axis=-1, keepdims=True) + 1e-05)
    return center * rstd, rstd


def with_rstd(xhat, rstd):
    return jnp.concatenate([xhat, jnp.broadcast_to(rstd, (xhat.shape[0], XW - C))], axis=1)


def norm_back(dy, xhat, rstd, gain):
    dxhat = dy * gain
    first = jnp.mean(dxhat, axis=-1, keepdims=True)
    second = jnp.mean(dxhat * xhat, axis=-1, keepdims=True)
    return rstd * (dxhat - first - xhat * second)


def add_norm_grads(acc_ref, index, dy, xhat):
    acc_ref[2 * index : 2 * index + 1] += jnp.sum(dy * xhat, axis=0, keepdims=True)
    acc_ref[2 * index + 1 : 2 * index + 2] += jnp.sum(dy, axis=0, keepdims=True)


def gelu_both(x):
    c0 = math.sqrt(2.0 / math.pi)
    c1 = c0 * 0.044715
    square = x * x
    slope = jnp.tanh(x * (c0 + c1 * square))
    half = 0.5 + 0.5 * slope
    active = x * half
    return active, half + active * ((1.0 - slope) * (c0 + (3.0 * c1) * square))


def head_masks():
    lane = lax.broadcasted_iota(jnp.int32, (1, C), 1) // HDIM
    return [(lane == h).astype(F32).astype(BF) for h in range(HEADS)]


def expand(x, masks, edge):
    rem = [x[128:144] * masks[h] for h in range(HEADS)] + [jnp.zeros((32, C), BF)]
    if edge:
        low = [x[0:64] * masks[h] for h in range(HEADS)]
        high = [x[64:128] * masks[h] for h in (4, 5, 0, 1, 2, 3)]
        return jnp.concatenate(low + rem + high, axis=0)
    return jnp.concatenate([x[0:128] * masks[h] for h in range(HEADS)] + rem, axis=0)


def low_lanes():
    return lax.broadcasted_iota(jnp.int32, (1, 128), 1) % 16 < 8


CHUNKS = ((0, 256), (256, 512), (512, 768), (768, 896))
EDGE_CHUNKS = ((0, 256), (256, 640), (640, 896))


def chunks_of(edge):
    return EDGE_CHUNKS if edge else CHUNKS


def add_bias(scores, bias):
    return jnp.concatenate([scores[0:HALF] + bias, scores[HALF:]], axis=0)


def score_chunk(keys, expanded, edge, at, bias=None):
    a, b = chunks_of(edge)[at]
    if not edge:
        return dot_nt(keys, expanded[a:b])
    if at != 1:
        out = dot_nt(keys[at // 2], expanded[a:b])
        return out if bias is None else add_bias(out, bias[at // 2])
    low = dot_nt(keys[0], expanded[256:512])
    high = dot_nt(keys[1], expanded[384:640])
    rem = jnp.where(low_lanes(), low[:, 128:256], high[:, 0:128])
    low, high = low[:, 0:128], high[:, 128:256]
    if bias is not None:
        low, high = add_bias(low, bias[0]), add_bias(high, bias[1])
        rem = add_bias(rem, jnp.where(low_lanes(), bias[0], bias[1]))
    return jnp.concatenate([low, rem, high], axis=1)


def query_chunk(vals_t, weights, edge, at):
    if not edge:
        return dot(vals_t[64 * at : 64 * at + 64] if at < 3 else vals_t, weights)
    if at != 1:
        return dot(vals_t[at // 2][0:128], weights)
    return dot(vals_t[0], weights[:, 0:256]), dot(vals_t[1], weights[:, 128:384])


def query_gather(parts, masks32, edge):
    if not edge:
        blocks = []
        for both in parts[:3]:
            blocks += [both[0:32, 0:128], both[32:64, 128:256]]
        rem = parts[3]
    else:
        low_a, (low_b, high_b), high_a = parts
        rem = jnp.where(low_lanes(), low_b[:, 128:256], high_b[:, 0:128])
        low_b, high_b = low_b[128:192, 0:128], high_b[128:192, 128:256]
        left = lax.broadcasted_iota(jnp.int32, (1, 128), 1) < 64
        blocks = []
        for h in range(HEADS):
            src_low, src_high, local = (low_a, high_a, h) if h < 4 else (low_b, high_b, h - 4)
            group = slice(128 * (local // 2), 128 * (local // 2) + 128)
            low = src_low[32 * local : 32 * local + 32, group]
            high = src_high[32 * local : 32 * local + 32, group]
            if h % 2:
                low = pltpu.roll(low, 64, 1)
            else:
                high = pltpu.roll(high, 64, 1)
            blocks.append(jnp.where(left, low, high))
    main = jnp.concatenate(blocks, axis=0).T
    back = rem.T
    total = back[0:16] * masks32[0]
    for h in range(1, HEADS):
        total = total + back[16 * h : 16 * h + 16] * masks32[h]
    return jnp.concatenate([main, total], axis=0)


def key_side(weights, expanded, edge):
    if not edge:
        return dot(jnp.concatenate(weights, axis=1), expanded)
    mask = low_lanes()
    rem = weights[1][:, 128:256]
    zero = jnp.zeros((), rem.dtype)
    low = jnp.concatenate([weights[0], weights[1][:, 0:128], jnp.where(mask, rem, zero)], axis=1)
    high = jnp.concatenate([jnp.where(mask, zero, rem), weights[1][:, 256:384], weights[2]], axis=1)
    return dot(low, expanded[0:512]), dot(high, expanded[384:896])


def attention_forward(q, k, vals, masks, masks32, edge, probs_ref, result, bias=None):
    queries = expand(q, masks, edge)
    vals_t = (vals[0].T, vals[1].T) if edge else vals.T
    spans = chunks_of(edge)
    ahead = score_chunk(k, queries, edge, 0, bias)
    yield 1
    parts = []
    for at, (a, b) in enumerate(spans):
        scores = ahead * SCALE2
        if at + 1 < len(spans):
            ahead = score_chunk(k, queries, edge, at + 1, bias)
        expo = jnp.exp2(scores - jnp.max(scores, axis=0, keepdims=True))
        probs = expo * (1.0 / jnp.sum(expo, axis=0, keepdims=True))
        probs_ref[:, a:b] = probs
        yield 1
        parts.append(query_chunk(vals_t, probs.astype(BF), edge, at))
        yield 1
    result.append(query_gather(parts, masks32, edge))


def attention_backward(q, k, vals, probs_ref, dmix, masks, masks32, edge, result):
    queries = expand(q, masks, edge)
    douts = expand(dmix, masks, edge)
    k_t = (k[0].T, k[1].T) if edge else k.T
    spans = chunks_of(edge)
    ahead = score_chunk(vals, douts, edge, 0)
    yield 1
    parts, lows, dlows = [], [], []
    for at, (a, b) in enumerate(spans):
        dprobs = ahead
        if at + 1 < len(spans):
            ahead = score_chunk(vals, douts, edge, at + 1)
        probs = probs_ref[:, a:b]
        row_terms = jnp.sum(dprobs * probs, axis=0, keepdims=True)
        dscores = (probs * (dprobs - row_terms)).astype(BF)
        lows.append(probs.astype(BF))
        dlows.append(dscores)
        yield 1
        parts.append(query_chunk(k_t, dscores, edge, at))
        yield 1
    dvals = key_side(lows, douts, edge)
    yield 1
    dkeys = key_side(dlows, queries, edge)
    yield 1
    dq = query_gather(parts, masks32, edge) * SCALE
    dkeys = (dkeys[0] * SCALE, dkeys[1] * SCALE) if edge else dkeys * SCALE
    result.extend([dq, dkeys, dvals])


def store_wide(out_ref, row, acc_ref, width):
    for j in range(width // 128):
        out_ref[row + C * j : row + C * j + C] = acc_ref[:, 128 * j : 128 * j + 128]


def store_qkv_proj(out_ref, row, qkv_ref, proj_ref):
    store_wide(out_ref, row, qkv_ref, 512)
    out_ref[row + 4 * C : row + 5 * C] = jnp.concatenate([qkv_ref[:, 512:576], proj_ref[:, 128:192]], axis=1)
    out_ref[row + 5 * C : row + 6 * C] = proj_ref[:, 0:128]


def clear_from(out_ref, row):
    if out_ref.shape[0] > row:
        out_ref[row:] = jnp.zeros((out_ref.shape[0] - row, 128), F32)


def store_narrow(out_ref, row, acc_ref, rows):
    out_ref[row : row + rows] = acc_ref[:, 0:128]
    out_ref[row + rows : row + 2 * rows] = jnp.concatenate(
        [acc_ref[:, 128:192], jnp.zeros((rows, 64), F32)], axis=1
    )


FLAT_MIDDLE = 19 * C + 24
FLAT_ZERO = 19 * C + 64


class Edges:
    def __init__(self, count, per_step, low_ref, high_ref, from_low_ref, from_high_ref, sems):
        self.at, self.count, self.per_step = lax.axis_index("lat"), count, per_step
        self.staged = (low_ref, high_ref)
        self.landing = (from_low_ref, from_high_ref)
        self.send_low, self.send_high, self.recv_low, self.recv_high, self.fill = sems
        self.has_low, self.has_high = self.at > 0, self.at < count - 1

    def greet(self):
        barrier = pltpu.get_barrier_semaphore()

        @pl.when(self.has_low)
        def _():
            pl.semaphore_signal(barrier, inc=1, device_id={"lat": self.at - 1}, device_id_type=pl.DeviceIdType.MESH)

        @pl.when(self.has_high)
        def _():
            pl.semaphore_signal(barrier, inc=1, device_id={"lat": self.at + 1}, device_id_type=pl.DeviceIdType.MESH)

    def met(self):
        there = jnp.where(self.has_low, 1, 0) + jnp.where(self.has_high, 1, 0)
        pl.semaphore_wait(pltpu.get_barrier_semaphore(), there)

    def copies(self, step):
        part = pl.ds(step * self.per_step, self.per_step)
        down = pltpu.make_async_remote_copy(
            src_ref=self.staged[0].at[part],
            dst_ref=self.landing[1].at[part],
            send_sem=self.send_low.at[step],
            recv_sem=self.recv_high.at[step],
            device_id={"lat": self.at - 1},
            device_id_type=pl.DeviceIdType.MESH,
        )
        up = pltpu.make_async_remote_copy(
            src_ref=self.staged[1].at[part],
            dst_ref=self.landing[0].at[part],
            send_sem=self.send_high.at[step],
            recv_sem=self.recv_low.at[step],
            device_id={"lat": self.at + 1},
            device_id_type=pl.DeviceIdType.MESH,
        )
        return down, up

    def send(self, step):
        down, up = self.copies(step)
        pl.when(self.has_low)(down.start)
        pl.when(self.has_high)(up.start)

    def finish(self, steps, zero_ref):
        zero_ref[...] = jnp.zeros_like(zero_ref)
        for step in range(steps):
            down, up = self.copies(step)
            part = pl.ds(step * self.per_step, self.per_step)

            def low_there(down=down, up=up):
                down.wait_send()
                up.wait_recv()

            def high_there(down=down, up=up):
                up.wait_send()
                down.wait_recv()

            pl.when(self.has_low)(low_there)
            pl.when(self.has_high)(high_there)

            def fill(side, part=part):
                copy = pltpu.make_async_copy(zero_ref, self.landing[side].at[part], self.fill)
                copy.start()
                copy.wait()

            pl.when(jnp.logical_not(self.has_low))(partial(fill, 0))
            pl.when(jnp.logical_not(self.has_high))(partial(fill, 1))


def edge_scratch(count, columns):
    steps = count // columns
    return [low(count, HALF, C), low(count, HALF, C), low(columns, HALF, C)] + [
        pltpu.SemaphoreType.DMA((steps,)) for _ in range(4)
    ] + [pltpu.SemaphoreType.DMA]


EDGE_SCRATCH = 8
ANYWHERE = pl.BlockSpec(memory_space=pl.ANY)


def forward_zero(columns, count, bands, *refs):
    an_ref, hot_ref, lead_ref, embed_ref, qkv_ref, proj_ref, up_ref, down_ref, norm_ref = refs[:9]
    x0_ref, pack_ref, probs_ref, mix_ref, x1_ref, act_ref, slope_ref, h1_ref, from_low_ref, from_high_ref = refs[9:19]
    wembed, wqkv, wproj, wup, wdown, top_ref, bot_ref, zero_ref, *sems = refs[19:]
    step = pl.program_id(0)
    edges = Edges(bands, columns, top_ref, bot_ref, from_low_ref, from_high_ref, sems)

    @pl.when(step == 0)
    def _():
        edges.greet()
        wembed[...] = embed_ref[...].astype(BF)
        wqkv[...] = qkv_ref[0].astype(BF)
        wproj[...] = proj_ref[0].astype(BF)
        wup[...] = up_ref[0].astype(BF)
        wdown[...] = down_ref[0].astype(BF)

    masks = head_masks()
    masks32 = [m.astype(F32) for m in masks]
    lead_row = jnp.sum(hot_ref[0, 0:LEADS] * lead_ref[...], axis=0, keepdims=True)

    def one(col):
        hidden = dot_nt(an_ref[col], wembed[...]) + lead_row
        yield 1
        xhat, rstd = norm_stats(hidden)
        x0_ref[col] = with_rstd(xhat, rstd)
        normed = (xhat * norm_ref[0, 0:1] + norm_ref[0, 1:2]).astype(BF)
        yield 1
        packed = dot(normed, wqkv[...]).astype(BF)
        pack_ref[col] = packed
        yield 1
        mixtures = []
        for w in range(2):
            part = packed[WIN * w : WIN * w + WIN]
            yield from attention_forward(
                part[:, 0:C], part[:, C : 2 * C], part[:, 2 * C :], masks, masks32, False, probs_ref.at[col, w], mixtures
            )
        mixture = jnp.concatenate(mixtures, axis=0).astype(BF)
        mix_ref[col] = mixture
        yield 1
        hidden_two = hidden + dot(mixture, wproj[...])
        yield 1
        xhat, rstd = norm_stats(hidden_two)
        x1_ref[col] = with_rstd(xhat, rstd)
        normed_two = (xhat * norm_ref[1, 0:1] + norm_ref[1, 1:2]).astype(BF)
        yield 1
        yield from feed_forward(normed_two, wup, act_ref.at[col], slope_ref.at[col])
        hidden_one = hidden_two + dot_nt(act_ref[col], wdown[...])
        h1_ref[col] = hidden_one
        yield 1
        xhat, _ = norm_stats(jnp.concatenate([hidden_one[0:HALF], hidden_one[COL - HALF :]], axis=0))
        normed = xhat * norm_ref[2, 0:1] + norm_ref[2, 1:2]
        top_ref[step * columns + col] = normed[0:HALF].astype(BF)
        bot_ref[step * columns + col] = normed[HALF:].astype(BF)

    drive([one(col) for col in range(columns)], OFFSET)

    @pl.when(step == 0)
    def _():
        edges.met()

    edges.send(step)

    @pl.when(step == pl.num_programs(0) - 1)
    def _():
        edges.finish(count // columns, zero_ref)


def feed_forward(normed_two, wup, act_ref, slope_ref):
    ahead = dot(normed_two, wup[:, 0:256])
    yield 1
    for c in range(3):
        span = slice(256 * c, 256 * c + 256)
        inner = ahead
        if c < 2:
            ahead = dot(normed_two, wup[:, 256 * c + 256 : 256 * c + 512])
        active, slope = gelu_both(inner)
        act_ref[:, span] = active.astype(BF)
        slope_ref[:, span] = slope
        yield 1


def feed_backward(grad_low, wdown, act_ref, slope_ref, normed_two, gup_ref, gdown_ref, du_ref, keep):
    ahead = dot(grad_low, wdown[:, 0:256])
    yield 1
    for c in range(3):
        span = slice(256 * c, 256 * c + 256)
        dactive = ahead
        if c < 2:
            ahead = dot(grad_low, wdown[:, 256 * c + 256 : 256 * c + 512])
        dinner = (dactive * slope_ref[:, span]).astype(BF)
        du_ref[:, span] = dinner
        yield 1
        gdown_ref[:, span] += dot_tn(grad_low[0:256], act_ref[0:256, span])
        yield 1
        gup_ref[:, span] += dot_tn(normed_two[0:256], dinner[0:256])
        yield 1
    keep("act", act_ref[256:COL, :])
    keep("du", du_ref[256:COL, :])
    keep("dm", grad_low[256:COL])
    keep("n2", normed_two[256:COL])


MIDDLE_KEEP = (
    ("act", TAIL, FF),
    ("du", TAIL, FF),
    ("dm", TAIL, C),
    ("n2", TAIL, C),
    ("mix", TAIL, C),
    ("da", TAIL, C),
    ("n", TAIL, C),
    ("dq", TAIL, C),
    ("nkv", KV - 256, C),
    ("dkv", KV - 256, 2 * C),
    ("last", TAIL, C),
    ("dp", TAIL, CIN),
)


def edge_first(ref):
    return jnp.concatenate([ref[0:64], ref[216:280], ref[64:72], ref[280:288], ref[72:216]], axis=0)


def middle(columns, count, bands, *refs):
    flag_ref, h1_ref, up_in_ref, down_in_ref, target_ref, mask_ref = refs[:6]
    qkv_ref, proj_ref, up_ref, down_ref, decode_ref, norm_ref, scale_ref = refs[6:13]
    grad_ref, dhe_ref, dne_ref, xe_ref, part_ref, flat_ref, from_low_ref, from_high_ref = refs[13:21]
    dtop_ref, dbot_ref, zero_ref, *sems = refs[21 : 21 + EDGE_SCRATCH]
    refs = refs[21 + EDGE_SCRATCH :]
    wqkv, wproj, wup, wdown, wdec, probs_ref, act_ref, slope_ref, du_ref = refs[:9]
    sums = refs[9:16]
    gqkv_ref, gproj_ref, gup_ref, gdown_ref, gdec_ref, gnorm_ref, gscale_ref = sums
    kept = {name: ref for (name, _, _), ref in zip(MIDDLE_KEEP, refs[16:])}
    step = pl.program_id(0)
    group = group_of(count // columns)
    edges = Edges(bands, columns, dtop_ref, dbot_ref, from_low_ref, from_high_ref, sems)

    @pl.when(step == 0)
    def _():
        edges.greet()
        wqkv[...] = qkv_ref[0].astype(BF)
        wproj[...] = proj_ref[0].astype(BF)
        wup[...] = up_ref[0].astype(BF)
        wdown[...] = down_ref[0].astype(BF)
        wdec[...] = decode_ref[...].astype(BF)
        for ref in sums:
            ref[...] = jnp.zeros_like(ref)

    masks = head_masks()
    masks32 = [m.astype(F32) for m in masks]
    bias = (flag_ref[0], flag_ref[1])
    inverse = jnp.exp(-scale_ref[...])

    def one(col):
        def keep(name, value):
            rows = value.shape[0]
            at = pl.multiple_of((lax.rem(step, group) * columns + col) * rows, 16)
            kept[name][pl.ds(at, rows), :] = value

        act, slope, du = act_ref.at[col], slope_ref.at[col], du_ref.at[col]
        h1 = edge_first(h1_ref[col])
        xhat_one, rstd_one = norm_stats(h1)
        normed = xhat_one * norm_ref[2, 0:1] + norm_ref[2, 1:2]
        normed_low = normed.astype(BF)
        n_top = jnp.concatenate([up_in_ref[col].astype(F32), normed[0:64], normed[128:136]], axis=0).astype(BF)
        n_bot = jnp.concatenate([down_in_ref[col].astype(F32), normed[64:128], normed[136:144]], axis=0).astype(BF)
        n_kv = jnp.concatenate([n_top, n_bot, normed_low[WIN:]], axis=0)
        yield 1
        keys_vals = dot(n_kv, wqkv[:, C:]).astype(BF)
        yield 1
        queries = dot(normed_low, wqkv[:, 0:C]).astype(BF)
        yield 1
        keys, vals = keys_vals[:, 0:C], keys_vals[:, C:]
        k_edge, v_edge = (keys[0:WIN], keys[WIN : 2 * WIN]), (vals[0:WIN], vals[WIN : 2 * WIN])
        k_mid, v_mid = keys[2 * WIN :], vals[2 * WIN :]
        mixtures = []
        yield from attention_forward(
            queries[0:WIN], k_edge, v_edge, masks, masks32, True, probs_ref.at[col, 0], mixtures, bias
        )
        yield from attention_forward(queries[WIN:], k_mid, v_mid, masks, masks32, False, probs_ref.at[col, 1], mixtures)
        mixture = jnp.concatenate(mixtures, axis=0).astype(BF)
        yield 1
        hidden_two = h1 + dot(mixture, wproj[...])
        yield 1
        xhat_two, rstd_two = norm_stats(hidden_two)
        normed_two = (xhat_two * norm_ref[3, 0:1] + norm_ref[3, 1:2]).astype(BF)
        yield 1
        yield from feed_forward(normed_two, wup, act, slope)
        hidden = hidden_two + dot_nt(act[...], wdown[...])
        yield 1
        xhat, rstd = norm_stats(hidden)
        normed_last = (xhat * norm_ref[4, 0:1] + norm_ref[4, 1:2]).astype(BF)
        yield 1
        predicted = dot(normed_last, wdec[...])
        cells = dot_tn(mask_ref[col], jnp.ones((8, CIN), BF))
        yield 1
        error = predicted - edge_first(target_ref[col])
        cells = edge_first(cells)
        square = error * error + 1.0
        back = lax.rsqrt(square)
        gscale_ref[0:1] += jnp.sum(cells * (1.0 - square * back * inverse), axis=0, keepdims=True)
        gscale_ref[1:2] += jnp.sum(cells, axis=0, keepdims=True)
        dpred = (cells * inverse * error * back).astype(BF)
        yield 1
        dnorm = dot_nt(dpred, wdec[...])
        yield 1
        gdec_ref[...] += dot_tn(normed_last[0:256], dpred[0:256])
        keep("last", normed_last[256:])
        keep("dp", dpred[256:])
        yield 1
        add_norm_grads(gnorm_ref, 2, dnorm, xhat)
        grad = norm_back(dnorm, xhat, rstd, norm_ref[4, 0:1])
        grad_low = grad.astype(BF)
        yield 1
        yield from feed_backward(grad_low, wdown, act, slope, normed_two, gup_ref, gdown_ref, du, keep)
        dnorm = dot_nt(du[...], wup[...])
        yield 1
        add_norm_grads(gnorm_ref, 1, dnorm, xhat_two)
        grad = grad + norm_back(dnorm, xhat_two, rstd_two, norm_ref[3, 0:1])
        grad_low = grad.astype(BF)
        dhe_ref[col, 0:64] = grad[0:64]
        dhe_ref[col, 64:72] = grad[128:136]
        dhe_ref[col, 72:136] = grad[64:128]
        dhe_ref[col, 136:144] = grad[136:144]
        kept_edge = with_rstd(xhat_one[0:WIN], rstd_one[0:WIN])
        xe_ref[col, 0:64] = kept_edge[0:64]
        xe_ref[col, 64:72] = kept_edge[128:136]
        xe_ref[col, 72:136] = kept_edge[64:128]
        xe_ref[col, 136:144] = kept_edge[136:144]
        yield 1
        dmix = dot_nt(grad_low, wproj[...]).astype(BF)
        yield 1
        gproj_ref[...] += dot_tn(mixture[0:256], grad_low[0:256])
        keep("mix", mixture[256:])
        keep("da", grad_low[256:])
        yield 1
        found = []
        yield from attention_backward(
            queries[0:WIN], k_edge, v_edge, probs_ref.at[col, 0], dmix[0:WIN], masks, masks32, True, found
        )
        yield 1
        yield from attention_backward(
            queries[WIN:], k_mid, v_mid, probs_ref.at[col, 1], dmix[WIN:], masks, masks32, False, found
        )
        dq_e, dk_e, dv_e, dq_m, dk_m, dv_m = found
        dq = jnp.concatenate([dq_e, dq_m], axis=0).astype(BF)
        dk = jnp.concatenate([dk_e[0], dk_e[1], dk_m], axis=0).astype(BF)
        dv = jnp.concatenate([dv_e[0], dv_e[1], dv_m], axis=0).astype(BF)
        dkv = jnp.concatenate([dk, dv], axis=1)
        yield 1
        dn_kv = dot_nt(dkv, wqkv[:, C:])
        dtop_ref[step * columns + col] = dn_kv[0:HALF].astype(BF)
        dbot_ref[step * columns + col] = dn_kv[WIN : WIN + HALF].astype(BF)
        yield 1
        dn_q = dot_nt(dq, wqkv[:, 0:C])
        yield 1
        dne_ref[col, 0:64] = dn_q[0:64] + dn_kv[72:136]
        dne_ref[col, 64:72] = dn_q[128:136] + dn_kv[136:144]
        dne_ref[col, 72:136] = dn_q[64:128] + dn_kv[216:280]
        dne_ref[col, 136:144] = dn_q[136:144] + dn_kv[280:288]
        dnorm = dn_q[WIN:] + dn_kv[2 * WIN :]
        add_norm_grads(gnorm_ref, 0, dnorm, xhat_one[WIN:])
        grad_ref[col] = grad[WIN:] + norm_back(dnorm, xhat_one[WIN:], rstd_one[WIN:], norm_ref[2, 0:1])
        yield 1
        gqkv_ref[:, 0:C] += dot_tn(normed_low[0:256], dq[0:256])
        yield 1
        gqkv_ref[:, C:] += dot_tn(n_kv[0:256], dkv[0:256])
        keep("n", normed_low[256:])
        keep("dq", dq[256:])
        keep("nkv", n_kv[256:])
        keep("dkv", dkv[256:])

    drive([one(col) for col in range(columns)], OFFSET)

    @pl.when(step == 0)
    def _():
        edges.met()

    edges.send(step)

    @pl.when(lax.rem(step, group) == group - 1)
    def _():
        gup_ref[...] += dot_tn(kept["n2"][...], kept["du"][...])
        gdown_ref[...] += dot_tn(kept["dm"][...], kept["act"][...])
        gproj_ref[...] += dot_tn(kept["mix"][...], kept["da"][...])
        gqkv_ref[:, 0:C] += dot_tn(kept["n"][...], kept["dq"][...])
        gqkv_ref[:, C:] += dot_tn(kept["nkv"][...], kept["dkv"][...])
        gdec_ref[...] += dot_tn(kept["last"][...], kept["dp"][...])

    @pl.when(step == pl.num_programs(0) - 1)
    def _():
        store_qkv_proj(flat_ref, 0, gqkv_ref, gproj_ref)
        store_wide(flat_ref, 6 * C, gup_ref, FF)
        store_wide(flat_ref, 12 * C, gdown_ref, FF)
        flat_ref[18 * C : 19 * C] = gdec_ref[...]
        part_ref[...] = gnorm_ref[...]
        gnorm_ref[0:2] = jnp.zeros((2, C), F32)
        store_narrow(flat_ref, 19 * C, gnorm_ref, 8)
        flat_ref[19 * C + 16 : 19 * C + 24] = gscale_ref[...]
        clear_from(flat_ref, FLAT_MIDDLE)
        edges.finish(count // columns, zero_ref)


ZERO_KEEP = (
    ("act", TAIL, FF),
    ("du", TAIL, FF),
    ("dm", TAIL, C),
    ("n2", TAIL, C),
    ("mix", TAIL, C),
    ("da", TAIL, C),
    ("n", TAIL, C),
    ("dp", TAIL, 3 * C),
    ("an", TAIL, CIN),
    ("dh", TAIL, C),
)


def backward_zero(columns, count, *refs):
    an_ref, hot_ref, x0_ref, pack_ref, probs_ref, mix_ref, x1_ref, act_ref, slope_ref = refs[:9]
    grad_in_ref, dhe_ref, dne_ref, xe_ref, part_ref, from_low_ref, from_high_ref = refs[9:16]
    qkv_ref, proj_ref, up_ref, down_ref, norm_ref = refs[16:21]
    flat_ref, wqkv, wproj, wup, wdown, du_ref = refs[21:27]
    sums = refs[27:34]
    gembed_ref, glead_ref, gqkv_ref, gproj_ref, gup_ref, gdown_ref, gnorm_ref = sums
    kept = {name: ref for (name, _, _), ref in zip(ZERO_KEEP, refs[34:])}
    step = pl.program_id(0)
    group = group_of(count // columns)

    @pl.when(step == 0)
    def _():
        wqkv[...] = qkv_ref[0].astype(BF)
        wproj[...] = proj_ref[0].astype(BF)
        wup[...] = up_ref[0].astype(BF)
        wdown[...] = down_ref[0].astype(BF)
        for ref in sums:
            ref[...] = jnp.zeros_like(ref)

    masks = head_masks()
    masks32 = [m.astype(F32) for m in masks]

    def one(col):
        def keep(name, value):
            rows = value.shape[0]
            at = pl.multiple_of((lax.rem(step, group) * columns + col) * rows, 16)
            kept[name][pl.ds(at, rows), :] = value

        dn = dne_ref[col] + jnp.concatenate([from_low_ref[col], from_high_ref[col]], axis=0).astype(F32)
        xhat = xe_ref[col, :, 0:C]
        add_norm_grads(gnorm_ref, 2, dn, xhat)
        edge = dhe_ref[col] + norm_back(dn, xhat, xe_ref[col, :, C : C + 1], norm_ref[2, 0:1])
        grad = jnp.concatenate([edge[0:HALF], grad_in_ref[col], edge[HALF:]], axis=0)
        grad_low = grad.astype(BF)
        yield 1
        xhat = x1_ref[col, :, 0:C]
        normed_two = (xhat * norm_ref[1, 0:1] + norm_ref[1, 1:2]).astype(BF)
        yield 1
        yield from feed_backward(
            grad_low, wdown, act_ref.at[col], slope_ref.at[col], normed_two, gup_ref, gdown_ref, du_ref.at[col], keep
        )
        dnorm = dot_nt(du_ref[col], wup[...])
        yield 1
        add_norm_grads(gnorm_ref, 1, dnorm, xhat)
        grad = grad + norm_back(dnorm, xhat, x1_ref[col, :, C : C + 1], norm_ref[1, 0:1])
        grad_low = grad.astype(BF)
        yield 1
        dmix = dot_nt(grad_low, wproj[...]).astype(BF)
        yield 1
        gproj_ref[...] += dot_tn(mix_ref[col, 0:256], grad_low[0:256])
        keep("mix", mix_ref[col, 256:COL])
        keep("da", grad_low[256:])
        yield 1
        parts = []
        for w in range(2):
            part = pack_ref[col, WIN * w : WIN * w + WIN]
            found = []
            yield from attention_backward(
                part[:, 0:C],
                part[:, C : 2 * C],
                part[:, 2 * C :],
                probs_ref.at[col, w],
                dmix[WIN * w : WIN * w + WIN],
                masks,
                masks32,
                False,
                found,
            )
            parts.append(jnp.concatenate([g.astype(BF) for g in found], axis=1))
        dpacked = jnp.concatenate(parts, axis=0)
        yield 1
        dn = dot_nt(dpacked, wqkv[...])
        yield 1
        xhat = x0_ref[col, :, 0:C]
        normed = (xhat * norm_ref[0, 0:1] + norm_ref[0, 1:2]).astype(BF)
        gqkv_ref[...] += dot_tn(normed[0:256], dpacked[0:256])
        keep("n", normed[256:])
        keep("dp", dpacked[256:])
        yield 1
        add_norm_grads(gnorm_ref, 0, dn, xhat)
        grad = grad + norm_back(dn, xhat, x0_ref[col, :, C : C + 1], norm_ref[0, 0:1])
        glead_ref[...] += hot_ref[0] * jnp.sum(grad, axis=0, keepdims=True)
        grad_low = grad.astype(BF)
        yield 1
        gembed_ref[...] += dot_tn(grad_low[0:256], an_ref[col, 0:256])
        keep("an", an_ref[col, 256:COL])
        keep("dh", grad_low[256:])

    drive([one(col) for col in range(columns)], OFFSET)

    @pl.when(lax.rem(step, group) == group - 1)
    def _():
        gup_ref[...] += dot_tn(kept["n2"][...], kept["du"][...])
        gdown_ref[...] += dot_tn(kept["dm"][...], kept["act"][...])
        gproj_ref[...] += dot_tn(kept["mix"][...], kept["da"][...])
        gqkv_ref[...] += dot_tn(kept["n"][...], kept["dp"][...])
        gembed_ref[...] += dot_tn(kept["dh"][...], kept["an"][...])

    @pl.when(step == pl.num_programs(0) - 1)
    def _():
        gnorm_ref[4:6] += part_ref[0:2]
        store_qkv_proj(flat_ref, 0, gqkv_ref, gproj_ref)
        store_wide(flat_ref, 6 * C, gup_ref, FF)
        store_wide(flat_ref, 12 * C, gdown_ref, FF)
        flat_ref[18 * C : 19 * C] = gembed_ref[...]
        store_narrow(flat_ref, 19 * C, gnorm_ref, 8)
        store_narrow(flat_ref, 19 * C + 16, glead_ref, 24)
        clear_from(flat_ref, FLAT_ZERO)


def exchanges(sizes):
    out = []
    for axis in ("batch", "lat"):
        size = sizes[axis]
        if size % 2 == 0:
            out.append((axis, 1, 2))
            if size > 2:
                out.append((axis, 2, size // 2))
        elif size > 1:
            out.append((axis, 1, size))
    return out


def streams_of(sizes, arrays, rows):
    base = exchanges(sizes)
    unit = 8 * sizes["lat"] * sizes["batch"]
    orders = [base]
    if len(base) == 4:
        orders = [[base[0], base[i], base[j], base[k]] for i, j, k in ORDERS]
    out = []
    for array in range(arrays):
        units = rows // unit
        at = 0
        for n, order in enumerate(orders):
            left = len(orders) - n
            share = units - at if left == 1 else min(units - at, -(-units * SHARES[n] // sum(SHARES)))
            if share:
                out.append((array, at * unit, share * unit, order))
            at += share
    return out


ORDERS = ((1, 2, 3), (2, 1, 3), (3, 1, 2))
SHARES = (2, 2, 1)


def all_sum(streams, arrays, *refs):
    sources, outs, scratch = refs[:arrays], refs[arrays : 2 * arrays], list(refs[2 * arrays :])

    def take(count):
        head = scratch[:count]
        del scratch[:count]
        return head

    met = []
    for _, _, _, order in streams:
        for stage in order:
            if stage not in met:
                met.append(stage)
    places, peers = {}, {}
    for axis, stride, count in met:
        index = lax.axis_index(axis)
        place = lax.rem(index // stride, count)
        others = []
        for hop in range(1, count):
            other = lax.rem(place + hop, count)
            others.append((other, {axis: index + (other - place) * stride}))
        places[axis, stride, count] = place
        peers[axis, stride, count] = others

    barrier = pltpu.get_barrier_semaphore()
    for others in peers.values():
        for _, device in others:
            pl.semaphore_signal(barrier, inc=1, device_id=device, device_id_type=pl.DeviceIdType.MESH)
    pl.semaphore_wait(barrier, sum(len(others) for others in peers.values()))

    def span(place, rows):
        return pl.ds(pl.multiple_of(place * rows, 8), rows)

    def stream(array, start, length, order):
        levels = len(order)
        held, landed, gathered = take(levels), take(levels), take(levels - 1)
        send, recv, send_back, recv_back = take(levels), take(levels), take(levels), take(levels)
        whole_in = sources[array].at[pl.ds(start, length)]
        whole_out = outs[array].at[pl.ds(start, length)]

        def out_copies(s, outgoing):
            rows = held[s].shape[0]
            source = whole_in if s == 0 else held[s - 1]
            place = places[order[s]]
            return [
                pltpu.make_async_remote_copy(
                    src_ref=source.at[span(other, rows)],
                    dst_ref=landed[s].at[place if outgoing else other],
                    send_sem=send[s].at[other],
                    recv_sem=recv[s].at[place if outgoing else other],
                    device_id=device,
                    device_id_type=pl.DeviceIdType.MESH,
                )
                for other, device in peers[order[s]]
            ]

        def back_copies(s, outgoing):
            rows = held[s].shape[0]
            own = held[s] if s == levels - 1 else gathered[s]
            target = whole_out if s == 0 else gathered[s - 1]
            place = places[order[s]]
            return [
                pltpu.make_async_remote_copy(
                    src_ref=own,
                    dst_ref=target.at[span(place if outgoing else other, rows)],
                    send_sem=send_back[s].at[other],
                    recv_sem=recv_back[s].at[place if outgoing else other],
                    device_id=device,
                    device_id_type=pl.DeviceIdType.MESH,
                )
                for other, device in peers[order[s]]
            ]

        for s in range(levels):
            rows = held[s].shape[0]
            source = whole_in if s == 0 else held[s - 1]
            for copy in out_copies(s, True):
                copy.start()
            yield 1
            for copy in out_copies(s, False):
                copy.wait()
            total = source[span(places[order[s]], rows), :]
            for other, _ in peers[order[s]]:
                total = total + landed[s][other]
            held[s][...] = total
        for s in reversed(range(levels)):
            rows = held[s].shape[0]
            own = held[s] if s == levels - 1 else gathered[s]
            target = whole_out if s == 0 else gathered[s - 1]
            for copy in back_copies(s, True):
                copy.start()
            target[span(places[order[s]], rows), :] = own[...]
            yield 1
            for copy in back_copies(s, False):
                copy.wait()

    drive([stream(*each) for each in streams], 0)


def run_all_sum(flats, sizes):
    rows = flats[0].shape[0]
    streams = streams_of(sizes, len(flats), rows)
    scratch = []
    for _, _, length, order in streams:
        held, landed, sems = [], [], []
        for _, _, count in order:
            length //= count
            held.append(pltpu.VMEM((length, 128), F32))
            landed.append(pltpu.VMEM((count, length, 128), F32))
            sems.append(pltpu.SemaphoreType.DMA((count,)))
        scratch += held + landed + held[:-1] + sems * 4
    return pl.pallas_call(
        partial(all_sum, streams, len(flats)),
        out_shape=[struct(flat.shape, F32) for flat in flats],
        in_specs=[pl.BlockSpec(memory_space=pltpu.VMEM)] * len(flats),
        out_specs=[pl.BlockSpec(memory_space=pltpu.VMEM)] * len(flats),
        scratch_shapes=scratch,
        compiler_params=pltpu.CompilerParams(
            collective_id=0, has_side_effects=True, vmem_limit_bytes=VMEM_BYTES
        ),
        name="all_sum",
    )(*flats)


def update(steps, mid_ref, zero_ref, *refs):
    weights, firsts, seconds = refs[0:9], refs[9:18], refs[18:27]
    news, moms, secs = refs[27:36], refs[36:45], refs[45:54]
    small_ref, factor_ref = refs[54], refs[55]
    step = pl.program_id(0)
    scale_at = 19 * C + 16

    @pl.when(step == 0)
    def _():
        total = mid_ref[scale_at + 1 : scale_at + 2]
        count = total * CIN
        inverse = 1.0 / count

        def squares(ref, a, b):
            part = ref[a:b] * inverse
            return jnp.sum((part * part).reshape((b - a) // 8, 8, 128), axis=0)

        row = lax.broadcasted_iota(jnp.int32, (8, 128), 0)
        scale_grad = mid_ref[scale_at : scale_at + 1]
        mean_grad = scale_grad * inverse
        norms = jnp.sum(
            squares(mid_ref, 0, scale_at)
            + squares(zero_ref, 0, FLAT_ZERO)
            + jnp.where(row == 0, mean_grad * mean_grad, 0.0),
        )
        norm = jnp.sqrt(jnp.broadcast_to(norms, (1, 128)))
        factor_ref[...] = jnp.minimum(1.0, clip_max / norm) * inverse
        loss = jnp.broadcast_to(jnp.sum(total - scale_grad + weights[8][...] * total), (1, 128))
        small_ref[...] = jnp.where(row == 0, loss, jnp.where(row == 1, count, norm))

    factor = factor_ref[...]

    def adam(at, where, grad):
        clipped = grad * factor[:, 0 : grad.shape[-1]]
        first = beta_one * firsts[at][where] + (1.0 - beta_one) * clipped
        second = beta_two * seconds[at][where] + ((1.0 - beta_two) * clipped) * clipped
        weight = weights[at][where]
        root = second * (1.0 / (1.0 - beta_two**STEP))
        root = root * lax.rsqrt(root) + adam_eps
        rate = rate_table[at] / (1.0 - beta_one**STEP)
        new = weight - rate * first * pl.reciprocal(root)
        if decay_table[at]:
            new = new - (rate_table[at] * decay_table[at]) * weight
        news[at][where] = new
        moms[at][where] = first
        secs[at][where] = second

    rows = C // steps
    low = step * rows

    def take(ref, base):
        return ref[pl.ds(pl.multiple_of(base + low, 8), rows), :]

    for layer_at, ref in enumerate((zero_ref, mid_ref)):

        def put(at, a, b, grad):
            adam(at, (layer_at, slice(None), slice(a, b)), grad)

        for j in range(4):
            put(2, 128 * j, 128 * j + 128, take(ref, j * C))
        both = take(ref, 4 * C)
        put(2, 512, 576, both[:, 0:64])
        put(3, 128, 192, both[:, 64:128])
        put(3, 0, 128, take(ref, 5 * C))
        for j in range(6):
            put(4, 128 * j, 128 * j + 128, take(ref, (6 + j) * C))
            put(5, 128 * j, 128 * j + 128, take(ref, (12 + j) * C))
    everything = (slice(None), slice(None))
    adam(0, everything, take(zero_ref, 18 * C))
    adam(6, everything, take(mid_ref, 18 * C))

    @pl.when(step == 0)
    def _():
        lead_at = 19 * C + 16
        adam(1, (slice(None), slice(0, 128)), zero_ref[lead_at : lead_at + LEADS])
        adam(1, (slice(None), slice(128, 192)), zero_ref[lead_at + 24 : lead_at + 24 + LEADS, 0:64])
        adam(8, everything, mid_ref[scale_at : scale_at + 1])
        for at, (ref, index) in enumerate(((zero_ref, 0), (zero_ref, 1), (zero_ref, 2), (mid_ref, 1), (mid_ref, 2))):
            a = 19 * C + 2 * index
            adam(7, (at, slice(None), slice(0, 128)), ref[a : a + 2])
            adam(7, (at, slice(None), slice(128, 192)), ref[a + 8 : a + 10, 0:64])


def run_update(mid, zero, weights, firsts, seconds):
    steps = 6
    rows = C // steps
    kinds = (
        ((C, CIN), True),
        ((LEADS, C), False),
        ((2, C, 3 * C), True),
        ((2, C, C), True),
        ((2, C, FF), True),
        ((2, C, FF), True),
        ((C, CIN), True),
        ((5, 2, C), False),
        ((1, CIN), False),
    )
    specs = []
    for shape, cut in kinds:
        if not cut:
            specs.append(whole(shape))
        elif len(shape) == 2:
            specs.append(pl.BlockSpec((rows, shape[1]), lambda i: (i, 0)))
        else:
            specs.append(pl.BlockSpec((2, rows, shape[2]), lambda i: (0, i, 0)))
    shapes = [struct(shape, F32) for shape, _ in kinds]
    out = pl.pallas_call(
        partial(update, steps),
        grid=(steps,),
        in_specs=[whole(mid.shape), whole(zero.shape)] + specs * 3,
        out_specs=specs * 3 + [whole((8, 128))],
        out_shape=shapes * 3 + [struct((8, 128), F32)],
        scratch_shapes=[pltpu.VMEM((1, 128), F32)],
        compiler_params=pltpu.CompilerParams(vmem_limit_bytes=VMEM_BYTES),
        name="update",
    )(mid, zero, *weights, *firsts, *seconds)
    return out[0:9], out[9:18], out[18:27], out[27]


def whole(shape):
    zeros = (0,) * len(shape)
    return pl.BlockSpec(shape, lambda i: zeros)


def layer(shape, index):
    at = (index,) + (0,) * len(shape)
    return pl.BlockSpec((1,) + shape, lambda i: at)


def rows_of(columns, offset, *shape):
    tail = (0,) * len(shape)
    return pl.BlockSpec((columns,) + shape, lambda i: (i + offset,) + tail)


def rows(columns, *shape):
    return rows_of(columns, 0, *shape)


SMEM = pl.BlockSpec(memory_space=pltpu.SMEM)


def struct(shape, dtype):
    return jax.ShapeDtypeStruct(shape, dtype)


def low(*shape):
    return pltpu.VMEM(shape, BF)


def full(*shape):
    return pltpu.VMEM(shape, F32)


def group_of(steps):
    return 2 if steps % 2 == 0 else 1


def kept_scratch(kept, count, columns):
    held = group_of(count // columns) * columns
    return [low(held * rows, width) for _, rows, width in kept]


def run_forward(tokens, hot, lead_table, embed_t, qkv_w, proj_w, up_w, down_t, norm_t, bands, per_sample, columns):
    count = tokens.shape[0]
    steps = count // columns
    outs = [
        ((count, COL, XW), F32),
        ((count, COL, 3 * C), BF),
        ((count, 2, WIN, LANES), F32),
        ((count, COL, C), BF),
        ((count, COL, XW), F32),
        ((count, COL, FF), BF),
        ((count, COL, FF), F32),
        ((count, COL, C), F32),
    ]
    return pl.pallas_call(
        partial(forward_zero, columns, count, bands),
        grid=(steps,),
        in_specs=[
            rows(columns, COL, CIN),
            hot_spec(per_sample // columns),
            whole((LEADS, C)),
            whole((C, CIN)),
            layer((C, 3 * C), 0),
            layer((C, C), 0),
            layer((C, FF), 0),
            layer((C, FF), 0),
            whole((5, 2, C)),
        ],
        out_specs=[rows(columns, *shape[1:]) for shape, _ in outs] + [ANYWHERE] * 2,
        out_shape=[struct(*o) for o in outs] + [struct((count, HALF, C), BF)] * 2,
        scratch_shapes=[low(C, CIN), low(C, 3 * C), low(C, C), low(C, FF), low(C, FF)] + edge_scratch(count, columns),
        compiler_params=pltpu.CompilerParams(vmem_limit_bytes=VMEM_BYTES, collective_id=1, has_side_effects=True),
        name="forward_zero",
    )(tokens, hot, lead_table, embed_t, qkv_w, proj_w, up_w, down_t, norm_t)


def run_middle(flags, h1, up_in, down_in, target, cells, qkv_w, proj_w, up_w, down_t, decode_w, norm_t, scale, flat_rows, bands, columns):
    count = h1.shape[0]
    steps = count // columns
    outs = [
        ((count, WIN, C), F32),
        ((count, WIN, C), F32),
        ((count, WIN, C), F32),
        ((count, WIN, XW), F32),
    ]
    return pl.pallas_call(
        partial(middle, columns, count, bands),
        grid=(steps,),
        in_specs=[
            SMEM,
            rows(columns, COL, C),
            rows(columns, HALF, C),
            rows(columns, HALF, C),
            rows(columns, COL, CIN),
            rows(columns, 8, COL),
            layer((C, 3 * C), 1),
            layer((C, C), 1),
            layer((C, FF), 1),
            layer((C, FF), 1),
            whole((C, CIN)),
            whole((5, 2, C)),
            whole((1, CIN)),
        ],
        out_specs=[rows(columns, *shape[1:]) for shape, _ in outs]
        + [whole((8, C)), whole((flat_rows, 128)), ANYWHERE, ANYWHERE],
        out_shape=[struct(*o) for o in outs]
        + [struct((8, C), F32), struct((flat_rows, 128), F32)]
        + [struct((count, HALF, C), BF)] * 2,
        scratch_shapes=edge_scratch(count, columns)
        + [
            low(C, 3 * C),
            low(C, C),
            low(C, FF),
            low(C, FF),
            low(C, CIN),
            full(columns, 2, WIN, LANES),
            low(columns, COL, FF),
            full(columns, COL, FF),
            low(columns, COL, FF),
            full(C, 3 * C),
            full(C, C),
            full(C, FF),
            full(C, FF),
            full(C, CIN),
            full(8, C),
            full(8, CIN),
        ]
        + kept_scratch(MIDDLE_KEEP, count, columns),
        compiler_params=pltpu.CompilerParams(vmem_limit_bytes=VMEM_BYTES, collective_id=2, has_side_effects=True),
        name="middle",
    )(flags, h1, up_in, down_in, target, cells, qkv_w, proj_w, up_w, down_t, decode_w, norm_t, scale)


def run_backward(tokens, hot, saved, mid_out, qkv_w, proj_w, up_w, down_t, norm_t, flat_rows, per_sample, columns):
    count = tokens.shape[0]
    steps = count // columns
    return pl.pallas_call(
        partial(backward_zero, columns, count),
        grid=(steps,),
        in_specs=[
            rows(columns, COL, CIN),
            hot_spec(per_sample // columns),
            rows(columns, COL, XW),
            rows(columns, COL, 3 * C),
            rows(columns, 2, WIN, LANES),
            rows(columns, COL, C),
            rows(columns, COL, XW),
            rows(columns, COL, FF),
            rows(columns, COL, FF),
            rows(columns, WIN, C),
            rows(columns, WIN, C),
            rows(columns, WIN, C),
            rows(columns, WIN, XW),
            whole((8, C)),
            rows(columns, HALF, C),
            rows(columns, HALF, C),
            layer((C, 3 * C), 0),
            layer((C, C), 0),
            layer((C, FF), 0),
            layer((C, FF), 0),
            whole((5, 2, C)),
        ],
        out_specs=whole((flat_rows, 128)),
        out_shape=struct((flat_rows, 128), F32),
        scratch_shapes=[
            low(C, 3 * C),
            low(C, C),
            low(C, FF),
            low(C, FF),
            low(columns, COL, FF),
            full(C, CIN),
            full(24, C),
            full(C, 3 * C),
            full(C, C),
            full(C, FF),
            full(C, FF),
            full(8, C),
        ]
        + kept_scratch(ZERO_KEEP, count, columns),
        compiler_params=pltpu.CompilerParams(vmem_limit_bytes=VMEM_BYTES),
        name="backward_zero",
    )(tokens, hot, *saved, *mid_out, qkv_w, proj_w, up_w, down_t, norm_t)


def hot_spec(steps):
    return pl.BlockSpec((1, 24, 1), lambda i: (i // steps, 0, 0))


def views(group):
    embed, lead, qkv, proj, up, down, decode, norm, scale = group
    return (embed.T, lead, qkv, proj, up, down.transpose(0, 2, 1), decode, norm.transpose(1, 0, 2), scale[None, :])


def unviews(group):
    embed, lead, qkv, proj, up, down, decode, norm, scale = group
    return (embed.T, lead, qkv, proj, up, down.transpose(0, 2, 1), decode, norm.transpose(1, 0, 2), scale[0])


def on_device(analysis, target, lead_step, loss_mask, *state):
    weights, firsts, seconds = (views(state[9 * i : 9 * i + 9]) for i in range(3))
    embed_t, lead_table, qkv_w, proj_w, up_w, down_t, decode_w, norm_t, scale = weights
    samples, blocks = analysis.shape[0], analysis.shape[1]
    sizes = {axis: lax.axis_size(axis) for axis in ("lat", "batch")}
    tokens = analysis.transpose(0, 1, 2, 4, 3, 5).reshape(samples * blocks, COL, CIN)
    truth = target.transpose(0, 1, 2, 4, 3, 5).reshape(samples * blocks, COL, CIN)
    cells = loss_mask.transpose(0, 1, 2, 4, 3).reshape(samples * blocks, 1, COL).astype(BF)
    cells = jnp.pad(cells, ((0, 0), (0, 7), (0, 0)))
    at = lax.axis_index("lat")
    flags = jnp.stack([jnp.where(at > 0, 0.0, -1e30), jnp.where(at < sizes["lat"] - 1, 0.0, -1e30)]).astype(F32)
    columns = next(c for c in (COLUMNS, 3, 2, 1) if blocks % c == 0)
    unit = 8 * sizes["lat"] * sizes["batch"]
    flat_rows = -(-max(FLAT_MIDDLE, FLAT_ZERO) // unit) * unit
    hot = (jnp.arange(24, dtype=jnp.int32)[None, :, None] == lead_step[:, None, None] - 1).astype(F32)

    *saved, h1, from_low, from_high = run_forward(
        tokens, hot, lead_table, embed_t, qkv_w, proj_w, up_w, down_t, norm_t, sizes["lat"], blocks, columns
    )
    *edge_out, part, mid, back_low, back_high = run_middle(
        flags, h1, from_low, from_high, truth, cells, qkv_w, proj_w, up_w, down_t, decode_w, norm_t, scale,
        flat_rows, sizes["lat"], columns,
    )
    zero = run_backward(
        tokens, hot, saved, (*edge_out, part, back_low, back_high), qkv_w, proj_w, up_w, down_t, norm_t,
        flat_rows, blocks, columns,
    )
    if unit > 8:
        mid, zero = run_all_sum([mid, zero], sizes)
    news, moments, squares, small = run_update(mid, zero, weights, firsts, seconds)
    return (*unviews(news), *unviews(moments), *unviews(squares), small[0, 0], small[1, 0], small[2, 0])


def solution(mesh):
    split = P("batch", None, "lat", None, None, None)
    placed = (split, split, P("batch"), P("batch", None, "lat", None, None)) + (P(),) * 27
    return jax.shard_map(
        on_device, mesh=mesh, in_specs=placed, out_specs=(P(),) * 30, check_vma=False
    )
```

```python
from functools import partial
import math

import jax
import jax.numpy as jnp
from jax import lax
from jax.experimental import pallas as pl
from jax.experimental.pallas import tpu as pltpu
from jax.sharding import PartitionSpec as P

HEADS = 6
LEADS = 20
STEP = 10
C = 192
FF = 768
CIN = 128
HDIM = 32
COL = 288
WIN = 144
HALF = 72
LANES = 896
TAIL = COL - 256
KV = 3 * WIN
SCALE = HDIM ** (-0.5)
SCALE2 = SCALE * math.log2(math.e)
BF = jnp.bfloat16
F32 = jnp.float32

beta_one = 0.9
beta_two = 0.999
adam_eps = 1e-08
clip_max = 0.005
rate_table = (0.2, 1.0, 0.2, 0.2, 0.2, 0.2, 0.2, 1.0, 1.0)
decay_table = (0.1, 0.1, 0.1, 0.1, 0.1, 0.1, 0.1, 0.0, 0.0)

VMEM_BYTES = 61 * 1024 * 1024
COLUMNS = 4
XW = 256


def dot(a, b):
    return lax.dot_general(a, b, (((1,), (0,)), ((), ())), preferred_element_type=F32)


def dot_nt(a, b):
    return lax.dot_general(a, b, (((1,), (1,)), ((), ())), preferred_element_type=F32)


def dot_tn(a, b):
    return lax.dot_general(a, b, (((0,), (0,)), ((), ())), preferred_element_type=F32)


def drive(parts):
    live = list(parts)
    while live:
        marks = [next(part, 0) for part in live]
        live = [part for part, mark in zip(live, marks) if mark == 1]


def norm_stats(x):
    center = x - jnp.mean(x, axis=-1, keepdims=True)
    rstd = lax.rsqrt(jnp.mean(center * center, axis=-1, keepdims=True) + 1e-05)
    return center * rstd, rstd


def with_rstd(xhat, rstd):
    return jnp.concatenate([xhat, jnp.broadcast_to(rstd, (xhat.shape[0], XW - C))], axis=1)


def norm_back(dy, xhat, rstd, gain):
    dxhat = dy * gain
    first = jnp.mean(dxhat, axis=-1, keepdims=True)
    second = jnp.mean(dxhat * xhat, axis=-1, keepdims=True)
    return rstd * (dxhat - first - xhat * second)


def add_norm_grads(acc_ref, index, dy, xhat):
    acc_ref[2 * index : 2 * index + 1] += jnp.sum(dy * xhat, axis=0, keepdims=True)
    acc_ref[2 * index + 1 : 2 * index + 2] += jnp.sum(dy, axis=0, keepdims=True)


def gelu_both(x):
    c0 = math.sqrt(2.0 / math.pi)
    c1 = c0 * 0.044715
    square = x * x
    slope = jnp.tanh(x * (c0 + c1 * square))
    half = 0.5 + 0.5 * slope
    active = x * half
    return active, half + active * ((1.0 - slope) * (c0 + (3.0 * c1) * square))


def head_masks():
    lane = lax.broadcasted_iota(jnp.int32, (1, C), 1) // HDIM
    return [(lane == h).astype(F32).astype(BF) for h in range(HEADS)]


def expand(x, masks, edge):
    rem = [x[128:144] * masks[h] for h in range(HEADS)] + [jnp.zeros((32, C), BF)]
    if edge:
        low = [x[0:64] * masks[h] for h in range(HEADS)]
        high = [x[64:128] * masks[h] for h in (4, 5, 0, 1, 2, 3)]
        return jnp.concatenate(low + rem + high, axis=0)
    return jnp.concatenate([x[0:128] * masks[h] for h in range(HEADS)] + rem, axis=0)


def low_lanes():
    return lax.broadcasted_iota(jnp.int32, (1, 128), 1) % 16 < 8


CHUNKS = ((0, 256), (256, 512), (512, 768), (768, 896))
EDGE_CHUNKS = ((0, 256), (256, 640), (640, 896))


def chunks_of(edge):
    return EDGE_CHUNKS if edge else CHUNKS


def add_bias(scores, bias):
    return jnp.concatenate([scores[0:HALF] + bias, scores[HALF:]], axis=0)


def score_chunk(keys, expanded, edge, at, bias=None):
    a, b = chunks_of(edge)[at]
    if not edge:
        return dot_nt(keys, expanded[a:b])
    if at != 1:
        out = dot_nt(keys[at // 2], expanded[a:b])
        return out if bias is None else add_bias(out, bias[at // 2])
    low = dot_nt(keys[0], expanded[256:512])
    high = dot_nt(keys[1], expanded[384:640])
    rem = jnp.where(low_lanes(), low[:, 128:256], high[:, 0:128])
    low, high = low[:, 0:128], high[:, 128:256]
    if bias is not None:
        low, high = add_bias(low, bias[0]), add_bias(high, bias[1])
        rem = add_bias(rem, jnp.where(low_lanes(), bias[0], bias[1]))
    return jnp.concatenate([low, rem, high], axis=1)


def query_chunk(vals_t, weights, edge, at):
    if not edge:
        return dot(vals_t[64 * at : 64 * at + 64] if at < 3 else vals_t, weights)
    if at != 1:
        return dot(vals_t[at // 2][0:128], weights)
    return dot(vals_t[0], weights[:, 0:256]), dot(vals_t[1], weights[:, 128:384])


def query_gather(parts, masks32, edge):
    if not edge:
        blocks = []
        for both in parts[:3]:
            blocks += [both[0:32, 0:128], both[32:64, 128:256]]
        rem = parts[3]
    else:
        low_a, (low_b, high_b), high_a = parts
        rem = jnp.where(low_lanes(), low_b[:, 128:256], high_b[:, 0:128])
        low_b, high_b = low_b[128:192, 0:128], high_b[128:192, 128:256]
        left = lax.broadcasted_iota(jnp.int32, (1, 128), 1) < 64
        blocks = []
        for h in range(HEADS):
            src_low, src_high, local = (low_a, high_a, h) if h < 4 else (low_b, high_b, h - 4)
            group = slice(128 * (local // 2), 128 * (local // 2) + 128)
            low = src_low[32 * local : 32 * local + 32, group]
            high = src_high[32 * local : 32 * local + 32, group]
            if h % 2:
                low = pltpu.roll(low, 64, 1)
            else:
                high = pltpu.roll(high, 64, 1)
            blocks.append(jnp.where(left, low, high))
    main = jnp.concatenate(blocks, axis=0).T
    back = rem.T
    total = back[0:16] * masks32[0]
    for h in range(1, HEADS):
        total = total + back[16 * h : 16 * h + 16] * masks32[h]
    return jnp.concatenate([main, total], axis=0)


def key_side(weights, expanded, edge):
    if not edge:
        return dot(jnp.concatenate(weights, axis=1), expanded)
    mask = low_lanes()
    rem = weights[1][:, 128:256]
    zero = jnp.zeros((), rem.dtype)
    low = jnp.concatenate([weights[0], weights[1][:, 0:128], jnp.where(mask, rem, zero)], axis=1)
    high = jnp.concatenate([jnp.where(mask, zero, rem), weights[1][:, 256:384], weights[2]], axis=1)
    return dot(low, expanded[0:512]), dot(high, expanded[384:896])


def attention_forward(q, k, vals, masks, masks32, edge, probs_ref, result, bias=None):
    queries = expand(q, masks, edge)
    vals_t = (vals[0].T, vals[1].T) if edge else vals.T
    spans = chunks_of(edge)
    ahead = score_chunk(k, queries, edge, 0, bias)
    yield 1
    parts = []
    for at, (a, b) in enumerate(spans):
        scores = ahead * SCALE2
        if at + 1 < len(spans):
            ahead = score_chunk(k, queries, edge, at + 1, bias)
        expo = jnp.exp2(scores - jnp.max(scores, axis=0, keepdims=True))
        probs = expo * (1.0 / jnp.sum(expo, axis=0, keepdims=True))
        probs_ref[:, a:b] = probs
        yield 1
        parts.append(query_chunk(vals_t, probs.astype(BF), edge, at))
        yield 1
    result.append(query_gather(parts, masks32, edge))


def attention_backward(q, k, vals, probs_ref, dmix, masks, masks32, edge, result):
    queries = expand(q, masks, edge)
    douts = expand(dmix, masks, edge)
    k_t = (k[0].T, k[1].T) if edge else k.T
    spans = chunks_of(edge)
    ahead = score_chunk(vals, douts, edge, 0)
    yield 1
    parts, lows, dlows = [], [], []
    for at, (a, b) in enumerate(spans):
        dprobs = ahead
        probs = probs_ref[:, a:b]
        if at + 1 < len(spans):
            ahead = score_chunk(vals, douts, edge, at + 1)
        row_terms = jnp.sum(dprobs * probs, axis=0, keepdims=True)
        dscores = (probs * (dprobs - row_terms)).astype(BF)
        lows.append(probs.astype(BF))
        dlows.append(dscores)
        yield 1
        parts.append(query_chunk(k_t, dscores, edge, at))
        yield 1
    dvals = key_side(lows, douts, edge)
    yield 1
    dkeys = key_side(dlows, queries, edge)
    yield 1
    dq = query_gather(parts, masks32, edge) * SCALE
    dkeys = (dkeys[0] * SCALE, dkeys[1] * SCALE) if edge else dkeys * SCALE
    result.extend([dq, dkeys, dvals])


def store_wide(out_ref, row, acc_ref, width):
    for j in range(width // 128):
        out_ref[row + C * j : row + C * j + C] = acc_ref[:, 128 * j : 128 * j + 128]


def store_qkv_proj(out_ref, row, qkv_ref, proj_ref):
    store_wide(out_ref, row, qkv_ref, 512)
    out_ref[row + 4 * C : row + 5 * C] = jnp.concatenate([qkv_ref[:, 512:576], proj_ref[:, 128:192]], axis=1)
    out_ref[row + 5 * C : row + 6 * C] = proj_ref[:, 0:128]


def clear_from(out_ref, row):
    if out_ref.shape[0] > row:
        out_ref[row:] = jnp.zeros((out_ref.shape[0] - row, 128), F32)


def store_narrow(out_ref, row, acc_ref, rows):
    out_ref[row : row + rows] = acc_ref[:, 0:128]
    out_ref[row + rows : row + 2 * rows] = jnp.concatenate(
        [acc_ref[:, 128:192], jnp.zeros((rows, 64), F32)], axis=1
    )


FLAT_MIDDLE = 19 * C + 24
FLAT_ZERO = 19 * C + 64


class Edges:
    def __init__(self, count, per_step, low_ref, high_ref, from_low_ref, from_high_ref, sems):
        self.at, self.count, self.per_step = lax.axis_index("lat"), count, per_step
        self.staged = (low_ref, high_ref)
        self.landing = (from_low_ref, from_high_ref)
        self.send_low, self.send_high, self.recv_low, self.recv_high, self.fill = sems
        self.has_low, self.has_high = self.at > 0, self.at < count - 1

    def greet(self):
        barrier = pltpu.get_barrier_semaphore()

        @pl.when(self.has_low)
        def _():
            pl.semaphore_signal(barrier, inc=1, device_id={"lat": self.at - 1}, device_id_type=pl.DeviceIdType.MESH)

        @pl.when(self.has_high)
        def _():
            pl.semaphore_signal(barrier, inc=1, device_id={"lat": self.at + 1}, device_id_type=pl.DeviceIdType.MESH)

    def met(self):
        there = jnp.where(self.has_low, 1, 0) + jnp.where(self.has_high, 1, 0)
        pl.semaphore_wait(pltpu.get_barrier_semaphore(), there)

    def copies(self, step):
        part = pl.ds(step * self.per_step, self.per_step)
        down = pltpu.make_async_remote_copy(
            src_ref=self.staged[0].at[part],
            dst_ref=self.landing[1].at[part],
            send_sem=self.send_low.at[step],
            recv_sem=self.recv_high.at[step],
            device_id={"lat": self.at - 1},
            device_id_type=pl.DeviceIdType.MESH,
        )
        up = pltpu.make_async_remote_copy(
            src_ref=self.staged[1].at[part],
            dst_ref=self.landing[0].at[part],
            send_sem=self.send_high.at[step],
            recv_sem=self.recv_low.at[step],
            device_id={"lat": self.at + 1},
            device_id_type=pl.DeviceIdType.MESH,
        )
        return down, up

    def send(self, step):
        down, up = self.copies(step)
        pl.when(self.has_low)(down.start)
        pl.when(self.has_high)(up.start)

    def finish(self, steps, zero_ref):
        zero_ref[...] = jnp.zeros_like(zero_ref)
        for step in range(steps):
            down, up = self.copies(step)
            part = pl.ds(step * self.per_step, self.per_step)

            def low_there(down=down, up=up):
                down.wait_send()
                up.wait_recv()

            def high_there(down=down, up=up):
                up.wait_send()
                down.wait_recv()

            pl.when(self.has_low)(low_there)
            pl.when(self.has_high)(high_there)

            def fill(side, part=part):
                copy = pltpu.make_async_copy(zero_ref, self.landing[side].at[part], self.fill)
                copy.start()
                copy.wait()

            pl.when(jnp.logical_not(self.has_low))(partial(fill, 0))
            pl.when(jnp.logical_not(self.has_high))(partial(fill, 1))


def edge_scratch(count, columns):
    steps = count // columns
    return [low(count, HALF, C), low(count, HALF, C), low(columns, HALF, C)] + [
        pltpu.SemaphoreType.DMA((steps,)) for _ in range(4)
    ] + [pltpu.SemaphoreType.DMA]


EDGE_SCRATCH = 8
ANYWHERE = pl.BlockSpec(memory_space=pl.ANY)


def lead_hot(step_ref, step, steps):
    sample = step // (steps // step_ref.shape[0])
    return (lax.broadcasted_iota(jnp.int32, (24, 1), 0) == step_ref[sample] - 1).astype(F32)


def forward_zero(columns, count, bands, *refs):
    step_ref, an_ref, lead_ref, embed_ref, qkv_ref, proj_ref, up_ref, down_ref, norm_ref = refs[:9]
    x0_ref, pack_ref, probs_ref, mix_ref, x1_ref, act_ref, slope_ref, h1_ref, from_low_ref, from_high_ref = refs[9:19]
    wembed, wqkv, wproj, wup, wdown, top_ref, bot_ref, zero_ref, *sems = refs[19:]
    step = pl.program_id(0)
    edges = Edges(bands, columns, top_ref, bot_ref, from_low_ref, from_high_ref, sems)

    @pl.when(step == 0)
    def _():
        edges.greet()
        wembed[...] = embed_ref[...].astype(BF)
        wqkv[...] = qkv_ref[0].astype(BF)
        wproj[...] = proj_ref[0].astype(BF)
        wup[...] = up_ref[0].astype(BF)
        wdown[...] = down_ref[0].astype(BF)

    masks = head_masks()
    masks32 = [m.astype(F32) for m in masks]
    lead_row = jnp.sum(lead_hot(step_ref, step, count // columns)[0:LEADS] * lead_ref[...], axis=0, keepdims=True)

    def one(col):
        hidden = dot_nt(an_ref[col], wembed[...]) + lead_row
        yield 1
        xhat, rstd = norm_stats(hidden)
        x0_ref[col] = with_rstd(xhat, rstd)
        normed = (xhat * norm_ref[0, 0:1] + norm_ref[0, 1:2]).astype(BF)
        yield 1
        packed = dot(normed, wqkv[...]).astype(BF)
        pack_ref[col] = packed
        yield 1
        mixtures = []
        for w in range(2):
            part = packed[WIN * w : WIN * w + WIN]

            yield from attention_forward(
                part[:, 0:C], part[:, C : 2 * C], part[:, 2 * C :], masks, masks32, False, probs_ref.at[col, w], mixtures
            )
        mixture = jnp.concatenate(mixtures, axis=0).astype(BF)
        mix_ref[col] = mixture
        yield 1
        hidden_two = hidden + dot(mixture, wproj[...])
        yield 1
        xhat, rstd = norm_stats(hidden_two)
        x1_ref[col] = with_rstd(xhat, rstd)
        normed_two = (xhat * norm_ref[1, 0:1] + norm_ref[1, 1:2]).astype(BF)
        yield 1
        yield from feed_forward(normed_two, wup, act_ref.at[col], slope_ref.at[col])
        hidden_one = hidden_two + dot_nt(act_ref[col], wdown[...])
        h1_ref[col] = hidden_one
        yield 1
        xhat, _ = norm_stats(jnp.concatenate([hidden_one[0:HALF], hidden_one[COL - HALF :]], axis=0))
        normed = xhat * norm_ref[2, 0:1] + norm_ref[2, 1:2]
        top_ref[step * columns + col] = normed[0:HALF].astype(BF)
        bot_ref[step * columns + col] = normed[HALF:].astype(BF)

    drive([one(col) for col in range(columns)])

    @pl.when(step == 0)
    def _():
        edges.met()

    edges.send(step)

    @pl.when(step == pl.num_programs(0) - 1)
    def _():
        edges.finish(count // columns, zero_ref)


def feed_forward(normed_two, wup, act_ref, slope_ref):
    ahead = dot(normed_two, wup[:, 0:256])
    yield 1
    for c in range(3):
        span = slice(256 * c, 256 * c + 256)
        inner = ahead
        if c < 2:
            ahead = dot(normed_two, wup[:, 256 * c + 256 : 256 * c + 512])
        active, slope = gelu_both(inner)
        act_ref[:, span] = active.astype(BF)
        slope_ref[:, span] = slope
        yield 1


def feed_backward(grad_low, wdown, act_ref, slope_ref, normed_two, gup_ref, gdown_ref, du_ref, keep):
    ahead = dot(grad_low, wdown[:, 0:256])
    yield 1
    for c in range(3):
        span = slice(256 * c, 256 * c + 256)
        dactive = ahead
        if c < 2:
            ahead = dot(grad_low, wdown[:, 256 * c + 256 : 256 * c + 512])
        dinner = (dactive * slope_ref[:, span]).astype(BF)
        du_ref[:, span] = dinner
        yield 1
        gdown_ref[:, span] += dot_tn(grad_low[0:256], act_ref[0:256, span])
        yield 1
        gup_ref[:, span] += dot_tn(normed_two[0:256], dinner[0:256])
        yield 1
    keep("act", act_ref[256:COL, :])
    keep("du", du_ref[256:COL, :])
    keep("dm", grad_low[256:COL])
    keep("n2", normed_two[256:COL])


MIDDLE_KEEP = (
    ("act", TAIL, FF),
    ("du", TAIL, FF),
    ("dm", TAIL, C),
    ("n2", TAIL, C),
    ("mix", TAIL, C),
    ("da", TAIL, C),
    ("n", TAIL, C),
    ("dq", TAIL, C),
    ("nkv", KV - 256, C),
    ("dkv", KV - 256, 2 * C),
    ("last", TAIL, C),
    ("dp", TAIL, CIN),
)


def edge_first(ref):
    return jnp.concatenate([ref[0:64], ref[216:280], ref[64:72], ref[280:288], ref[72:216]], axis=0)


def cell_selectors():
    token = lax.broadcasted_iota(jnp.int32, (COL, 24), 0)
    line = lax.broadcasted_iota(jnp.int32, (COL, 24), 1)
    of_line = (token // 24 * 2 + token % 2 == line).astype(F32).astype(BF)
    token = lax.broadcasted_iota(jnp.int32, (COL, 12), 0)
    place = lax.broadcasted_iota(jnp.int32, (COL, 12), 1)
    return of_line, (token % 24 // 2 == place).astype(F32)


def middle(columns, count, bands, *refs):
    h1_ref, up_in_ref, down_in_ref, target_ref, mask_ref = refs[:5]
    qkv_ref, proj_ref, up_ref, down_ref, decode_ref, norm_ref, scale_ref = refs[5:12]
    grad_ref, dhe_ref, dne_ref, xe_ref, part_ref, flat_ref, from_low_ref, from_high_ref = refs[12:20]
    dtop_ref, dbot_ref, zero_ref, *sems = refs[20 : 20 + EDGE_SCRATCH]
    refs = refs[20 + EDGE_SCRATCH :]
    wqkv, wproj, wup, wdown, wdec, line_ref, place_ref, probs_ref, act_ref, slope_ref, du_ref = refs[:11]
    sums = refs[11:18]
    gqkv_ref, gproj_ref, gup_ref, gdown_ref, gdec_ref, gnorm_ref, gscale_ref = sums
    kept = {name: ref for (name, _, _), ref in zip(MIDDLE_KEEP, refs[18:])}
    step = pl.program_id(0)
    group = group_of(count // columns)
    edges = Edges(bands, columns, dtop_ref, dbot_ref, from_low_ref, from_high_ref, sems)

    @pl.when(step == 0)
    def _():
        edges.greet()
        wqkv[...] = qkv_ref[0].astype(BF)
        wproj[...] = proj_ref[0].astype(BF)
        wup[...] = up_ref[0].astype(BF)
        wdown[...] = down_ref[0].astype(BF)
        wdec[...] = decode_ref[...].astype(BF)
        line_ref[...], place_ref[...] = cell_selectors()
        for ref in sums:
            ref[...] = jnp.zeros_like(ref)

    masks = head_masks()
    masks32 = [m.astype(F32) for m in masks]
    bias = (jnp.where(edges.has_low, 0.0, -1e30), jnp.where(edges.has_high, 0.0, -1e30))
    inverse = jnp.exp(-scale_ref[...])

    def one(col):
        def keep(name, value):
            rows = value.shape[0]
            at = pl.multiple_of((lax.rem(step, group) * columns + col) * rows, 16)
            kept[name][pl.ds(at, rows), :] = value

        act, slope, du = act_ref.at[col], slope_ref.at[col], du_ref.at[col]
        h1 = edge_first(h1_ref[col])
        xhat_one, rstd_one = norm_stats(h1)
        normed = xhat_one * norm_ref[2, 0:1] + norm_ref[2, 1:2]
        normed_low = normed.astype(BF)
        n_top = jnp.concatenate([up_in_ref[col].astype(F32), normed[0:64], normed[128:136]], axis=0).astype(BF)
        n_bot = jnp.concatenate([down_in_ref[col].astype(F32), normed[64:128], normed[136:144]], axis=0).astype(BF)
        n_kv = jnp.concatenate([n_top, n_bot, normed_low[WIN:]], axis=0)
        yield 1
        keys_vals = dot(n_kv, wqkv[:, C:]).astype(BF)
        yield 1
        queries = dot(normed_low, wqkv[:, 0:C]).astype(BF)
        yield 1
        keys, vals = keys_vals[:, 0:C], keys_vals[:, C:]
        k_edge, v_edge = (keys[0:WIN], keys[WIN : 2 * WIN]), (vals[0:WIN], vals[WIN : 2 * WIN])
        k_mid, v_mid = keys[2 * WIN :], vals[2 * WIN :]
        mixtures = []
        yield from attention_forward(
            queries[0:WIN], k_edge, v_edge, masks, masks32, True, probs_ref.at[col, 0], mixtures, bias
        )
        yield from attention_forward(queries[WIN:], k_mid, v_mid, masks, masks32, False, probs_ref.at[col, 1], mixtures)
        mixture = jnp.concatenate(mixtures, axis=0).astype(BF)
        yield 1
        hidden_two = h1 + dot(mixture, wproj[...])
        yield 1
        xhat_two, rstd_two = norm_stats(hidden_two)
        normed_two = (xhat_two * norm_ref[3, 0:1] + norm_ref[3, 1:2]).astype(BF)
        yield 1
        yield from feed_forward(normed_two, wup, act, slope)
        hidden = hidden_two + dot_nt(act[...], wdown[...])
        yield 1
        xhat, rstd = norm_stats(hidden)
        normed_last = (xhat * norm_ref[4, 0:1] + norm_ref[4, 1:2]).astype(BF)
        yield 1
        predicted = dot(normed_last, wdec[...])
        cells = dot((dot(line_ref[...], mask_ref[col]) * place_ref[...]).astype(BF), jnp.ones((12, CIN), BF))
        yield 1
        error = predicted - edge_first(target_ref[col])
        cells = edge_first(cells)
        square = error * error + 1.0
        back = lax.rsqrt(square)
        gscale_ref[0:1] += jnp.sum(cells * (1.0 - square * back * inverse), axis=0, keepdims=True)
        gscale_ref[1:2] += jnp.sum(cells, axis=0, keepdims=True)
        dpred = (cells * inverse * error * back).astype(BF)
        yield 1
        dnorm = dot_nt(dpred, wdec[...])
        yield 1
        gdec_ref[...] += dot_tn(normed_last[0:256], dpred[0:256])
        keep("last", normed_last[256:])
        keep("dp", dpred[256:])
        yield 1
        add_norm_grads(gnorm_ref, 2, dnorm, xhat)
        grad = norm_back(dnorm, xhat, rstd, norm_ref[4, 0:1])
        grad_low = grad.astype(BF)
        yield 1
        yield from feed_backward(grad_low, wdown, act, slope, normed_two, gup_ref, gdown_ref, du, keep)
        dnorm = dot_nt(du[...], wup[...])
        yield 1
        add_norm_grads(gnorm_ref, 1, dnorm, xhat_two)
        grad = grad + norm_back(dnorm, xhat_two, rstd_two, norm_ref[3, 0:1])
        grad_low = grad.astype(BF)
        dhe_ref[col, 0:64] = grad[0:64]
        dhe_ref[col, 64:72] = grad[128:136]
        dhe_ref[col, 72:136] = grad[64:128]
        dhe_ref[col, 136:144] = grad[136:144]
        kept_edge = with_rstd(xhat_one[0:WIN], rstd_one[0:WIN])
        xe_ref[col, 0:64] = kept_edge[0:64]
        xe_ref[col, 64:72] = kept_edge[128:136]
        xe_ref[col, 72:136] = kept_edge[64:128]
        xe_ref[col, 136:144] = kept_edge[136:144]
        yield 1
        dmix = dot_nt(grad_low, wproj[...]).astype(BF)
        yield 1
        gproj_ref[...] += dot_tn(mixture[0:256], grad_low[0:256])
        keep("mix", mixture[256:])
        keep("da", grad_low[256:])
        yield 1
        found = []
        yield from attention_backward(
            queries[0:WIN], k_edge, v_edge, probs_ref.at[col, 0], dmix[0:WIN], masks, masks32, True, found
        )
        yield 1
        yield from attention_backward(
            queries[WIN:], k_mid, v_mid, probs_ref.at[col, 1], dmix[WIN:], masks, masks32, False, found
        )
        dq_e, dk_e, dv_e, dq_m, dk_m, dv_m = found
        dq = jnp.concatenate([dq_e, dq_m], axis=0).astype(BF)
        dk = jnp.concatenate([dk_e[0], dk_e[1], dk_m], axis=0).astype(BF)
        dv = jnp.concatenate([dv_e[0], dv_e[1], dv_m], axis=0).astype(BF)
        dkv = jnp.concatenate([dk, dv], axis=1)
        yield 1
        dn_kv = dot_nt(dkv, wqkv[:, C:])
        dtop_ref[step * columns + col] = dn_kv[0:HALF].astype(BF)
        dbot_ref[step * columns + col] = dn_kv[WIN : WIN + HALF].astype(BF)
        yield 1
        dn_q = dot_nt(dq, wqkv[:, 0:C])
        yield 1
        dne_ref[col, 0:64] = dn_q[0:64] + dn_kv[72:136]
        dne_ref[col, 64:72] = dn_q[128:136] + dn_kv[136:144]
        dne_ref[col, 72:136] = dn_q[64:128] + dn_kv[216:280]
        dne_ref[col, 136:144] = dn_q[136:144] + dn_kv[280:288]
        dnorm = dn_q[WIN:] + dn_kv[2 * WIN :]
        add_norm_grads(gnorm_ref, 0, dnorm, xhat_one[WIN:])
        grad_ref[col] = grad[WIN:] + norm_back(dnorm, xhat_one[WIN:], rstd_one[WIN:], norm_ref[2, 0:1])
        yield 1
        gqkv_ref[:, 0:C] += dot_tn(normed_low[0:256], dq[0:256])
        yield 1
        gqkv_ref[:, C:] += dot_tn(n_kv[0:256], dkv[0:256])
        keep("n", normed_low[256:])
        keep("dq", dq[256:])
        keep("nkv", n_kv[256:])
        keep("dkv", dkv[256:])

    drive([one(col) for col in range(columns)])

    @pl.when(step == 0)
    def _():
        edges.met()

    edges.send(step)

    @pl.when(lax.rem(step, group) == group - 1)
    def _():
        gup_ref[...] += dot_tn(kept["n2"][...], kept["du"][...])
        gdown_ref[...] += dot_tn(kept["dm"][...], kept["act"][...])
        gproj_ref[...] += dot_tn(kept["mix"][...], kept["da"][...])
        gqkv_ref[:, 0:C] += dot_tn(kept["n"][...], kept["dq"][...])
        gqkv_ref[:, C:] += dot_tn(kept["nkv"][...], kept["dkv"][...])
        gdec_ref[...] += dot_tn(kept["last"][...], kept["dp"][...])

    @pl.when(step == pl.num_programs(0) - 1)
    def _():
        store_qkv_proj(flat_ref, 0, gqkv_ref, gproj_ref)
        store_wide(flat_ref, 6 * C, gup_ref, FF)
        store_wide(flat_ref, 12 * C, gdown_ref, FF)
        flat_ref[18 * C : 19 * C] = gdec_ref[...]
        part_ref[...] = gnorm_ref[...]
        gnorm_ref[0:2] = jnp.zeros((2, C), F32)
        store_narrow(flat_ref, 19 * C, gnorm_ref, 8)
        flat_ref[19 * C + 16 : 19 * C + 24] = gscale_ref[...]
        clear_from(flat_ref, FLAT_MIDDLE)
        edges.finish(count // columns, zero_ref)


def exchanges(sizes):
    out = []
    for axis in ("batch", "lat"):
        size = sizes[axis]
        if size % 2 == 0:
            out.append((axis, 1, 2))
            if size > 2:
                out.append((axis, 2, size // 2))
        elif size > 1:
            out.append((axis, 1, size))
    return out


ORDERS = ((1, 2, 3), (2, 1, 3), (3, 1, 2))
SHARES = (2, 2, 1)


def streams_of(sizes, rows):
    base = exchanges(sizes)
    unit = 8 * sizes["lat"] * sizes["batch"]
    orders = [base]
    if len(base) == 4:
        orders = [[base[0], base[i], base[j], base[k]] for i, j, k in ORDERS]
    units = rows // unit
    at = 0
    out = []
    for n, order in enumerate(orders):
        share = units - at if n == len(orders) - 1 else min(units - at, -(-units * SHARES[n] // sum(SHARES)))
        if share:
            out.append((at * unit, share * unit, order))
        at += share
    return out


def stream_buffers(streams):
    scratch = []
    for _, length, order in streams:
        held, landed = [], []
        for _, _, count in order:
            length //= count
            held.append(full(length, 128))
            landed.append(full(count - 1, length, 128))
        scratch += held + landed + held[:-1]
    return scratch


def stream_sems(streams):
    out = []
    for _, _, order in streams:
        out += [pltpu.SemaphoreType.DMA((count,)) for _ in range(4) for _, _, count in order] + [pltpu.SemaphoreType.DMA]
    return out


def span(place, rows):
    return pl.ds(pl.multiple_of(place * rows, 8), rows)


class Peers:
    def __init__(self, streams):
        self.places, self.others = {}, {}
        for _, _, order in streams:
            for stage in order:
                if stage in self.places:
                    continue
                axis, stride, count = stage
                index = lax.axis_index(axis)
                place = lax.rem(index // stride, count)
                self.places[stage] = place
                self.others[stage] = []
                for hop in range(1, count):
                    other = lax.rem(place + hop, count)
                    self.others[stage].append((other, {axis: index + (other - place) * stride}))

    def greet(self):
        barrier = pltpu.get_barrier_semaphore()
        for others in self.others.values():
            for _, device in others:
                pl.semaphore_signal(barrier, inc=1, device_id=device, device_id_type=pl.DeviceIdType.MESH)

    def met(self):
        number = sum(len(others) for others in self.others.values())
        if number:
            pl.semaphore_wait(pltpu.get_barrier_semaphore(), number)

    def stream(self, which, source_ref, target_ref, buffers, sems):
        start, length, order = which
        levels = len(order)

        def take(scratch, count):
            head = scratch[:count]
            del scratch[:count]
            return head

        held, landed, gathered = (take(buffers, count) for count in (levels, levels, max(levels - 1, 0)))
        send, recv, send_back, recv_back = (take(sems, levels) for _ in range(4))
        (own_sem,) = take(sems, 1)
        sources = [source_ref.at[pl.ds(start, length)]] + held
        targets = [target_ref.at[pl.ds(start, length)]] + gathered + held[-1:]

        def remote(source, target, send_sem, recv_sem, device):
            return pltpu.make_async_remote_copy(
                src_ref=source,
                dst_ref=target,
                send_sem=send_sem,
                recv_sem=recv_sem,
                device_id=device,
                device_id_type=pl.DeviceIdType.MESH,
            )

        def out(s, outgoing):
            rows, place = held[s].shape[0], self.places[order[s]]
            return [
                remote(
                    sources[s].at[span(other, rows)],
                    landed[s].at[order[s][2] - 2 - hop if outgoing else hop],
                    send[s].at[other],
                    recv[s].at[place if outgoing else other],
                    device,
                )
                for hop, (other, device) in enumerate(self.others[order[s]])
            ]

        def back(s, outgoing):
            rows, place = held[s].shape[0], self.places[order[s]]
            return [
                remote(
                    targets[s + 1],
                    targets[s].at[span(place if outgoing else other, rows)],
                    send_back[s].at[other],
                    recv_back[s].at[place if outgoing else other],
                    device,
                )
                for other, device in self.others[order[s]]
            ]

        def start_out(s):
            for copy in out(s, True):
                copy.start()

        def end_out(s):
            for copy in out(s, False):
                copy.wait()
            rows = held[s].shape[0]
            total = sources[s][span(self.places[order[s]], rows), :]
            for hop in range(order[s][2] - 1):
                total = total + landed[s][hop]
            held[s][...] = total

        def start_back(s):
            for copy in back(s, True):
                copy.start()
            place = span(self.places[order[s]], held[s].shape[0])
            if s:
                targets[s][place, :] = targets[s + 1][...]
            else:
                pltpu.make_async_copy(targets[1], targets[0].at[place], own_sem).start()

        def end_back(s):
            for copy in back(s, False):
                copy.wait()
            if not s:
                place = span(self.places[order[0]], held[0].shape[0])
                pltpu.make_async_copy(targets[1], targets[0].at[place], own_sem).wait()

        if not levels:

            def alone():
                copy = pltpu.make_async_copy(source_ref, target_ref, own_sem)
                copy.start()
                copy.wait()

            return [alone]
        moves = [(start_out, end_out, s) for s in range(levels)]
        moves += [(start_back, end_back, s) for s in reversed(range(levels))]

        def tick(at):
            def run():
                if at:
                    _, end, s = moves[at - 1]
                    end(s)
                if at < len(moves):
                    begin, _, s = moves[at]
                    begin(s)

            return run

        return [tick(at) for at in range(len(moves) + 1)]


ZERO_KEEP = (
    ("act", TAIL, FF),
    ("du", TAIL, FF),
    ("dm", TAIL, C),
    ("n2", TAIL, C),
    ("mix", TAIL, C),
    ("da", TAIL, C),
    ("n", TAIL, C),
    ("dp", TAIL, 3 * C),
    ("an", TAIL, CIN),
    ("dh", TAIL, C),
)


def backward_zero(columns, count, streams, *refs):
    step_ref, an_ref, x0_ref, pack_ref, probs_ref, mix_ref, x1_ref, act_ref, slope_ref = refs[:9]
    grad_in_ref, dhe_ref, dne_ref, xe_ref, part_ref, from_low_ref, from_high_ref = refs[9:16]
    qkv_ref, proj_ref, up_ref, down_ref, norm_ref, mid_ref, mid_out_ref, zero_out_ref = refs[16:24]
    flat_ref, wqkv, wproj, wup, wdown, du_ref = refs[24:30]
    sums = refs[30:37]
    gembed_ref, glead_ref, gqkv_ref, gproj_ref, gup_ref, gdown_ref, gnorm_ref = sums
    kept = {name: ref for (name, _, _), ref in zip(ZERO_KEEP, refs[37:])}
    step = pl.program_id(0)
    steps = count // columns
    group = group_of(steps)
    comm = list(refs[37 + len(ZERO_KEEP) :])
    kinds = (stream_buffers(streams), stream_sems(streams))
    early_comm, late_comm = [], []
    for kind in kinds:
        for group_comm in (early_comm, late_comm):
            group_comm.append(comm[: len(kind)])
            del comm[: len(kind)]
    peers = Peers(streams)
    early = [peers.stream(each, mid_ref, mid_out_ref, *early_comm) for each in streams]
    late = [peers.stream(each, flat_ref, zero_out_ref, *late_comm) for each in streams]
    ticks = max(len(each) for each in early)
    between = min(steps - 1, ticks - 1)

    @pl.when(step == 0)
    def _():
        peers.greet()
        wqkv[...] = qkv_ref[0].astype(BF)
        wproj[...] = proj_ref[0].astype(BF)
        wup[...] = up_ref[0].astype(BF)
        wdown[...] = down_ref[0].astype(BF)
        for ref in sums:
            ref[...] = jnp.zeros_like(ref)
        peers.met()

    hot = lead_hot(step_ref, step, steps)
    masks = head_masks()
    masks32 = [m.astype(F32) for m in masks]

    def one(col):
        def keep(name, value):
            rows = value.shape[0]
            at = pl.multiple_of((lax.rem(step, group) * columns + col) * rows, 16)
            kept[name][pl.ds(at, rows), :] = value

        dn = dne_ref[col] + jnp.concatenate([from_low_ref[col], from_high_ref[col]], axis=0).astype(F32)
        xhat = xe_ref[col, :, 0:C]
        add_norm_grads(gnorm_ref, 2, dn, xhat)
        edge = dhe_ref[col] + norm_back(dn, xhat, xe_ref[col, :, C : C + 1], norm_ref[2, 0:1])
        grad = jnp.concatenate([edge[0:HALF], grad_in_ref[col], edge[HALF:]], axis=0)
        grad_low = grad.astype(BF)
        yield 1
        xhat = x1_ref[col, :, 0:C]
        normed_two = (xhat * norm_ref[1, 0:1] + norm_ref[1, 1:2]).astype(BF)
        yield 1
        yield from feed_backward(
            grad_low, wdown, act_ref.at[col], slope_ref.at[col], normed_two, gup_ref, gdown_ref, du_ref.at[col], keep
        )
        dnorm = dot_nt(du_ref[col], wup[...])
        yield 1
        add_norm_grads(gnorm_ref, 1, dnorm, xhat)
        grad = grad + norm_back(dnorm, xhat, x1_ref[col, :, C : C + 1], norm_ref[1, 0:1])
        grad_low = grad.astype(BF)
        yield 1
        dmix = dot_nt(grad_low, wproj[...]).astype(BF)
        yield 1
        gproj_ref[...] += dot_tn(mix_ref[col, 0:256], grad_low[0:256])
        keep("mix", mix_ref[col, 256:COL])
        keep("da", grad_low[256:])
        yield 1
        parts = []
        for w in range(2):
            part = pack_ref[col, WIN * w : WIN * w + WIN]
            found = []
            yield from attention_backward(
                part[:, 0:C],
                part[:, C : 2 * C],
                part[:, 2 * C :],
                probs_ref.at[col, w],
                dmix[WIN * w : WIN * w + WIN],
                masks,
                masks32,
                False,
                found,
            )
            parts.append(jnp.concatenate([g.astype(BF) for g in found], axis=1))
        dpacked = jnp.concatenate(parts, axis=0)
        yield 1
        dn = dot_nt(dpacked, wqkv[...])
        yield 1
        xhat = x0_ref[col, :, 0:C]
        normed = (xhat * norm_ref[0, 0:1] + norm_ref[0, 1:2]).astype(BF)
        gqkv_ref[...] += dot_tn(normed[0:256], dpacked[0:256])
        keep("n", normed[256:])
        keep("dp", dpacked[256:])
        yield 1
        add_norm_grads(gnorm_ref, 0, dn, xhat)
        grad = grad + norm_back(dn, xhat, x0_ref[col, :, C : C + 1], norm_ref[0, 0:1])
        glead_ref[...] += hot * jnp.sum(grad, axis=0, keepdims=True)
        grad_low = grad.astype(BF)
        yield 1
        gembed_ref[...] += dot_tn(grad_low[0:256], an_ref[col, 0:256])
        keep("an", an_ref[col, 256:COL])
        keep("dh", grad_low[256:])

    parts = [one(col) for col in range(columns)]
    drive(parts)

    for at in range(between):

        def now(at=at):
            for each in early:
                each[at]()

        pl.when(step == at)(now)

    @pl.when(lax.rem(step, group) == group - 1)
    def _():
        gup_ref[...] += dot_tn(kept["n2"][...], kept["du"][...])
        gdown_ref[...] += dot_tn(kept["dm"][...], kept["act"][...])
        gproj_ref[...] += dot_tn(kept["mix"][...], kept["da"][...])
        gqkv_ref[...] += dot_tn(kept["n"][...], kept["dp"][...])
        gembed_ref[...] += dot_tn(kept["dh"][...], kept["an"][...])

    @pl.when(step == pl.num_programs(0) - 1)
    def _():
        gnorm_ref[4:6] += part_ref[0:2]
        store_qkv_proj(flat_ref, 0, gqkv_ref, gproj_ref)
        store_wide(flat_ref, 6 * C, gup_ref, FF)
        store_wide(flat_ref, 12 * C, gdown_ref, FF)
        flat_ref[18 * C : 19 * C] = gembed_ref[...]
        store_narrow(flat_ref, 19 * C, gnorm_ref, 8)
        store_narrow(flat_ref, 19 * C + 16, glead_ref, 24)
        clear_from(flat_ref, FLAT_ZERO)
        for at in range(max(ticks, ticks - between)):
            for each in late:
                each[at]()
            if between + at < ticks:
                for each in early:
                    each[between + at]()


def update(steps, mid_ref, zero_ref, *refs):
    weights, firsts, seconds = refs[0:9], refs[9:18], refs[18:27]
    news, moms, secs = refs[27:36], refs[36:45], refs[45:54]
    small_ref, factor_ref = refs[54], refs[55]
    step = pl.program_id(0)
    scale_at = 19 * C + 16

    @pl.when(step == 0)
    def _():
        total = mid_ref[scale_at + 1 : scale_at + 2]
        count = total * CIN
        inverse = 1.0 / count

        def squares(ref, a, b):
            part = ref[a:b] * inverse
            return jnp.sum((part * part).reshape((b - a) // 8, 8, 128), axis=0)

        row = lax.broadcasted_iota(jnp.int32, (8, 128), 0)
        scale_grad = mid_ref[scale_at : scale_at + 1]
        mean_grad = scale_grad * inverse
        norms = jnp.sum(
            squares(mid_ref, 0, scale_at)
            + squares(zero_ref, 0, FLAT_ZERO)
            + jnp.where(row == 0, mean_grad * mean_grad, 0.0),
        )
        norm = jnp.sqrt(jnp.broadcast_to(norms, (1, 128)))
        factor_ref[...] = jnp.minimum(1.0, clip_max / norm) * inverse
        loss = jnp.broadcast_to(jnp.sum(total - scale_grad + weights[8][...] * total), (1, 128))
        small_ref[...] = jnp.where(row == 0, loss, jnp.where(row == 1, count, norm))

    factor = factor_ref[...]

    def adam(at, where, grad):
        clipped = grad * factor[:, 0 : grad.shape[-1]]
        first = beta_one * firsts[at][where] + (1.0 - beta_one) * clipped
        second = beta_two * seconds[at][where] + ((1.0 - beta_two) * clipped) * clipped
        weight = weights[at][where]
        root = second * (1.0 / (1.0 - beta_two**STEP))
        root = root * lax.rsqrt(root) + adam_eps
        rate = rate_table[at] / (1.0 - beta_one**STEP)
        new = weight - rate * first * pl.reciprocal(root)
        if decay_table[at]:
            new = new - (rate_table[at] * decay_table[at]) * weight
        news[at][where] = new
        moms[at][where] = first
        secs[at][where] = second

    rows = C // steps
    low = step * rows

    def take(ref, base):
        return ref[pl.ds(pl.multiple_of(base + low, 8), rows), :]

    for layer_at, ref in enumerate((zero_ref, mid_ref)):

        def put(at, a, b, grad):
            adam(at, (layer_at, slice(None), slice(a, b)), grad)

        for j in range(4):
            put(2, 128 * j, 128 * j + 128, take(ref, j * C))
        both = take(ref, 4 * C)
        put(2, 512, 576, both[:, 0:64])
        put(3, 128, 192, both[:, 64:128])
        put(3, 0, 128, take(ref, 5 * C))
        for j in range(6):
            put(4, 128 * j, 128 * j + 128, take(ref, (6 + j) * C))
            put(5, 128 * j, 128 * j + 128, take(ref, (12 + j) * C))
    everything = (slice(None), slice(None))
    adam(0, everything, take(zero_ref, 18 * C))
    adam(6, everything, take(mid_ref, 18 * C))

    @pl.when(step == 0)
    def _():
        lead_at = 19 * C + 16
        adam(1, (slice(None), slice(0, 128)), zero_ref[lead_at : lead_at + LEADS])
        adam(1, (slice(None), slice(128, 192)), zero_ref[lead_at + 24 : lead_at + 24 + LEADS, 0:64])
        adam(8, everything, mid_ref[scale_at : scale_at + 1])
        for at, (ref, index) in enumerate(((zero_ref, 0), (zero_ref, 1), (zero_ref, 2), (mid_ref, 1), (mid_ref, 2))):
            a = 19 * C + 2 * index
            adam(7, (at, slice(None), slice(0, 128)), ref[a : a + 2])
            adam(7, (at, slice(None), slice(128, 192)), ref[a + 8 : a + 10, 0:64])


def run_update(mid, zero, weights, firsts, seconds):
    steps = 6
    rows = C // steps
    kinds = (
        ((C, CIN), True),
        ((LEADS, C), False),
        ((2, C, 3 * C), True),
        ((2, C, C), True),
        ((2, C, FF), True),
        ((2, C, FF), True),
        ((C, CIN), True),
        ((5, 2, C), False),
        ((1, CIN), False),
    )
    specs = []
    for shape, cut in kinds:
        if not cut:
            specs.append(whole(shape))
        elif len(shape) == 2:
            specs.append(pl.BlockSpec((rows, shape[1]), lambda i: (i, 0)))
        else:
            specs.append(pl.BlockSpec((2, rows, shape[2]), lambda i: (0, i, 0)))
    shapes = [struct(shape, F32) for shape, _ in kinds]
    out = pl.pallas_call(
        partial(update, steps),
        grid=(steps,),
        in_specs=[whole(mid.shape), whole(zero.shape)] + specs * 3,
        out_specs=specs * 3 + [whole((8, 128))],
        out_shape=shapes * 3 + [struct((8, 128), F32)],
        scratch_shapes=[pltpu.VMEM((1, 128), F32)],
        compiler_params=pltpu.CompilerParams(vmem_limit_bytes=VMEM_BYTES),
        name="update",
    )(mid, zero, *weights, *firsts, *seconds)
    return out[0:9], out[9:18], out[18:27], out[27]


def whole(shape, once=False):
    zeros = (0,) * len(shape)
    return pl.BlockSpec(shape, lambda i: zeros, pipeline_mode=pl.Buffered(1) if once else None)


def layer(shape, index):
    at = (index,) + (0,) * len(shape)
    return pl.BlockSpec((1,) + shape, lambda i: at, pipeline_mode=pl.Buffered(1))


def rows_of(columns, offset, *shape):
    tail = (0,) * len(shape)
    return pl.BlockSpec((columns,) + shape, lambda i: (i + offset,) + tail)


def rows(columns, *shape):
    return rows_of(columns, 0, *shape)


SMEM = pl.BlockSpec(memory_space=pltpu.SMEM)


def struct(shape, dtype):
    return jax.ShapeDtypeStruct(shape, dtype)


def low(*shape):
    return pltpu.VMEM(shape, BF)


def full(*shape):
    return pltpu.VMEM(shape, F32)


def group_of(steps):
    return 2 if steps % 2 == 0 else 1


def kept_scratch(kept, count, columns):
    held = group_of(count // columns) * columns
    return [low(held * rows, width) for _, rows, width in kept]


def run_forward(lead_step, tokens, lead_table, embed_t, qkv_w, proj_w, up_w, down_t, norm_t, bands, columns):
    count = tokens.shape[0]
    steps = count // columns
    outs = [
        ((count, COL, XW), F32),
        ((count, COL, 3 * C), BF),
        ((count, 2, WIN, LANES), F32),
        ((count, COL, C), BF),
        ((count, COL, XW), F32),
        ((count, COL, FF), BF),
        ((count, COL, FF), F32),
        ((count, COL, C), F32),
    ]
    return pl.pallas_call(
        partial(forward_zero, columns, count, bands),
        grid=(steps,),
        in_specs=[
            SMEM,
            rows(columns, COL, CIN),
            whole((LEADS, C)),
            whole((C, CIN)),
            layer((C, 3 * C), 0),
            layer((C, C), 0),
            layer((C, FF), 0),
            layer((C, FF), 0),
            whole((5, 2, C)),
        ],
        out_specs=[rows(columns, *shape[1:]) for shape, _ in outs] + [ANYWHERE] * 2,
        out_shape=[struct(*o) for o in outs] + [struct((count, HALF, C), BF)] * 2,
        scratch_shapes=[low(C, CIN), low(C, 3 * C), low(C, C), low(C, FF), low(C, FF)] + edge_scratch(count, columns),
        compiler_params=pltpu.CompilerParams(vmem_limit_bytes=VMEM_BYTES, collective_id=1, has_side_effects=True),
        name="forward_zero",
    )(lead_step, tokens, lead_table, embed_t, qkv_w, proj_w, up_w, down_t, norm_t)


def run_middle(h1, up_in, down_in, target, mask, qkv_w, proj_w, up_w, down_t, decode_w, norm_t, scale, flat_rows, bands, columns):
    count = h1.shape[0]
    steps = count // columns
    outs = [
        ((count, WIN, C), F32),
        ((count, WIN, C), F32),
        ((count, WIN, C), F32),
        ((count, WIN, XW), F32),
    ]
    return pl.pallas_call(
        partial(middle, columns, count, bands),
        grid=(steps,),
        in_specs=[
            rows(columns, COL, C),
            rows(columns, HALF, C),
            rows(columns, HALF, C),
            rows(columns, COL, CIN),
            rows(columns, 24, 12),
            layer((C, 3 * C), 1),
            layer((C, C), 1),
            layer((C, FF), 1),
            layer((C, FF), 1),
            whole((C, CIN)),
            whole((5, 2, C)),
            whole((1, CIN)),
        ],
        out_specs=[rows(columns, *shape[1:]) for shape, _ in outs]
        + [whole((8, C)), whole((flat_rows, 128)), ANYWHERE, ANYWHERE],
        out_shape=[struct(*o) for o in outs]
        + [struct((8, C), F32), struct((flat_rows, 128), F32)]
        + [struct((count, HALF, C), BF)] * 2,
        scratch_shapes=edge_scratch(count, columns)
        + [
            low(C, 3 * C),
            low(C, C),
            low(C, FF),
            low(C, FF),
            low(C, CIN),
            low(COL, 24),
            full(COL, 12),
            full(columns, 2, WIN, LANES),
            low(columns, COL, FF),
            full(columns, COL, FF),
            low(columns, COL, FF),
            full(C, 3 * C),
            full(C, C),
            full(C, FF),
            full(C, FF),
            full(C, CIN),
            full(8, C),
            full(8, CIN),
        ]
        + kept_scratch(MIDDLE_KEEP, count, columns),
        compiler_params=pltpu.CompilerParams(vmem_limit_bytes=VMEM_BYTES, collective_id=2, has_side_effects=True),
        name="middle",
    )(h1, up_in, down_in, target, mask, qkv_w, proj_w, up_w, down_t, decode_w, norm_t, scale)


def run_backward(lead_step, tokens, saved, mid_out, mid, qkv_w, proj_w, up_w, down_t, norm_t, sizes, columns):
    count = tokens.shape[0]
    steps = count // columns
    streams = streams_of(sizes, mid.shape[0])
    return pl.pallas_call(
        partial(backward_zero, columns, count, streams),
        grid=(steps,),
        in_specs=[
            SMEM,
            rows(columns, COL, CIN),
            rows(columns, COL, XW),
            rows(columns, COL, 3 * C),
            rows(columns, 2, WIN, LANES),
            rows(columns, COL, C),
            rows(columns, COL, XW),
            rows(columns, COL, FF),
            rows(columns, COL, FF),
            rows(columns, WIN, C),
            rows(columns, WIN, C),
            rows(columns, WIN, C),
            rows(columns, WIN, XW),
            whole((8, C)),
            rows(columns, HALF, C),
            rows(columns, HALF, C),
            layer((C, 3 * C), 0),
            layer((C, C), 0),
            layer((C, FF), 0),
            layer((C, FF), 0),
            whole((5, 2, C)),
            whole(mid.shape, True),
        ],
        out_specs=[ANYWHERE] * 2,
        out_shape=[struct(mid.shape, F32)] * 2,
        scratch_shapes=[
            full(*mid.shape),
            low(C, 3 * C),
            low(C, C),
            low(C, FF),
            low(C, FF),
            low(columns, COL, FF),
            full(C, CIN),
            full(24, C),
            full(C, 3 * C),
            full(C, C),
            full(C, FF),
            full(C, FF),
            full(8, C),
        ]
        + kept_scratch(ZERO_KEEP, count, columns)
        + stream_buffers(streams) * 2
        + stream_sems(streams) * 2,
        compiler_params=pltpu.CompilerParams(vmem_limit_bytes=VMEM_BYTES, collective_id=3, has_side_effects=True),
        name="backward_zero",
    )(lead_step, tokens, *saved, *mid_out, qkv_w, proj_w, up_w, down_t, norm_t, mid)


def views(group):
    embed, lead, qkv, proj, up, down, decode, norm, scale = group
    return (embed.T, lead, qkv, proj, up, down.transpose(0, 2, 1), decode, norm.transpose(1, 0, 2), scale[None, :])


def unviews(group):
    embed, lead, qkv, proj, up, down, decode, norm, scale = group
    return (embed.T, lead, qkv, proj, up, down.transpose(0, 2, 1), decode, norm.transpose(1, 0, 2), scale[0])


def on_device(analysis, target, lead_step, loss_mask, *state):
    weights, firsts, seconds = (views(state[9 * i : 9 * i + 9]) for i in range(3))
    embed_t, lead_table, qkv_w, proj_w, up_w, down_t, decode_w, norm_t, scale = weights
    samples, blocks = analysis.shape[0], analysis.shape[1]
    sizes = {axis: lax.axis_size(axis) for axis in ("lat", "batch")}
    tokens = analysis.transpose(0, 1, 2, 4, 3, 5).reshape(samples * blocks, COL, CIN)
    truth = target.transpose(0, 1, 2, 4, 3, 5).reshape(samples * blocks, COL, CIN)
    lines = loss_mask.reshape(samples * blocks, 24, 12).astype(BF)
    columns = next(c for c in (COLUMNS, 3, 2, 1) if blocks % c == 0)
    unit = 8 * sizes["lat"] * sizes["batch"]
    flat_rows = -(-max(FLAT_MIDDLE, FLAT_ZERO) // unit) * unit

    *saved, h1, from_low, from_high = run_forward(
        lead_step, tokens, lead_table, embed_t, qkv_w, proj_w, up_w, down_t, norm_t, sizes["lat"], columns
    )
    *edge_out, part, mid, back_low, back_high = run_middle(
        h1, from_low, from_high, truth, lines, qkv_w, proj_w, up_w, down_t, decode_w, norm_t, scale,
        flat_rows, sizes["lat"], columns,
    )
    mid, zero = run_backward(
        lead_step, tokens, saved, (*edge_out, part, back_low, back_high), mid, qkv_w, proj_w, up_w, down_t, norm_t,
        sizes, columns,
    )
    news, moments, squares, small = run_update(mid, zero, weights, firsts, seconds)
    return (*unviews(news), *unviews(moments), *unviews(squares), small[0, 0], small[1, 0], small[2, 0])


def solution(mesh):
    split = P("batch", None, "lat", None, None, None)
    placed = (split, split, P("batch"), P("batch", None, "lat", None, None)) + (P(),) * 27
    return jax.shard_map(
        on_device, mesh=mesh, in_specs=placed, out_specs=(P(),) * 30, check_vma=False
    )
```

```python
from functools import partial
import math

import jax
import jax.numpy as jnp
from jax import lax
from jax.experimental import pallas as pl
from jax.experimental.pallas import tpu as pltpu
from jax.sharding import PartitionSpec as P

HEADS = 6
LEADS = 20
STEP = 10
C = 192
FF = 768
CIN = 128
HDIM = 32
COL = 288
WIN = 144
HALF = 72
LANES = 896
TAIL = COL - 256
KV = 3 * WIN
SCALE = HDIM ** (-0.5)
SCALE2 = SCALE * math.log2(math.e)
BF = jnp.bfloat16
F32 = jnp.float32

beta_one = 0.9
beta_two = 0.999
adam_eps = 1e-08
clip_max = 0.005
rate_table = (0.2, 1.0, 0.2, 0.2, 0.2, 0.2, 0.2, 1.0, 1.0)
decay_table = (0.1, 0.1, 0.1, 0.1, 0.1, 0.1, 0.1, 0.0, 0.0)

VMEM_BYTES = 61 * 1024 * 1024
COLUMNS = 4
COLUMNS_FIRST = 6
XW = 256


def dot(a, b):
    return lax.dot_general(a, b, (((1,), (0,)), ((), ())), preferred_element_type=F32)


def dot_nt(a, b):
    return lax.dot_general(a, b, (((1,), (1,)), ((), ())), preferred_element_type=F32)


def dot_tn(a, b):
    return lax.dot_general(a, b, (((0,), (0,)), ((), ())), preferred_element_type=F32)


def drive(parts):
    live = list(parts)
    while live:
        marks = [next(part, 0) for part in live]
        live = [part for part, mark in zip(live, marks) if mark == 1]


def norm_stats(x):
    center = x - jnp.mean(x, axis=-1, keepdims=True)
    rstd = lax.rsqrt(jnp.mean(center * center, axis=-1, keepdims=True) + 1e-05)
    return center * rstd, rstd


def with_rstd(xhat, rstd):
    return jnp.concatenate([xhat, jnp.broadcast_to(rstd, (xhat.shape[0], XW - C))], axis=1)


def norm_back(dy, xhat, rstd, gain):
    dxhat = dy * gain
    first = jnp.mean(dxhat, axis=-1, keepdims=True)
    second = jnp.mean(dxhat * xhat, axis=-1, keepdims=True)
    return rstd * (dxhat - first - xhat * second)


def add_norm_grads(acc_ref, index, dy, xhat):
    acc_ref[2 * index : 2 * index + 1] += jnp.sum(dy * xhat, axis=0, keepdims=True)
    acc_ref[2 * index + 1 : 2 * index + 2] += jnp.sum(dy, axis=0, keepdims=True)


def gelu_both(x):
    c0 = math.sqrt(2.0 / math.pi)
    c1 = c0 * 0.044715
    square = x * x
    slope = jnp.tanh(x * (c0 + c1 * square))
    half = 0.5 + 0.5 * slope
    active = x * half
    return active, half + active * ((1.0 - slope) * (c0 + (3.0 * c1) * square))


def head_masks():
    lane = lax.broadcasted_iota(jnp.int32, (1, C), 1) // HDIM
    return [(lane == h).astype(F32).astype(BF) for h in range(HEADS)]


def expand(x, masks, edge):
    rem = [x[128:144] * masks[h] for h in range(HEADS)] + [jnp.zeros((32, C), BF)]
    if edge:
        low = [x[0:64] * masks[h] for h in range(HEADS)]
        high = [x[64:128] * masks[h] for h in (4, 5, 0, 1, 2, 3)]
        return jnp.concatenate(low + rem + high, axis=0)
    return jnp.concatenate([x[0:128] * masks[h] for h in range(HEADS)] + rem, axis=0)


def low_lanes():
    return lax.broadcasted_iota(jnp.int32, (1, 128), 1) % 16 < 8


CHUNKS = ((0, 256), (256, 512), (512, 768), (768, 896))
EDGE_CHUNKS = ((0, 256), (256, 640), (640, 896))


def chunks_of(edge):
    return EDGE_CHUNKS if edge else CHUNKS


def add_bias(scores, bias):
    return jnp.concatenate([scores[0:HALF] + bias, scores[HALF:]], axis=0)


def score_chunk(keys, expanded, edge, at, bias=None):
    a, b = chunks_of(edge)[at]
    if not edge:
        return dot_nt(keys, expanded[a:b])
    if at != 1:
        out = dot_nt(keys[at // 2], expanded[a:b])
        return out if bias is None else add_bias(out, bias[at // 2])
    low = dot_nt(keys[0], expanded[256:512])
    high = dot_nt(keys[1], expanded[384:640])
    rem = jnp.where(low_lanes(), low[:, 128:256], high[:, 0:128])
    low, high = low[:, 0:128], high[:, 128:256]
    if bias is not None:
        low, high = add_bias(low, bias[0]), add_bias(high, bias[1])
        rem = add_bias(rem, jnp.where(low_lanes(), bias[0], bias[1]))
    return jnp.concatenate([low, rem, high], axis=1)


def query_chunk(vals_t, weights, edge, at):
    if not edge:
        return dot(vals_t[64 * at : 64 * at + 64] if at < 3 else vals_t, weights)
    if at != 1:
        return dot(vals_t[at // 2][0:128], weights)
    return dot(vals_t[0], weights[:, 0:256]), dot(vals_t[1], weights[:, 128:384])


def query_gather(parts, masks32, edge):
    if not edge:
        blocks = []
        for both in parts[:3]:
            blocks += [both[0:32, 0:128], both[32:64, 128:256]]
        rem = parts[3]
    else:
        low_a, (low_b, high_b), high_a = parts
        rem = jnp.where(low_lanes(), low_b[:, 128:256], high_b[:, 0:128])
        low_b, high_b = low_b[128:192, 0:128], high_b[128:192, 128:256]
        left = lax.broadcasted_iota(jnp.int32, (1, 128), 1) < 64
        blocks = []
        for h in range(HEADS):
            src_low, src_high, local = (low_a, high_a, h) if h < 4 else (low_b, high_b, h - 4)
            group = slice(128 * (local // 2), 128 * (local // 2) + 128)
            low = src_low[32 * local : 32 * local + 32, group]
            high = src_high[32 * local : 32 * local + 32, group]
            if h % 2:
                low = pltpu.roll(low, 64, 1)
            else:
                high = pltpu.roll(high, 64, 1)
            blocks.append(jnp.where(left, low, high))
    main = jnp.concatenate(blocks, axis=0).T
    back = rem.T
    total = back[0:16] * masks32[0]
    for h in range(1, HEADS):
        total = total + back[16 * h : 16 * h + 16] * masks32[h]
    return jnp.concatenate([main, total], axis=0)


def key_side(weights, expanded, edge):
    if not edge:
        return dot(jnp.concatenate(weights, axis=1), expanded)
    mask = low_lanes()
    rem = weights[1][:, 128:256]
    zero = jnp.zeros((), rem.dtype)
    low = jnp.concatenate([weights[0], weights[1][:, 0:128], jnp.where(mask, rem, zero)], axis=1)
    high = jnp.concatenate([jnp.where(mask, zero, rem), weights[1][:, 256:384], weights[2]], axis=1)
    return dot(low, expanded[0:512]), dot(high, expanded[384:896])


def attention_forward(q, k, vals, masks, masks32, edge, probs_ref, result, bias=None):
    queries = expand(q, masks, edge)
    vals_t = (vals[0].T, vals[1].T) if edge else vals.T
    spans = chunks_of(edge)
    ahead = score_chunk(k, queries, edge, 0, bias)
    yield 1
    parts = []
    for at, (a, b) in enumerate(spans):
        scores = ahead * SCALE2
        if at + 1 < len(spans):
            ahead = score_chunk(k, queries, edge, at + 1, bias)
        expo = jnp.exp2(scores - jnp.max(scores, axis=0, keepdims=True))
        probs = expo * (1.0 / jnp.sum(expo, axis=0, keepdims=True))
        probs_ref[:, a:b] = probs
        yield 1
        parts.append(query_chunk(vals_t, probs.astype(BF), edge, at))
        yield 1
    result.append(query_gather(parts, masks32, edge))


def attention_backward(q, k, vals, probs_ref, dmix, masks, masks32, edge, result):
    queries = expand(q, masks, edge)
    douts = expand(dmix, masks, edge)
    k_t = (k[0].T, k[1].T) if edge else k.T
    spans = chunks_of(edge)
    ahead = score_chunk(vals, douts, edge, 0)
    yield 1
    parts, lows, dlows = [], [], []
    for at, (a, b) in enumerate(spans):
        dprobs = ahead
        probs = probs_ref[:, a:b]
        if at + 1 < len(spans):
            ahead = score_chunk(vals, douts, edge, at + 1)
        row_terms = jnp.sum(dprobs * probs, axis=0, keepdims=True)
        dscores = (probs * (dprobs - row_terms)).astype(BF)
        lows.append(probs.astype(BF))
        dlows.append(dscores)
        yield 1
        parts.append(query_chunk(k_t, dscores, edge, at))
        yield 1
    dvals = key_side(lows, douts, edge)
    yield 1
    dkeys = key_side(dlows, queries, edge)
    yield 1
    dq = query_gather(parts, masks32, edge) * SCALE
    dkeys = (dkeys[0] * SCALE, dkeys[1] * SCALE) if edge else dkeys * SCALE
    result.extend([dq, dkeys, dvals])


def store_wide(out_ref, row, acc_ref, width):
    for j in range(width // 128):
        out_ref[row + C * j : row + C * j + C] = acc_ref[:, 128 * j : 128 * j + 128]


def store_qkv_proj(out_ref, row, qkv_ref, proj_ref):
    store_wide(out_ref, row, qkv_ref, 512)
    out_ref[row + 4 * C : row + 5 * C] = jnp.concatenate([qkv_ref[:, 512:576], proj_ref[:, 128:192]], axis=1)
    out_ref[row + 5 * C : row + 6 * C] = proj_ref[:, 0:128]


def clear_from(out_ref, row):
    if out_ref.shape[0] > row:
        out_ref[row:] = jnp.zeros((out_ref.shape[0] - row, 128), F32)


def store_narrow(out_ref, row, acc_ref, rows):
    out_ref[row : row + rows] = acc_ref[:, 0:128]
    out_ref[row + rows : row + 2 * rows] = jnp.concatenate(
        [acc_ref[:, 128:192], jnp.zeros((rows, 64), F32)], axis=1
    )


FLAT_MIDDLE = 19 * C + 24
FLAT_ZERO = 19 * C + 64


class Edges:
    def __init__(self, count, per_step, low_ref, high_ref, from_low_ref, from_high_ref, sems):
        self.at, self.count, self.per_step = lax.axis_index("lat"), count, per_step
        self.staged = (low_ref, high_ref)
        self.landing = (from_low_ref, from_high_ref)
        self.send_low, self.send_high, self.recv_low, self.recv_high, self.fill = sems
        self.has_low, self.has_high = self.at > 0, self.at < count - 1

    def greet(self):
        barrier = pltpu.get_barrier_semaphore()

        @pl.when(self.has_low)
        def _():
            pl.semaphore_signal(barrier, inc=1, device_id={"lat": self.at - 1}, device_id_type=pl.DeviceIdType.MESH)

        @pl.when(self.has_high)
        def _():
            pl.semaphore_signal(barrier, inc=1, device_id={"lat": self.at + 1}, device_id_type=pl.DeviceIdType.MESH)

    def met(self):
        there = jnp.where(self.has_low, 1, 0) + jnp.where(self.has_high, 1, 0)
        pl.semaphore_wait(pltpu.get_barrier_semaphore(), there)

    def copies(self, step):
        part = pl.ds(step * self.per_step, self.per_step)
        down = pltpu.make_async_remote_copy(
            src_ref=self.staged[0].at[part],
            dst_ref=self.landing[1].at[part],
            send_sem=self.send_low.at[step],
            recv_sem=self.recv_high.at[step],
            device_id={"lat": self.at - 1},
            device_id_type=pl.DeviceIdType.MESH,
        )
        up = pltpu.make_async_remote_copy(
            src_ref=self.staged[1].at[part],
            dst_ref=self.landing[0].at[part],
            send_sem=self.send_high.at[step],
            recv_sem=self.recv_low.at[step],
            device_id={"lat": self.at + 1},
            device_id_type=pl.DeviceIdType.MESH,
        )
        return down, up

    def send(self, step):
        down, up = self.copies(step)
        pl.when(self.has_low)(down.start)
        pl.when(self.has_high)(up.start)

    def finish(self, steps, zero_ref):
        zero_ref[...] = jnp.zeros_like(zero_ref)
        for step in range(steps):
            down, up = self.copies(step)
            part = pl.ds(step * self.per_step, self.per_step)

            def low_there(down=down, up=up):
                down.wait_send()
                up.wait_recv()

            def high_there(down=down, up=up):
                up.wait_send()
                down.wait_recv()

            pl.when(self.has_low)(low_there)
            pl.when(self.has_high)(high_there)

            def fill(side, part=part):
                copy = pltpu.make_async_copy(zero_ref, self.landing[side].at[part], self.fill)
                copy.start()
                copy.wait()

            pl.when(jnp.logical_not(self.has_low))(partial(fill, 0))
            pl.when(jnp.logical_not(self.has_high))(partial(fill, 1))


def edge_scratch(count, columns):
    steps = count // columns
    return [low(count, HALF, C), low(count, HALF, C), low(columns, HALF, C)] + [
        pltpu.SemaphoreType.DMA((steps,)) for _ in range(4)
    ] + [pltpu.SemaphoreType.DMA]


EDGE_SCRATCH = 8
ANYWHERE = pl.BlockSpec(memory_space=pl.ANY)


def lead_hot(step_ref, step, steps):
    sample = step // (steps // step_ref.shape[0])
    return (lax.broadcasted_iota(jnp.int32, (24, 1), 0) == step_ref[sample] - 1).astype(F32)


def forward_zero(columns, count, bands, *refs):
    step_ref, an_ref, lead_ref, embed_ref, qkv_ref, proj_ref, up_ref, down_ref, norm_ref = refs[:9]
    x0_ref, pack_ref, probs_ref, mix_ref, x1_ref, act_ref, slope_ref, h1_ref, from_low_ref, from_high_ref = refs[9:19]
    wembed, wqkv, wproj, wup, wdown, top_ref, bot_ref, zero_ref, *sems = refs[19:]
    step = pl.program_id(0)
    edges = Edges(bands, columns, top_ref, bot_ref, from_low_ref, from_high_ref, sems)

    @pl.when(step == 0)
    def _():
        edges.greet()
        wembed[...] = embed_ref[...].astype(BF)
        wqkv[...] = qkv_ref[0].astype(BF)
        wproj[...] = proj_ref[0].astype(BF)
        wup[...] = up_ref[0].astype(BF)
        wdown[...] = down_ref[0].astype(BF)

    masks = head_masks()
    masks32 = [m.astype(F32) for m in masks]
    lead_row = jnp.sum(lead_hot(step_ref, step, count // columns)[0:LEADS] * lead_ref[...], axis=0, keepdims=True)

    def one(col):
        hidden = dot_nt(an_ref[col], wembed[...]) + lead_row
        yield 1
        xhat, rstd = norm_stats(hidden)
        x0_ref[col] = with_rstd(xhat, rstd)
        normed = (xhat * norm_ref[0, 0:1] + norm_ref[0, 1:2]).astype(BF)
        yield 1
        packed = dot(normed, wqkv[...]).astype(BF)
        pack_ref[col] = packed
        yield 1
        mixtures = []
        for w in range(2):
            part = packed[WIN * w : WIN * w + WIN]

            yield from attention_forward(
                part[:, 0:C], part[:, C : 2 * C], part[:, 2 * C :], masks, masks32, False, probs_ref.at[col, w], mixtures
            )
        mixture = jnp.concatenate(mixtures, axis=0).astype(BF)
        mix_ref[col] = mixture
        yield 1
        hidden_two = hidden + dot(mixture, wproj[...])
        yield 1
        xhat, rstd = norm_stats(hidden_two)
        x1_ref[col] = with_rstd(xhat, rstd)
        normed_two = (xhat * norm_ref[1, 0:1] + norm_ref[1, 1:2]).astype(BF)
        yield 1
        yield from feed_forward(normed_two, wup, act_ref.at[col], slope_ref.at[col])
        hidden_one = hidden_two + dot_nt(act_ref[col], wdown[...])
        h1_ref[col] = hidden_one
        yield 1
        xhat, _ = norm_stats(jnp.concatenate([hidden_one[0:HALF], hidden_one[COL - HALF :]], axis=0))
        normed = xhat * norm_ref[2, 0:1] + norm_ref[2, 1:2]
        top_ref[step * columns + col] = normed[0:HALF].astype(BF)
        bot_ref[step * columns + col] = normed[HALF:].astype(BF)

    drive([one(col) for col in range(columns)])

    @pl.when(step == 0)
    def _():
        edges.met()

    edges.send(step)

    @pl.when(step == pl.num_programs(0) - 1)
    def _():
        edges.finish(count // columns, zero_ref)


def feed_forward(normed_two, wup, act_ref, slope_ref):
    ahead = dot(normed_two, wup[:, 0:256])
    yield 1
    for c in range(3):
        span = slice(256 * c, 256 * c + 256)
        inner = ahead
        if c < 2:
            ahead = dot(normed_two, wup[:, 256 * c + 256 : 256 * c + 512])
        active, slope = gelu_both(inner)
        act_ref[:, span] = active.astype(BF)
        slope_ref[:, span] = slope
        yield 1


def feed_grads(grad_low, act_ref, normed_two, gup_ref, gdown_ref, du_ref, keep):
    for c in range(3):
        span = slice(256 * c, 256 * c + 256)
        gdown_ref[:, span] += dot_tn(grad_low[0:256], act_ref[0:256, span])
        yield 1
        gup_ref[:, span] += dot_tn(normed_two[0:256], du_ref[0:256, span])
        yield 1
    keep("act", act_ref[256:COL, :])
    keep("du", du_ref[256:COL, :])
    keep("dm", grad_low[256:COL])
    keep("n2", normed_two[256:COL])


def feed_backward(grad_low, wdown, slope_ref, du_ref):
    ahead = dot(grad_low, wdown[:, 0:256])
    yield 1
    for c in range(3):
        span = slice(256 * c, 256 * c + 256)
        dactive = ahead
        if c < 2:
            ahead = dot(grad_low, wdown[:, 256 * c + 256 : 256 * c + 512])
        dinner = (dactive * slope_ref[:, span]).astype(BF)
        du_ref[:, span] = dinner
        yield 1


MIDDLE_KEEP = (
    ("act", TAIL, FF),
    ("du", TAIL, FF),
    ("dm", TAIL, C),
    ("n2", TAIL, C),
    ("mix", TAIL, C),
    ("da", TAIL, C),
    ("n", TAIL, C),
    ("dq", TAIL, C),
    ("nkv", KV - 256, C),
    ("dkv", KV - 256, 2 * C),
    ("last", TAIL, C),
    ("dp", TAIL, CIN),
)


def edge_first(ref):
    return jnp.concatenate([ref[0:64], ref[216:280], ref[64:72], ref[280:288], ref[72:216]], axis=0)


def cell_selectors():
    token = lax.broadcasted_iota(jnp.int32, (COL, 24), 0)
    line = lax.broadcasted_iota(jnp.int32, (COL, 24), 1)
    of_line = (token // 24 * 2 + token % 2 == line).astype(F32).astype(BF)
    token = lax.broadcasted_iota(jnp.int32, (COL, 12), 0)
    place = lax.broadcasted_iota(jnp.int32, (COL, 12), 1)
    return of_line, (token % 24 // 2 == place).astype(F32)


def middle(columns, count, bands, *refs):
    h1_ref, up_in_ref, down_in_ref, target_ref, mask_ref = refs[:5]
    qkv_ref, proj_ref, up_ref, down_ref, decode_ref, norm_ref, scale_ref = refs[5:12]
    grad_ref, dhe_ref, dne_ref, xe_ref, part_ref, flat_ref, from_low_ref, from_high_ref = refs[12:20]
    dtop_ref, dbot_ref, zero_ref, *sems = refs[20 : 20 + EDGE_SCRATCH]
    refs = refs[20 + EDGE_SCRATCH :]
    wqkv, wproj, wup, wdown, wdec, line_ref, place_ref, probs_ref, act_ref, slope_ref, du_ref = refs[:11]
    sums = refs[11:18]
    gqkv_ref, gproj_ref, gup_ref, gdown_ref, gdec_ref, gnorm_ref, gscale_ref = sums
    kept = {name: ref for (name, _, _), ref in zip(MIDDLE_KEEP, refs[18:])}
    step = pl.program_id(0)
    group = group_of(count // columns)
    edges = Edges(bands, columns, dtop_ref, dbot_ref, from_low_ref, from_high_ref, sems)

    @pl.when(step == 0)
    def _():
        edges.greet()
        wqkv[...] = qkv_ref[0].astype(BF)
        wproj[...] = proj_ref[0].astype(BF)
        wup[...] = up_ref[0].astype(BF)
        wdown[...] = down_ref[0].astype(BF)
        wdec[...] = decode_ref[...].astype(BF)
        line_ref[...], place_ref[...] = cell_selectors()
        for ref in sums:
            ref[...] = jnp.zeros_like(ref)

    masks = head_masks()
    masks32 = [m.astype(F32) for m in masks]
    bias = (jnp.where(edges.has_low, 0.0, -1e30), jnp.where(edges.has_high, 0.0, -1e30))
    inverse = jnp.exp(-scale_ref[...])

    def one(col):
        def keep(name, value):
            rows = value.shape[0]
            at = pl.multiple_of((lax.rem(step, group) * columns + col) * rows, 16)
            kept[name][pl.ds(at, rows), :] = value

        act, slope, du = act_ref.at[col], slope_ref.at[col], du_ref.at[col]
        h1 = edge_first(h1_ref[col])
        xhat_one, rstd_one = norm_stats(h1)
        normed = xhat_one * norm_ref[2, 0:1] + norm_ref[2, 1:2]
        normed_low = normed.astype(BF)
        n_top = jnp.concatenate([up_in_ref[col].astype(F32), normed[0:64], normed[128:136]], axis=0).astype(BF)
        n_bot = jnp.concatenate([down_in_ref[col].astype(F32), normed[64:128], normed[136:144]], axis=0).astype(BF)
        n_kv = jnp.concatenate([n_top, n_bot, normed_low[WIN:]], axis=0)
        yield 1
        keys_vals = dot(n_kv, wqkv[:, C:]).astype(BF)
        yield 1
        queries = dot(normed_low, wqkv[:, 0:C]).astype(BF)
        yield 1
        keys, vals = keys_vals[:, 0:C], keys_vals[:, C:]
        k_edge, v_edge = (keys[0:WIN], keys[WIN : 2 * WIN]), (vals[0:WIN], vals[WIN : 2 * WIN])
        k_mid, v_mid = keys[2 * WIN :], vals[2 * WIN :]
        mixtures = []
        yield from attention_forward(
            queries[0:WIN], k_edge, v_edge, masks, masks32, True, probs_ref.at[col, 0], mixtures, bias
        )
        yield from attention_forward(queries[WIN:], k_mid, v_mid, masks, masks32, False, probs_ref.at[col, 1], mixtures)
        mixture = jnp.concatenate(mixtures, axis=0).astype(BF)
        yield 1
        hidden_two = h1 + dot(mixture, wproj[...])
        yield 1
        xhat_two, rstd_two = norm_stats(hidden_two)
        normed_two = (xhat_two * norm_ref[3, 0:1] + norm_ref[3, 1:2]).astype(BF)
        yield 1
        yield from feed_forward(normed_two, wup, act, slope)
        hidden = hidden_two + dot_nt(act[...], wdown[...])
        yield 1
        xhat, rstd = norm_stats(hidden)
        normed_last = (xhat * norm_ref[4, 0:1] + norm_ref[4, 1:2]).astype(BF)
        yield 1
        predicted = dot(normed_last, wdec[...])
        cells = dot((dot(line_ref[...], mask_ref[col]) * place_ref[...]).astype(BF), jnp.ones((12, CIN), BF))
        yield 1
        error = predicted - edge_first(target_ref[col])
        cells = edge_first(cells)
        square = error * error + 1.0
        back = lax.rsqrt(square)
        gscale_ref[0:1] += jnp.sum(cells * (1.0 - square * back * inverse), axis=0, keepdims=True)
        gscale_ref[1:2] += jnp.sum(cells, axis=0, keepdims=True)
        dpred = (cells * inverse * error * back).astype(BF)
        yield 1
        dnorm = dot_nt(dpred, wdec[...])
        yield 1
        gdec_ref[...] += dot_tn(normed_last[0:256], dpred[0:256])
        add_norm_grads(gnorm_ref, 2, dnorm, xhat)
        keep("last", normed_last[256:])
        keep("dp", dpred[256:])
        grad = norm_back(dnorm, xhat, rstd, norm_ref[4, 0:1])
        grad_low = grad.astype(BF)
        yield 1
        yield from feed_backward(grad_low, wdown, slope, du)
        dnorm = dot_nt(du[...], wup[...])
        yield 1
        pieces = feed_grads(grad_low, act, normed_two, gup_ref, gdown_ref, du, keep)
        next(pieces)
        add_norm_grads(gnorm_ref, 1, dnorm, xhat_two)
        next(pieces)
        yield 1
        next(pieces)
        next(pieces)
        grad = grad + norm_back(dnorm, xhat_two, rstd_two, norm_ref[3, 0:1])
        grad_low = grad.astype(BF)
        dhe_ref[col, 0:64] = grad[0:64]
        dhe_ref[col, 64:72] = grad[128:136]
        dhe_ref[col, 72:136] = grad[64:128]
        dhe_ref[col, 136:144] = grad[136:144]
        kept_edge = with_rstd(xhat_one[0:WIN], rstd_one[0:WIN])
        xe_ref[col, 0:64] = kept_edge[0:64]
        xe_ref[col, 64:72] = kept_edge[128:136]
        xe_ref[col, 72:136] = kept_edge[64:128]
        xe_ref[col, 136:144] = kept_edge[136:144]
        next(pieces)
        next(pieces)
        yield 1
        dmix = dot_nt(grad_low, wproj[...]).astype(BF)
        next(pieces, 0)
        yield 1
        gproj_ref[...] += dot_tn(mixture[0:256], grad_low[0:256])
        keep("mix", mixture[256:])
        keep("da", grad_low[256:])
        yield 1
        found = []
        yield from attention_backward(
            queries[0:WIN], k_edge, v_edge, probs_ref.at[col, 0], dmix[0:WIN], masks, masks32, True, found
        )
        yield 1
        yield from attention_backward(
            queries[WIN:], k_mid, v_mid, probs_ref.at[col, 1], dmix[WIN:], masks, masks32, False, found
        )
        dq_e, dk_e, dv_e, dq_m, dk_m, dv_m = found
        dq = jnp.concatenate([dq_e, dq_m], axis=0).astype(BF)
        dk = jnp.concatenate([dk_e[0], dk_e[1], dk_m], axis=0).astype(BF)
        dv = jnp.concatenate([dv_e[0], dv_e[1], dv_m], axis=0).astype(BF)
        dkv = jnp.concatenate([dk, dv], axis=1)
        yield 1
        dn_kv = dot_nt(dkv, wqkv[:, C:])
        dtop_ref[step * columns + col] = dn_kv[0:HALF].astype(BF)
        dbot_ref[step * columns + col] = dn_kv[WIN : WIN + HALF].astype(BF)
        yield 1
        dn_q = dot_nt(dq, wqkv[:, 0:C])
        yield 1
        dne_ref[col, 0:64] = dn_q[0:64] + dn_kv[72:136]
        dne_ref[col, 64:72] = dn_q[128:136] + dn_kv[136:144]
        dne_ref[col, 72:136] = dn_q[64:128] + dn_kv[216:280]
        dne_ref[col, 136:144] = dn_q[136:144] + dn_kv[280:288]
        dnorm = dn_q[WIN:] + dn_kv[2 * WIN :]
        add_norm_grads(gnorm_ref, 0, dnorm, xhat_one[WIN:])
        grad_ref[col] = grad[WIN:] + norm_back(dnorm, xhat_one[WIN:], rstd_one[WIN:], norm_ref[2, 0:1])
        yield 1
        gqkv_ref[:, 0:C] += dot_tn(normed_low[0:256], dq[0:256])
        yield 1
        gqkv_ref[:, C:] += dot_tn(n_kv[0:256], dkv[0:256])
        keep("n", normed_low[256:])
        keep("dq", dq[256:])
        keep("nkv", n_kv[256:])
        keep("dkv", dkv[256:])

    drive([one(col) for col in range(columns)])

    @pl.when(step == 0)
    def _():
        edges.met()

    edges.send(step)

    @pl.when(lax.rem(step, group) == group - 1)
    def _():
        gup_ref[...] += dot_tn(kept["n2"][...], kept["du"][...])
        gdown_ref[...] += dot_tn(kept["dm"][...], kept["act"][...])
        gproj_ref[...] += dot_tn(kept["mix"][...], kept["da"][...])
        gqkv_ref[:, 0:C] += dot_tn(kept["n"][...], kept["dq"][...])
        gqkv_ref[:, C:] += dot_tn(kept["nkv"][...], kept["dkv"][...])
        gdec_ref[...] += dot_tn(kept["last"][...], kept["dp"][...])

    @pl.when(step == pl.num_programs(0) - 1)
    def _():
        store_qkv_proj(flat_ref, 0, gqkv_ref, gproj_ref)
        store_wide(flat_ref, 6 * C, gup_ref, FF)
        store_wide(flat_ref, 12 * C, gdown_ref, FF)
        flat_ref[18 * C : 19 * C] = gdec_ref[...]
        part_ref[...] = gnorm_ref[...]
        gnorm_ref[0:2] = jnp.zeros((2, C), F32)
        store_narrow(flat_ref, 19 * C, gnorm_ref, 8)
        flat_ref[19 * C + 16 : 19 * C + 24] = gscale_ref[...]
        clear_from(flat_ref, FLAT_MIDDLE)
        edges.finish(count // columns, zero_ref)


def exchanges(sizes):
    out = []
    for axis in ("batch", "lat"):
        size = sizes[axis]
        if size % 2 == 0:
            out.append((axis, 1, 2))
            if size > 2:
                out.append((axis, 2, size // 2))
        elif size > 1:
            out.append((axis, 1, size))
    return out


ORDERS = ((1, 2, 3), (2, 1, 3), (3, 1, 2))
SHARES = (2, 2, 1)


def streams_of(sizes, rows):
    base = exchanges(sizes)
    unit = 8 * sizes["lat"] * sizes["batch"]
    orders = [base]
    if len(base) == 4:
        orders = [[base[0], base[i], base[j], base[k]] for i, j, k in ORDERS]
    units = rows // unit
    at = 0
    out = []
    for n, order in enumerate(orders):
        share = units - at if n == len(orders) - 1 else min(units - at, -(-units * SHARES[n] // sum(SHARES)))
        if share:
            out.append((at * unit, share * unit, order))
        at += share
    return out


def stream_buffers(streams):
    scratch = []
    for _, length, order in streams:
        held, landed = [], []
        for _, _, count in order:
            length //= count
            held.append(full(length, 128))
            landed.append(full(count - 1, length, 128))
        scratch += held + landed + held[:-1]
    return scratch


def stream_sems(streams):
    out = []
    for _, _, order in streams:
        out += [pltpu.SemaphoreType.DMA((count,)) for _ in range(4) for _, _, count in order] + [pltpu.SemaphoreType.DMA]
    return out


def span(place, rows):
    return pl.ds(pl.multiple_of(place * rows, 8), rows)


class Peers:
    def __init__(self, streams):
        self.places, self.others = {}, {}
        for _, _, order in streams:
            for stage in order:
                if stage in self.places:
                    continue
                axis, stride, count = stage
                index = lax.axis_index(axis)
                place = lax.rem(index // stride, count)
                self.places[stage] = place
                self.others[stage] = []
                for hop in range(1, count):
                    other = lax.rem(place + hop, count)
                    self.others[stage].append((other, {axis: index + (other - place) * stride}))

    def greet(self):
        barrier = pltpu.get_barrier_semaphore()
        for others in self.others.values():
            for _, device in others:
                pl.semaphore_signal(barrier, inc=1, device_id=device, device_id_type=pl.DeviceIdType.MESH)

    def met(self):
        number = sum(len(others) for others in self.others.values())
        if number:
            pl.semaphore_wait(pltpu.get_barrier_semaphore(), number)

    def stream(self, which, source_ref, target_ref, buffers, sems):
        start, length, order = which
        levels = len(order)

        def take(scratch, count):
            head = scratch[:count]
            del scratch[:count]
            return head

        held, landed, gathered = (take(buffers, count) for count in (levels, levels, max(levels - 1, 0)))
        send, recv, send_back, recv_back = (take(sems, levels) for _ in range(4))
        (own_sem,) = take(sems, 1)
        sources = [source_ref.at[pl.ds(start, length)]] + held
        targets = [target_ref.at[pl.ds(start, length)]] + gathered + held[-1:]

        def remote(source, target, send_sem, recv_sem, device):
            return pltpu.make_async_remote_copy(
                src_ref=source,
                dst_ref=target,
                send_sem=send_sem,
                recv_sem=recv_sem,
                device_id=device,
                device_id_type=pl.DeviceIdType.MESH,
            )

        def out(s, outgoing):
            rows, place = held[s].shape[0], self.places[order[s]]
            return [
                remote(
                    sources[s].at[span(other, rows)],
                    landed[s].at[order[s][2] - 2 - hop if outgoing else hop],
                    send[s].at[other],
                    recv[s].at[place if outgoing else other],
                    device,
                )
                for hop, (other, device) in enumerate(self.others[order[s]])
            ]

        def back(s, outgoing):
            rows, place = held[s].shape[0], self.places[order[s]]
            return [
                remote(
                    targets[s + 1],
                    targets[s].at[span(place if outgoing else other, rows)],
                    send_back[s].at[other],
                    recv_back[s].at[place if outgoing else other],
                    device,
                )
                for other, device in self.others[order[s]]
            ]

        def start_out(s):
            for copy in out(s, True):
                copy.start()

        def end_out(s):
            for copy in out(s, False):
                copy.wait()
            rows = held[s].shape[0]
            total = sources[s][span(self.places[order[s]], rows), :]
            for hop in range(order[s][2] - 1):
                total = total + landed[s][hop]
            held[s][...] = total

        def start_back(s):
            for copy in back(s, True):
                copy.start()
            place = span(self.places[order[s]], held[s].shape[0])
            if s:
                targets[s][place, :] = targets[s + 1][...]
            else:
                pltpu.make_async_copy(targets[1], targets[0].at[place], own_sem).start()

        def end_back(s):
            for copy in back(s, False):
                copy.wait()
            if not s:
                place = span(self.places[order[0]], held[0].shape[0])
                pltpu.make_async_copy(targets[1], targets[0].at[place], own_sem).wait()

        if not levels:

            def alone():
                copy = pltpu.make_async_copy(source_ref, target_ref, own_sem)
                copy.start()
                copy.wait()

            return [alone]
        moves = [(start_out, end_out, s) for s in range(levels)]
        moves += [(start_back, end_back, s) for s in reversed(range(levels))]

        def tick(at):
            def run():
                if at:
                    _, end, s = moves[at - 1]
                    end(s)
                if at < len(moves):
                    begin, _, s = moves[at]
                    begin(s)

            return run

        return [tick(at) for at in range(len(moves) + 1)]


ZERO_KEEP = (
    ("act", TAIL, FF),
    ("du", TAIL, FF),
    ("dm", TAIL, C),
    ("n2", TAIL, C),
    ("mix", TAIL, C),
    ("da", TAIL, C),
    ("n", TAIL, C),
    ("dp", TAIL, 3 * C),
    ("an", TAIL, CIN),
    ("dh", TAIL, C),
)


def backward_zero(columns, count, streams, *refs):
    step_ref, an_ref, x0_ref, pack_ref, probs_ref, mix_ref, x1_ref, act_ref, slope_ref = refs[:9]
    grad_in_ref, dhe_ref, dne_ref, xe_ref, part_ref, from_low_ref, from_high_ref = refs[9:16]
    qkv_ref, proj_ref, up_ref, down_ref, norm_ref, mid_ref, mid_out_ref, zero_out_ref = refs[16:24]
    flat_ref, wqkv, wproj, wup, wdown, du_ref = refs[24:30]
    sums = refs[30:37]
    gembed_ref, glead_ref, gqkv_ref, gproj_ref, gup_ref, gdown_ref, gnorm_ref = sums
    kept = {name: ref for (name, _, _), ref in zip(ZERO_KEEP, refs[37:])}
    step = pl.program_id(0)
    steps = count // columns
    group = group_of(steps)
    comm = list(refs[37 + len(ZERO_KEEP) :])
    kinds = (stream_buffers(streams), stream_sems(streams))
    early_comm, late_comm = [], []
    for kind in kinds:
        for group_comm in (early_comm, late_comm):
            group_comm.append(comm[: len(kind)])
            del comm[: len(kind)]
    peers = Peers(streams)
    early = [peers.stream(each, mid_ref, mid_out_ref, *early_comm) for each in streams]
    late = [peers.stream(each, flat_ref, zero_out_ref, *late_comm) for each in streams]
    ticks = max(len(each) for each in early)
    between = min(steps - 1, ticks - 1)

    @pl.when(step == 0)
    def _():
        peers.greet()
        wqkv[...] = qkv_ref[0].astype(BF)
        wproj[...] = proj_ref[0].astype(BF)
        wup[...] = up_ref[0].astype(BF)
        wdown[...] = down_ref[0].astype(BF)
        for ref in sums:
            ref[...] = jnp.zeros_like(ref)
        peers.met()

    hot = lead_hot(step_ref, step, steps)
    masks = head_masks()
    masks32 = [m.astype(F32) for m in masks]

    def one(col):
        def keep(name, value):
            rows = value.shape[0]
            at = pl.multiple_of((lax.rem(step, group) * columns + col) * rows, 16)
            kept[name][pl.ds(at, rows), :] = value

        dn = dne_ref[col] + jnp.concatenate([from_low_ref[col], from_high_ref[col]], axis=0).astype(F32)
        xhat = xe_ref[col, :, 0:C]
        add_norm_grads(gnorm_ref, 2, dn, xhat)
        edge = dhe_ref[col] + norm_back(dn, xhat, xe_ref[col, :, C : C + 1], norm_ref[2, 0:1])
        grad = jnp.concatenate([edge[0:HALF], grad_in_ref[col], edge[HALF:]], axis=0)
        grad_low = grad.astype(BF)
        yield 1
        xhat = x1_ref[col, :, 0:C]
        normed_two = (xhat * norm_ref[1, 0:1] + norm_ref[1, 1:2]).astype(BF)
        yield 1
        yield from feed_backward(grad_low, wdown, slope_ref.at[col], du_ref.at[col])
        dnorm = dot_nt(du_ref[col], wup[...])
        yield 1
        pieces = feed_grads(grad_low, act_ref.at[col], normed_two, gup_ref, gdown_ref, du_ref.at[col], keep)
        next(pieces)
        add_norm_grads(gnorm_ref, 1, dnorm, xhat)
        next(pieces)
        yield 1
        next(pieces)
        next(pieces)
        grad = grad + norm_back(dnorm, xhat, x1_ref[col, :, C : C + 1], norm_ref[1, 0:1])
        grad_low = grad.astype(BF)
        yield 1
        dmix = dot_nt(grad_low, wproj[...]).astype(BF)
        next(pieces)
        next(pieces)
        next(pieces, 0)
        yield 1
        gproj_ref[...] += dot_tn(mix_ref[col, 0:256], grad_low[0:256])
        keep("mix", mix_ref[col, 256:COL])
        keep("da", grad_low[256:])
        yield 1
        parts = []
        for w in range(2):
            part = pack_ref[col, WIN * w : WIN * w + WIN]
            found = []
            yield from attention_backward(
                part[:, 0:C],
                part[:, C : 2 * C],
                part[:, 2 * C :],
                probs_ref.at[col, w],
                dmix[WIN * w : WIN * w + WIN],
                masks,
                masks32,
                False,
                found,
            )
            parts.append(jnp.concatenate([g.astype(BF) for g in found], axis=1))
        dpacked = jnp.concatenate(parts, axis=0)
        yield 1
        dn = dot_nt(dpacked, wqkv[...])
        yield 1
        xhat = x0_ref[col, :, 0:C]
        normed = (xhat * norm_ref[0, 0:1] + norm_ref[0, 1:2]).astype(BF)
        gqkv_ref[...] += dot_tn(normed[0:256], dpacked[0:256])
        keep("n", normed[256:])
        keep("dp", dpacked[256:])
        yield 1
        add_norm_grads(gnorm_ref, 0, dn, xhat)
        grad = grad + norm_back(dn, xhat, x0_ref[col, :, C : C + 1], norm_ref[0, 0:1])
        glead_ref[...] += hot * jnp.sum(grad, axis=0, keepdims=True)
        grad_low = grad.astype(BF)
        yield 1
        gembed_ref[...] += dot_tn(grad_low[0:256], an_ref[col, 0:256])
        keep("an", an_ref[col, 256:COL])
        keep("dh", grad_low[256:])

    parts = [one(col) for col in range(columns)]
    drive(parts)

    for at in range(between):

        def now(at=at):
            for each in early:
                each[at]()

        pl.when(step == at)(now)

    @pl.when(lax.rem(step, group) == group - 1)
    def _():
        gup_ref[...] += dot_tn(kept["n2"][...], kept["du"][...])
        gdown_ref[...] += dot_tn(kept["dm"][...], kept["act"][...])
        gproj_ref[...] += dot_tn(kept["mix"][...], kept["da"][...])
        gqkv_ref[...] += dot_tn(kept["n"][...], kept["dp"][...])
        gembed_ref[...] += dot_tn(kept["dh"][...], kept["an"][...])

    @pl.when(step == pl.num_programs(0) - 1)
    def _():
        gnorm_ref[4:6] += part_ref[0:2]
        store_qkv_proj(flat_ref, 0, gqkv_ref, gproj_ref)
        store_wide(flat_ref, 6 * C, gup_ref, FF)
        store_wide(flat_ref, 12 * C, gdown_ref, FF)
        flat_ref[18 * C : 19 * C] = gembed_ref[...]
        store_narrow(flat_ref, 19 * C, gnorm_ref, 8)
        store_narrow(flat_ref, 19 * C + 16, glead_ref, 24)
        clear_from(flat_ref, FLAT_ZERO)
        for at in range(max(ticks, ticks - between)):
            for each in late:
                each[at]()
            if between + at < ticks:
                for each in early:
                    each[between + at]()


def update(steps, mid_ref, zero_ref, *refs):
    weights, firsts, seconds = refs[0:9], refs[9:18], refs[18:27]
    news, moms, secs = refs[27:36], refs[36:45], refs[45:54]
    small_ref, factor_ref = refs[54], refs[55]
    step = pl.program_id(0)
    scale_at = 19 * C + 16

    @pl.when(step == 0)
    def _():
        total = mid_ref[scale_at + 1 : scale_at + 2]
        count = total * CIN
        inverse = 1.0 / count

        def squares(ref, a, b):
            part = ref[a:b] * inverse
            return jnp.sum((part * part).reshape((b - a) // 8, 8, 128), axis=0)

        row = lax.broadcasted_iota(jnp.int32, (8, 128), 0)
        scale_grad = mid_ref[scale_at : scale_at + 1]
        mean_grad = scale_grad * inverse
        norms = jnp.sum(
            squares(mid_ref, 0, scale_at)
            + squares(zero_ref, 0, FLAT_ZERO)
            + jnp.where(row == 0, mean_grad * mean_grad, 0.0),
        )
        norm = jnp.sqrt(jnp.broadcast_to(norms, (1, 128)))
        factor_ref[...] = jnp.minimum(1.0, clip_max / norm) * inverse
        loss = jnp.broadcast_to(jnp.sum(total - scale_grad + weights[8][...] * total), (1, 128))
        small_ref[...] = jnp.where(row == 0, loss, jnp.where(row == 1, count, norm))

    factor = factor_ref[...]

    def adam(at, where, grad):
        clipped = grad * factor[:, 0 : grad.shape[-1]]
        first = beta_one * firsts[at][where] + (1.0 - beta_one) * clipped
        second = beta_two * seconds[at][where] + ((1.0 - beta_two) * clipped) * clipped
        weight = weights[at][where]
        root = second * (1.0 / (1.0 - beta_two**STEP))
        root = root * lax.rsqrt(root) + adam_eps
        rate = rate_table[at] / (1.0 - beta_one**STEP)
        new = weight - rate * first * pl.reciprocal(root)
        if decay_table[at]:
            new = new - (rate_table[at] * decay_table[at]) * weight
        news[at][where] = new
        moms[at][where] = first
        secs[at][where] = second

    rows = C // steps
    low = step * rows

    def take(ref, base):
        return ref[pl.ds(pl.multiple_of(base + low, 8), rows), :]

    for layer_at, ref in enumerate((zero_ref, mid_ref)):

        def put(at, a, b, grad):
            adam(at, (layer_at, slice(None), slice(a, b)), grad)

        for j in range(4):
            put(2, 128 * j, 128 * j + 128, take(ref, j * C))
        both = take(ref, 4 * C)
        put(2, 512, 576, both[:, 0:64])
        put(3, 128, 192, both[:, 64:128])
        put(3, 0, 128, take(ref, 5 * C))
        for j in range(6):
            put(4, 128 * j, 128 * j + 128, take(ref, (6 + j) * C))
            put(5, 128 * j, 128 * j + 128, take(ref, (12 + j) * C))
    everything = (slice(None), slice(None))
    adam(0, everything, take(zero_ref, 18 * C))
    adam(6, everything, take(mid_ref, 18 * C))

    @pl.when(step == 0)
    def _():
        lead_at = 19 * C + 16
        adam(1, (slice(None), slice(0, 128)), zero_ref[lead_at : lead_at + LEADS])
        adam(1, (slice(None), slice(128, 192)), zero_ref[lead_at + 24 : lead_at + 24 + LEADS, 0:64])
        adam(8, everything, mid_ref[scale_at : scale_at + 1])
        for at, (ref, index) in enumerate(((zero_ref, 0), (zero_ref, 1), (zero_ref, 2), (mid_ref, 1), (mid_ref, 2))):
            a = 19 * C + 2 * index
            adam(7, (at, slice(None), slice(0, 128)), ref[a : a + 2])
            adam(7, (at, slice(None), slice(128, 192)), ref[a + 8 : a + 10, 0:64])


def run_update(mid, zero, weights, firsts, seconds):
    steps = 3
    rows = C // steps
    kinds = (
        ((C, CIN), True),
        ((LEADS, C), False),
        ((2, C, 3 * C), True),
        ((2, C, C), True),
        ((2, C, FF), True),
        ((2, C, FF), True),
        ((C, CIN), True),
        ((5, 2, C), False),
        ((1, CIN), False),
    )
    specs = []
    for shape, cut in kinds:
        if not cut:
            specs.append(whole(shape))
        elif len(shape) == 2:
            specs.append(pl.BlockSpec((rows, shape[1]), lambda i: (i, 0)))
        else:
            specs.append(pl.BlockSpec((2, rows, shape[2]), lambda i: (0, i, 0)))
    shapes = [struct(shape, F32) for shape, _ in kinds]
    out = pl.pallas_call(
        partial(update, steps),
        grid=(steps,),
        in_specs=[whole(mid.shape), whole(zero.shape)] + specs * 3,
        out_specs=specs * 3 + [whole((8, 128))],
        out_shape=shapes * 3 + [struct((8, 128), F32)],
        scratch_shapes=[pltpu.VMEM((1, 128), F32)],
        compiler_params=pltpu.CompilerParams(vmem_limit_bytes=VMEM_BYTES),
        name="update",
    )(mid, zero, *weights, *firsts, *seconds)
    return out[0:9], out[9:18], out[18:27], out[27]


def whole(shape, once=False):
    zeros = (0,) * len(shape)
    return pl.BlockSpec(shape, lambda i: zeros, pipeline_mode=pl.Buffered(1) if once else None)


def layer(shape, index):
    at = (index,) + (0,) * len(shape)
    return pl.BlockSpec((1,) + shape, lambda i: at, pipeline_mode=pl.Buffered(1))


def rows_of(columns, offset, *shape):
    tail = (0,) * len(shape)
    return pl.BlockSpec((columns,) + shape, lambda i: (i + offset,) + tail)


def rows(columns, *shape):
    return rows_of(columns, 0, *shape)


SMEM = pl.BlockSpec(memory_space=pltpu.SMEM)


def struct(shape, dtype):
    return jax.ShapeDtypeStruct(shape, dtype)


def low(*shape):
    return pltpu.VMEM(shape, BF)


def full(*shape):
    return pltpu.VMEM(shape, F32)


def group_of(steps):
    return 2 if steps % 2 == 0 else 1


def kept_scratch(kept, count, columns):
    held = group_of(count // columns) * columns
    return [low(held * rows, width) for _, rows, width in kept]


def run_forward(lead_step, tokens, lead_table, embed_t, qkv_w, proj_w, up_w, down_t, norm_t, bands, columns):
    count = tokens.shape[0]
    steps = count // columns
    outs = [
        ((count, COL, XW), F32),
        ((count, COL, 3 * C), BF),
        ((count, 2, WIN, LANES), F32),
        ((count, COL, C), BF),
        ((count, COL, XW), F32),
        ((count, COL, FF), BF),
        ((count, COL, FF), F32),
        ((count, COL, C), F32),
    ]
    return pl.pallas_call(
        partial(forward_zero, columns, count, bands),
        grid=(steps,),
        in_specs=[
            SMEM,
            rows(columns, COL, CIN),
            whole((LEADS, C)),
            whole((C, CIN)),
            layer((C, 3 * C), 0),
            layer((C, C), 0),
            layer((C, FF), 0),
            layer((C, FF), 0),
            whole((5, 2, C)),
        ],
        out_specs=[rows(columns, *shape[1:]) for shape, _ in outs] + [ANYWHERE] * 2,
        out_shape=[struct(*o) for o in outs] + [struct((count, HALF, C), BF)] * 2,
        scratch_shapes=[low(C, CIN), low(C, 3 * C), low(C, C), low(C, FF), low(C, FF)] + edge_scratch(count, columns),
        compiler_params=pltpu.CompilerParams(vmem_limit_bytes=VMEM_BYTES, collective_id=1, has_side_effects=True),
        name="forward_zero",
    )(lead_step, tokens, lead_table, embed_t, qkv_w, proj_w, up_w, down_t, norm_t)


def run_middle(h1, up_in, down_in, target, mask, qkv_w, proj_w, up_w, down_t, decode_w, norm_t, scale, flat_rows, bands, columns):
    count = h1.shape[0]
    steps = count // columns
    outs = [
        ((count, WIN, C), F32),
        ((count, WIN, C), F32),
        ((count, WIN, C), F32),
        ((count, WIN, XW), F32),
    ]
    return pl.pallas_call(
        partial(middle, columns, count, bands),
        grid=(steps,),
        in_specs=[
            rows(columns, COL, C),
            rows(columns, HALF, C),
            rows(columns, HALF, C),
            rows(columns, COL, CIN),
            rows(columns, 24, 12),
            layer((C, 3 * C), 1),
            layer((C, C), 1),
            layer((C, FF), 1),
            layer((C, FF), 1),
            whole((C, CIN)),
            whole((5, 2, C)),
            whole((1, CIN)),
        ],
        out_specs=[rows(columns, *shape[1:]) for shape, _ in outs]
        + [whole((8, C)), whole((flat_rows, 128)), ANYWHERE, ANYWHERE],
        out_shape=[struct(*o) for o in outs]
        + [struct((8, C), F32), struct((flat_rows, 128), F32)]
        + [struct((count, HALF, C), BF)] * 2,
        scratch_shapes=edge_scratch(count, columns)
        + [
            low(C, 3 * C),
            low(C, C),
            low(C, FF),
            low(C, FF),
            low(C, CIN),
            low(COL, 24),
            full(COL, 12),
            full(columns, 2, WIN, LANES),
            low(columns, COL, FF),
            full(columns, COL, FF),
            low(columns, COL, FF),
            full(C, 3 * C),
            full(C, C),
            full(C, FF),
            full(C, FF),
            full(C, CIN),
            full(8, C),
            full(8, CIN),
        ]
        + kept_scratch(MIDDLE_KEEP, count, columns),
        compiler_params=pltpu.CompilerParams(vmem_limit_bytes=VMEM_BYTES, collective_id=2, has_side_effects=True),
        name="middle",
    )(h1, up_in, down_in, target, mask, qkv_w, proj_w, up_w, down_t, decode_w, norm_t, scale)


def run_backward(lead_step, tokens, saved, mid_out, mid, qkv_w, proj_w, up_w, down_t, norm_t, sizes, columns):
    count = tokens.shape[0]
    steps = count // columns
    streams = streams_of(sizes, mid.shape[0])
    return pl.pallas_call(
        partial(backward_zero, columns, count, streams),
        grid=(steps,),
        in_specs=[
            SMEM,
            rows(columns, COL, CIN),
            rows(columns, COL, XW),
            rows(columns, COL, 3 * C),
            rows(columns, 2, WIN, LANES),
            rows(columns, COL, C),
            rows(columns, COL, XW),
            rows(columns, COL, FF),
            rows(columns, COL, FF),
            rows(columns, WIN, C),
            rows(columns, WIN, C),
            rows(columns, WIN, C),
            rows(columns, WIN, XW),
            whole((8, C)),
            rows(columns, HALF, C),
            rows(columns, HALF, C),
            layer((C, 3 * C), 0),
            layer((C, C), 0),
            layer((C, FF), 0),
            layer((C, FF), 0),
            whole((5, 2, C)),
            whole(mid.shape, True),
        ],
        out_specs=[ANYWHERE] * 2,
        out_shape=[struct(mid.shape, F32)] * 2,
        scratch_shapes=[
            full(*mid.shape),
            low(C, 3 * C),
            low(C, C),
            low(C, FF),
            low(C, FF),
            low(columns, COL, FF),
            full(C, CIN),
            full(24, C),
            full(C, 3 * C),
            full(C, C),
            full(C, FF),
            full(C, FF),
            full(8, C),
        ]
        + kept_scratch(ZERO_KEEP, count, columns)
        + stream_buffers(streams) * 2
        + stream_sems(streams) * 2,
        compiler_params=pltpu.CompilerParams(vmem_limit_bytes=VMEM_BYTES, collective_id=3, has_side_effects=True),
        name="backward_zero",
    )(lead_step, tokens, *saved, *mid_out, qkv_w, proj_w, up_w, down_t, norm_t, mid)


def views(group):
    embed, lead, qkv, proj, up, down, decode, norm, scale = group
    return (embed.T, lead, qkv, proj, up, down.transpose(0, 2, 1), decode, norm.transpose(1, 0, 2), scale[None, :])


def unviews(group):
    embed, lead, qkv, proj, up, down, decode, norm, scale = group
    return (embed.T, lead, qkv, proj, up, down.transpose(0, 2, 1), decode, norm.transpose(1, 0, 2), scale[0])


def on_device(analysis, target, lead_step, loss_mask, *state):
    weights, firsts, seconds = (views(state[9 * i : 9 * i + 9]) for i in range(3))
    embed_t, lead_table, qkv_w, proj_w, up_w, down_t, decode_w, norm_t, scale = weights
    samples, blocks = analysis.shape[0], analysis.shape[1]
    sizes = {axis: lax.axis_size(axis) for axis in ("lat", "batch")}
    tokens = analysis.transpose(0, 1, 2, 4, 3, 5).reshape(samples * blocks, COL, CIN)
    truth = target.transpose(0, 1, 2, 4, 3, 5).reshape(samples * blocks, COL, CIN)
    lines = loss_mask.reshape(samples * blocks, 24, 12).astype(BF)
    columns = next(c for c in (COLUMNS, 3, 2, 1) if blocks % c == 0)
    columns_first = next(c for c in (COLUMNS_FIRST, columns) if blocks % c == 0)
    unit = 8 * sizes["lat"] * sizes["batch"]
    flat_rows = -(-max(FLAT_MIDDLE, FLAT_ZERO) // unit) * unit

    *saved, h1, from_low, from_high = run_forward(
        lead_step, tokens, lead_table, embed_t, qkv_w, proj_w, up_w, down_t, norm_t, sizes["lat"], columns_first
    )
    *edge_out, part, mid, back_low, back_high = run_middle(
        h1, from_low, from_high, truth, lines, qkv_w, proj_w, up_w, down_t, decode_w, norm_t, scale,
        flat_rows, sizes["lat"], columns,
    )
    mid, zero = run_backward(
        lead_step, tokens, saved, (*edge_out, part, back_low, back_high), mid, qkv_w, proj_w, up_w, down_t, norm_t,
        sizes, columns,
    )
    news, moments, squares, small = run_update(mid, zero, weights, firsts, seconds)
    return (*unviews(news), *unviews(moments), *unviews(squares), small[0, 0], small[1, 0], small[2, 0])


def solution(mesh):
    split = P("batch", None, "lat", None, None, None)
    placed = (split, split, P("batch"), P("batch", None, "lat", None, None)) + (P(),) * 27
    return jax.shard_map(
        on_device, mesh=mesh, in_specs=placed, out_specs=(P(),) * 30, check_vma=False
    )
```
